32 devices in a mesh: tile: 8 (over z, y), sec: 4 (over x, core).
Axes of the slice: x: 2, y: 2, z: 4, core: 2. Of those that a mesh axis runs over, the one named last changes fastest.
Arguments:
- voltage: float32 [1024, 512], P('tile', 'sec'), may hold values from -6 to 6
- conductance: float32 [1024, 512], P('tile', 'sec'), may hold values from 0.2 to 2
- reversal: float32 [1024, 512], P('tile', 'sec'), may hold values from -1 to 1
- drive: bfloat16 [8, 1024, 512], P(None, 'tile', 'sec'), may hold values from -6 to 6
- inv_cable: float32 [128, 128], replicated, may hold values from -1 to 1
- owner_map: int32 [1024], P('tile'), may hold values from 0 to 7, as said below
- peer_counts: int32 [8, 8], P('tile'), may hold values from 0 to 32, as said below
- pattern: int32 [4, 1024, 2], P('sec', 'tile'), may hold values from 0 to 31, all different within a row
- transfer: bfloat16 [4, 1024, 2, 128, 128], P('sec', 'tile'), may hold values from -0.03125 to 0.03125
Outputs:
- final_voltage: float32 [1024, 512], P('tile', 'sec')
- probe: float32 [8, 4096], P(None, ('tile', 'sec'))
The draws below stay inside these ranges and needn't reach their ends.
Inputs may be any that keep to these rules, and one draw needn't show every extreme that they name: `owner_map`: every depth tile owns exactly 128 cells; the cells c with c // 128 = u include at most 32 cells of one owner, and exactly 32 of some owner. peer_counts[d, u] is the number of cells c with c // 128 = u and owner_map[c] = d. `pattern`: the 2 contact tiles of one slot and section differ.
All inputs are finite; a program needn't handle non-finite values.
Results may differ from the reference program's by a relative error of at most 0.0029.
Values may be sent and summed in bfloat16 or wider, within the bound.
No kernel may reach another device: no remote copies, remote signals or barrier semaphores. Data moves between devices by JAX's collectives and lax.ppermute only.
A program may use at most 64 MiB of HBM per device.

```python
import math
import jax
import jax.numpy as jnp
from jax import lax

SEG = 128
CW = 128
CONTACTS = 4096
KB = 2
CELL_DEV = 128
STEPS = 8
OWNERS = 8
SECTIONS = 4
CELLS = 1024
COMPS = 512
CAP = 32
N_TILE = 8
N_SEC = 4


def tile_layout(key):
    base_key = jax.random.fold_in(key, 11)
    load_key, perm_key, shuffle_key = jax.random.split(base_key, 3)
    half_count = OWNERS // 2
    chosen = jax.random.randint(load_key, (half_count,), 0, CAP + 1).astype(jnp.int32)
    chosen = chosen.at[0].set(CAP)
    peer_loads = jnp.concatenate([chosen, CAP - chosen])
    peer_loads = peer_loads[jax.random.permutation(perm_key, OWNERS)]
    owners = jnp.arange(OWNERS, dtype=jnp.int32)
    counts = peer_loads[(owners[:, None] - owners[None, :]) % OWNERS]
    bounds = jnp.cumsum(counts, axis=0)
    places = jnp.arange(CELL_DEV, dtype=jnp.int32)
    owner_pos = jnp.sum((bounds.T[:, None, :] <= places[None, :, None]).astype(jnp.int32), axis=2)
    orders = jax.vmap(lambda one_key: jax.random.permutation(one_key, CELL_DEV))(jax.random.split(shuffle_key, OWNERS))
    owner_map = jnp.take_along_axis(owner_pos, orders, axis=1).reshape(-1)
    return (owner_map.astype(jnp.int32), counts.astype(jnp.int32))


def draw_owner_map(key, part):
    return tile_layout(key)[0]


def draw_peer_counts(key, part):
    return tile_layout(key)[1]


def draw_inv_cable(key, part):
    first_key, second_key = jax.random.split(jax.random.fold_in(key, 5))
    diagonal = jax.random.uniform(first_key, (SEG,), jnp.float32, 0.4, 0.6)
    spread = jnp.clip(jax.random.normal(second_key, (SEG, SEG), jnp.float32), -4.0, 4.0) * (0.2 / math.sqrt(SEG))
    return spread + jnp.eye(SEG, dtype=jnp.float32) * diagonal[None, :]


def shard_levels(own_key, shape, shards, smallest, top_value):
    factor_of, own = 1.0, jax.random.fold_in(own_key, 6)
    for dim, shards_of in shards:
        draws = jnp.exp(jax.random.uniform(jax.random.fold_in(own, dim), (shards_of,), jnp.float32, smallest / len(shards), top_value / len(shards)))
        factor_of = factor_of * jnp.repeat(draws, shape[dim] // shards_of).reshape([-1 if axis == dim else 1 for axis in range(len(shape))])
    return factor_of


def choose_distinct(stream_key, rows, count, top, lift):
    order = jax.random.permutation(jax.random.fold_in(stream_key, 1), count)
    boost = order
    for power in range(3):
        boost = boost * boost // count
    boost = boost * lift // count
    chance = jax.random.randint(jax.random.fold_in(stream_key, 2), (rows, count), 0, 4096) + boost
    holders = jax.random.permutation(jax.random.fold_in(stream_key, 3), rows)[jnp.arange(count) % rows]
    chance = jnp.where(jnp.arange(rows)[:, None] == holders[None, :], 1 << 14, chance)
    priority = chance * count + jnp.arange(count)
    return lax.top_k(priority.astype(jnp.int32), top)[1].astype(jnp.int32)


def normal_values(own_key, extent, width, most, cuts=(), kind=jnp.bfloat16):
    drawn = width * jax.random.normal(own_key, extent, jnp.float32)
    if cuts:
        drawn = drawn * shard_levels(own_key, extent, cuts, -0.22, 0.18)
    return jnp.clip(drawn, -most, most).astype(kind)


def setup_inputs(seed: int = 0) -> dict:
    seeds = jax.random.split(jax.random.key(seed), 10)
    return {
        "voltage": normal_values(seeds[0], (CELLS, COMPS), 1.0, 6.0, ((0, 8), (1, 4)), jnp.float32),
        "conductance": jnp.clip(jnp.exp(math.log(2.0) - 2.3025851 * jax.random.uniform(seeds[1], (CELLS, COMPS), jnp.float32) ** shard_levels(seeds[1], (CELLS, COMPS), ((0, 8), (1, 4)), -0.2, 0.2)), 0.2, 2.0),
        "reversal": jnp.clip(jax.random.uniform(seeds[2], (CELLS, COMPS), jnp.float32, -1.0, 1.0) * shard_levels(seeds[2], (CELLS, COMPS), ((0, 8), (1, 4)), -0.4, 0.0), -1.0, 1.0),
        "drive": normal_values(seeds[3], (STEPS, CELLS, COMPS), 1.0, 6.0, ((1, 8), (2, 4))),
        "inv_cable": draw_inv_cable(jax.random.fold_in(seeds[9], 71), 0),
        "owner_map": draw_owner_map(jax.random.fold_in(seeds[9], 71), 0),
        "peer_counts": draw_peer_counts(jax.random.fold_in(seeds[9], 71), 0),
        "pattern": choose_distinct(seeds[7], SECTIONS * CELLS, CONTACTS // CW, KB, 0).reshape((SECTIONS, CELLS, KB)),
        "transfer": normal_values(seeds[8], (SECTIONS, CELLS, KB, SEG, CW), (N_TILE * N_SEC * CELL_DEV * KB * SEG // (CONTACTS // CW)) ** -0.5, 0.03125, ((0, 4), (1, 8))),
    }


TIME_STEP = 0.25
AXIAL = 2.0


def cable_update(voltage_now, conductance, reversal, drive_now, inv_cable):
    zero_col = jnp.zeros((voltage_now.shape[0], 1), jnp.float32)
    left_end = jnp.concatenate([zero_col, voltage_now[:, :-1, -1]], axis=1)
    right_end = jnp.concatenate([voltage_now[:, 1:, 0], zero_col], axis=1)
    columns = jnp.arange(SEG, dtype=jnp.int32)
    first_col = (columns == 0).astype(jnp.float32)
    last_col = (columns == SEG - 1).astype(jnp.float32)
    boundary = first_col * (left_end[:, :, None] - voltage_now) + last_col * (right_end[:, :, None] - voltage_now)
    driven = drive_now.astype(jnp.float32)
    right_side = voltage_now * (1.0 - TIME_STEP * conductance) + TIME_STEP * (conductance * reversal + driven + AXIAL * boundary)
    voltage_next = jnp.einsum("cni,ji->cnj", right_side, inv_cable, precision=lax.Precision.HIGHEST)
    current = (conductance * (voltage_next - reversal) - driven).astype(jnp.bfloat16)
    return voltage_next, current


def reference(voltage, conductance, reversal, drive, inv_cable, owner_map, peer_counts, pattern, transfer):
    cell_shape = (CELLS, SECTIONS, SEG)
    voltage_now = voltage.reshape(cell_shape)
    cond_cells = conductance.reshape(cell_shape)
    rev_cells = reversal.reshape(cell_shape)
    currents = []
    for step_index in range(STEPS):
        voltage_now, current = cable_update(voltage_now, cond_cells, rev_cells, drive[step_index].reshape(cell_shape), inv_cable)
        currents.append(current)
    current_all = jnp.stack(currents)
    owners = jnp.arange(OWNERS, dtype=jnp.int32)
    member = (owner_map[:, None] == owners[None, :]).astype(jnp.int32)
    running = jnp.cumsum(member.reshape(OWNERS, CELL_DEV, OWNERS), axis=1).reshape(CELLS, OWNERS)
    rank_within = jnp.sum(running * member, axis=1) - 1
    source = jnp.arange(CELLS, dtype=jnp.int32) // CELL_DEV
    starts = jnp.cumsum(peer_counts, axis=1) - peer_counts
    destination = (owner_map * CELL_DEV + starts[owner_map, source] + rank_within).astype(jnp.int32)
    ordered = jnp.zeros_like(current_all).at[:, destination].set(current_all)
    tile_total = CONTACTS // CW
    tile_ids = jnp.arange(tile_total, dtype=jnp.int32)

    def owner_block(probe_sum, owner_index):
        first_row = (owner_index * CELL_DEV).astype(jnp.int32)
        owner_rows = lax.dynamic_slice_in_dim(ordered, first_row, CELL_DEV, 1)
        for section in range(SECTIONS):
            weights = lax.dynamic_slice_in_dim(transfer[section], first_row, CELL_DEV, 0).astype(jnp.float32)
            layout = lax.dynamic_slice_in_dim(pattern[section], first_row, CELL_DEV, 0)
            tile_sums = jnp.einsum("tsi,skic->tskc", owner_rows[:, :, section].astype(jnp.float32), weights, precision=lax.Precision.HIGHEST)
            select = (layout[:, :, None] == tile_ids[None, None, :]).astype(jnp.float32)
            probe_sum = probe_sum + jnp.einsum("tskc,skq->tqc", tile_sums, select, precision=lax.Precision.HIGHEST).reshape(STEPS, CONTACTS)
        return probe_sum, None

    probe_sum, unused_out = lax.scan(owner_block, jnp.zeros((STEPS, CONTACTS), jnp.float32), owners)
    return voltage_now.reshape(CELLS, SECTIONS * SEG), probe_sum
```

```python
import functools

import jax
import jax.numpy as jnp
from jax import lax
from jax.experimental import pallas as pl
from jax.experimental.pallas import tpu as pltpu
from jax.sharding import PartitionSpec as P

CONTACTS = 4096
TIME_STEP = 0.25
AXIAL = 2.0
END_ROWS = 48
BF = jnp.bfloat16
F32 = jnp.float32


def split_hi_lo(x):
    hi = x.astype(BF)
    return hi, (x - hi.astype(F32)).astype(BF)


def local_kernel(v_ref, g_ref, e_ref, drive_ref, cable_ref, vloc_ref, resp_ref, ends_ref):
    cells, width = v_ref.shape
    steps = drive_ref.shape[0]
    cond = g_ref[...]
    lane = lax.broadcasted_iota(jnp.int32, (cells, width), 1)
    at_end = jnp.where((lane == 0) | (lane == width - 1), TIME_STEP * AXIAL, 0.0).astype(F32)
    keep = 1.0 - TIME_STEP * cond - at_end
    source = TIME_STEP * cond * e_ref[...]
    cable = cable_ref[...].T
    cable_hi, cable_lo = split_hi_lo(cable)
    half = jnp.concatenate([cable_hi, cable_lo], axis=1)
    weights = jnp.concatenate([half, half], axis=0)
    pick_row = lax.broadcasted_iota(jnp.int32, (16, width), 0)
    pick_lane = lax.broadcasted_iota(jnp.int32, (16, width), 1)
    pick = jnp.where(
        ((pick_row == 0) & (pick_lane == 0)) | ((pick_row == 1) & (pick_lane == width - 1)),
        1.0,
        0.0,
    ).astype(BF)

    def solve(rhs):
        hi, lo = split_hi_lo(rhs)
        both = jnp.dot(jnp.concatenate([hi, lo], axis=1), weights, preferred_element_type=F32)
        return both[:, :width] + both[:, width:]

    def ends_of(x):
        return lax.dot_general(
            pick, x.astype(BF), (((1,), (1,)), ((), ())), preferred_element_type=F32
        )[0:2]

    voltage = v_ref[...]
    lag_left = jnp.broadcast_to(TIME_STEP * AXIAL * cable[0:1, :], (cells, width))
    lag_right = jnp.broadcast_to(TIME_STEP * AXIAL * cable[width - 1 : width, :], (cells, width))
    keep2 = jnp.concatenate([keep, keep], axis=0)
    resp = jnp.concatenate([lag_left, lag_right], axis=0)
    v_ends, l_ends, r_ends = [ends_of(voltage)], [], []
    both_ends = ends_of(resp)
    l_ends.append(both_ends[:, :cells])
    r_ends.append(both_ends[:, cells:])
    for k in range(steps):
        rhs = voltage * keep + source + TIME_STEP * drive_ref[k].astype(F32)
        if k < steps - 1:
            out = solve(jnp.concatenate([rhs, resp * keep2], axis=0))
            voltage, resp = out[:cells], out[cells:]
            resp_ref[k] = resp
            v_ends.append(ends_of(voltage))
            if k < steps - 2:
                both_ends = ends_of(resp)
                l_ends.append(both_ends[:, :cells])
                r_ends.append(both_ends[:, cells:])
        else:
            voltage = solve(rhs)
        vloc_ref[k] = voltage
    rows = v_ends + l_ends + r_ends
    rows.append(jnp.zeros((END_ROWS - 2 * len(rows), cells), F32))
    ends_ref[...] = jnp.concatenate(rows, axis=0).astype(BF)


def couple_kernel(
    tiles,
    sec_ref,
    ends_ref,
    vloc_ref,
    resp_ref,
    g_ref,
    e_ref,
    drive_ref,
    cable_ref,
    owner_ref,
    final_ref,
    out_ref,
    ends32,
    incoming,
    leak,
):
    steps, cells, width = drive_ref.shape
    sections = ends_ref.shape[0]
    ends32[...] = ends_ref[...].astype(F32)

    def rows(q):
        return ends32[:, q, :]

    base_l, base_r = 2 * steps, 4 * steps - 2
    left_a = [None] + [rows(base_l + 2 * l) for l in range(steps - 1)]
    left_b = [None] + [rows(base_l + 2 * l + 1) for l in range(steps - 1)]
    right_a = [None] + [rows(base_r + 2 * l) for l in range(steps - 1)]
    right_b = [None] + [rows(base_r + 2 * l + 1) for l in range(steps - 1)]
    zero = jnp.zeros((1, cells), F32)
    from_left, from_right = [], []
    for k in range(steps):
        first, last = rows(2 * k), rows(2 * k + 1)
        for j in range(k):
            first = first + (left_a[k - j] * from_left[j] + right_a[k - j] * from_right[j])
            last = last + (left_b[k - j] * from_left[j] + right_b[k - j] * from_right[j])
        from_left.append(jnp.concatenate([zero, last[:-1]], axis=0))
        from_right.append(jnp.concatenate([first[1:], zero], axis=0))
    mine = lax.broadcasted_iota(jnp.int32, (sections, cells), 0) == sec_ref[0]
    for j in range(steps):
        incoming[pl.ds(2 * j, 1), :] = jnp.sum(
            jnp.where(mine, from_left[j], 0.0), axis=0, keepdims=True
        )
        incoming[pl.ds(2 * j + 1, 1), :] = jnp.sum(
            jnp.where(mine, from_right[j], 0.0), axis=0, keepdims=True
        )
    by_cell = incoming[...].T

    cable = cable_ref[...].T
    block = 8
    lag_left = jnp.broadcast_to(TIME_STEP * AXIAL * cable[0:1, :], (block, width))
    lag_right = jnp.broadcast_to(TIME_STEP * AXIAL * cable[width - 1 : width, :], (block, width))
    for c in range(0, cells, block):
        span = slice(c, c + block)
        unit = [
            jnp.broadcast_to(by_cell[span, q : q + 1], (block, width)) for q in range(2 * steps)
        ]
        lefts = [None, lag_left] + [resp_ref[l, span, :] for l in range(steps - 1)]
        rights = [None, lag_right] + [
            resp_ref[l, cells + c : cells + c + block, :] for l in range(steps - 1)
        ]
        cond, rev = g_ref[span, :], e_ref[span, :]
        for k in range(1, steps + 1):
            total = vloc_ref[k - 1, span, :]
            for j in range(k):
                total = total + (unit[2 * j] * lefts[k - j] + unit[2 * j + 1] * rights[k - j])
            leak[k - 1, span, :] = cond * (total - rev)
        final_ref[span, :] = total

    capacity = out_ref.shape[0] // tiles
    owner = owner_ref[...]
    member = owner == lax.broadcasted_iota(jnp.int32, (tiles, cells), 0)
    before = lax.broadcasted_iota(jnp.int32, (cells, cells), 0) < lax.broadcasted_iota(
        jnp.int32, (cells, cells), 1
    )
    rank = jnp.dot(
        jnp.where(member, 1.0, 0.0).astype(BF),
        jnp.where(before, 1.0, 0.0).astype(BF),
        preferred_element_type=F32,
    )
    rank = jnp.sum(jnp.where(member, rank, 0.0), axis=0, keepdims=True).astype(jnp.int32)
    target = owner * capacity + rank
    spread = lax.broadcasted_iota(jnp.int32, (out_ref.shape[0], cells), 0) == target
    spread = jnp.where(spread, 1.0, 0.0).astype(BF)
    for k in range(steps):
        current = (leak[k] - drive_ref[k].astype(F32)).astype(BF)
        out_ref[:, k * width : (k + 1) * width] = jnp.dot(
            spread, current, preferred_element_type=F32
        ).astype(BF)


def readout_kernel(
    tiles, steps, counts_ref, pattern_ref, rows_ref, transfer_ref, out_ref, slots
):
    block, kinds, width, contacts = transfer_ref.shape
    step = pl.program_id(0)
    row_count = rows_ref.shape[0]
    capacity = row_count // tiles
    slot_count = block * pl.num_programs(0)

    @pl.when(step == 0)
    def _():
        row = lax.broadcasted_iota(jnp.int32, (1, row_count), 1)
        slot_of = jnp.full((1, row_count), -1, jnp.int32)
        start = jnp.int32(0)
        for u in range(tiles):
            count = counts_ref[0, u]
            place = row - u * capacity
            slot_of = jnp.where((place >= 0) & (place < count), place + start, slot_of)
            start = start + count
        order = lax.broadcasted_iota(jnp.int32, (slot_count, row_count), 0) == slot_of
        order = jnp.where(order, 1.0, 0.0).astype(BF)
        for k in range(steps):
            slots[pl.ds(k, slot_count, stride=steps), :] = jnp.dot(
                order, rows_ref[:, k * width : (k + 1) * width], preferred_element_type=F32
            )
        out_ref[...] = jnp.zeros_like(out_ref)

    for s in range(block):
        slot = step * block + s
        current = slots[pl.ds(pl.multiple_of(slot * steps, steps), steps), :].astype(BF)
        for t in range(kinds):
            q = pattern_ref[t, slot]
            out_ref[q] += jnp.dot(current, transfer_ref[s, t], preferred_element_type=F32)


def on_device(
    voltage, conductance, reversal, drive, inv_cable, owner_map, peer_counts, pattern, transfer
):
    cells, width = voltage.shape
    steps = drive.shape[0]
    tiles = lax.axis_size("tile")
    sections = lax.axis_size("sec")
    capacity = 2 * cells // tiles
    row_count = tiles * capacity
    vmem = pl.BlockSpec(memory_space=pltpu.VMEM)
    smem = pl.BlockSpec(memory_space=pltpu.SMEM)
    big = pltpu.CompilerParams(vmem_limit_bytes=32 * 1024 * 1024)

    vloc, resp, ends = pl.pallas_call(
        local_kernel,
        out_shape=(
            jax.ShapeDtypeStruct((steps, cells, width), F32),
            jax.ShapeDtypeStruct((steps - 1, 2 * cells, width), F32),
            jax.ShapeDtypeStruct((END_ROWS, cells), BF),
        ),
        in_specs=[vmem] * 5,
        out_specs=(vmem,) * 3,
        compiler_params=big,
        name="local_steps",
    )(voltage, conductance, reversal, drive, inv_cable)

    all_ends = lax.all_gather(ends, "sec", axis=0, tiled=False)
    final_voltage, outgoing = pl.pallas_call(
        functools.partial(couple_kernel, tiles),
        out_shape=(
            jax.ShapeDtypeStruct((cells, width), F32),
            jax.ShapeDtypeStruct((row_count, steps * width), BF),
        ),
        in_specs=[smem] + [vmem] * 8,
        out_specs=(vmem,) * 2,
        scratch_shapes=[
            pltpu.VMEM((sections, END_ROWS, cells), F32),
            pltpu.VMEM((2 * steps, cells), F32),
            pltpu.VMEM((steps, cells, width), F32),
        ],
        compiler_params=big,
        name="couple_sections",
    )(
        lax.axis_index("sec").reshape(1),
        all_ends,
        vloc,
        resp,
        conductance,
        reversal,
        drive,
        inv_cable,
        owner_map.reshape(1, cells),
    )

    arrived = lax.all_to_all(outgoing, "tile", split_axis=0, concat_axis=0, tiled=True)

    weights = transfer[0]
    slot_count, kinds, _, contact_width = weights.shape
    contact_tiles = CONTACTS // contact_width
    block = 16
    partial_sum = pl.pallas_call(
        functools.partial(readout_kernel, tiles, steps),
        out_shape=jax.ShapeDtypeStruct((contact_tiles, steps, contact_width), F32),
        grid=(slot_count // block,),
        in_specs=[
            smem,
            smem,
            pl.BlockSpec((row_count, steps * width), lambda i: (0, 0)),
            pl.BlockSpec((block, kinds, width, contact_width), lambda i: (i, 0, 0, 0)),
        ],
        out_specs=pl.BlockSpec((contact_tiles, steps, contact_width), lambda i: (0, 0, 0)),
        scratch_shapes=[pltpu.VMEM((slot_count * steps, width), F32)],
        compiler_params=big,
        name="readout",
    )(peer_counts, pattern[0].T, arrived, weights)

    devices = tiles * sections
    share = CONTACTS // devices
    parts = contact_width // share
    if parts > 1:
        partial_sum = partial_sum.reshape(contact_tiles, steps, parts, share)
        partial_sum = partial_sum.transpose(0, 2, 1, 3).reshape(devices, steps, share)
    shares = lax.all_to_all(partial_sum, ("tile", "sec"), split_axis=0, concat_axis=0, tiled=True)
    return final_voltage, jnp.sum(shares, axis=0)


def solution(mesh):
    placed = (
        P("tile", "sec"),
        P("tile", "sec"),
        P("tile", "sec"),
        P(None, "tile", "sec"),
        P(),
        P("tile"),
        P("tile", None),
        P("sec", "tile", None),
        P("sec", "tile", None, None, None),
    )
    return jax.shard_map(
        on_device,
        mesh=mesh,
        in_specs=placed,
        out_specs=(P("tile", "sec"), P(None, ("tile", "sec"))),
        check_vma=False,
    )
```

```python
import functools

import jax
import jax.numpy as jnp
from jax import lax
from jax.experimental import pallas as pl
from jax.experimental.pallas import tpu as pltpu
from jax.sharding import PartitionSpec as P

CONTACTS = 4096
TIME_STEP = 0.25
AXIAL = 2.0
END_ROWS = 48
PAIRED = True
BF = jnp.bfloat16
F32 = jnp.float32
PARAMS = pltpu.CompilerParams(vmem_limit_bytes=24 * 1024 * 1024)


def split_hi_lo(x):
    hi = x.astype(BF)
    return hi, (x - hi.astype(F32)).astype(BF)


def one_hot(condition):
    return jnp.where(condition, 1.0, 0.0).astype(BF)


def iota(shape, dim):
    return lax.broadcasted_iota(jnp.int32, shape, dim)


def local_kernel(
    tiles,
    paired,
    me_ref,
    v_hbm,
    g_hbm,
    e_hbm,
    drive_hbm,
    cable_hbm,
    owner_hbm,
    counts_hbm,
    pattern_hbm,
    vloc_ref,
    resp_ref,
    ends_ref,
    g_ref,
    e_ref,
    drive_ref,
    lags_ref,
    spread_ref,
    order_ref,
    pattern_ref,
    v_ref,
    cable_ref,
    owner_ref,
    counts_ref,
    sems,
):
    pairs = [
        (g_hbm, g_ref),
        (v_hbm, v_ref),
        (e_hbm, e_ref),
        (cable_hbm, cable_ref),
        (drive_hbm, drive_ref),
        (owner_hbm, owner_ref),
        (counts_hbm, counts_ref),
        (pattern_hbm, pattern_ref),
    ]
    copies = [pltpu.make_async_copy(src, dst, sems.at[i]) for i, (src, dst) in enumerate(pairs)]
    for copy in copies:
        copy.start()
    for copy in copies[:5]:
        copy.wait()

    cells, width = v_ref.shape
    steps = drive_ref.shape[0]
    cond = g_ref[...]
    lane = iota((cells, width), 1)
    at_end = jnp.where((lane == 0) | (lane == width - 1), TIME_STEP * AXIAL, 0.0).astype(F32)
    keep = 1.0 - TIME_STEP * cond - at_end
    source = TIME_STEP * cond * e_ref[...]
    cable = cable_ref[...].T
    cable_hi, cable_lo = split_hi_lo(cable)
    half = jnp.concatenate([cable_hi, cable_lo], axis=1)
    weights = jnp.concatenate([half, half], axis=0)
    pick_row, pick_lane = iota((16, width), 0), iota((16, width), 1)
    pick = one_hot(
        ((pick_row == 0) & (pick_lane == 0)) | ((pick_row == 1) & (pick_lane == width - 1))
    )

    def solve(rhs):
        hi, lo = split_hi_lo(rhs)
        both = jnp.dot(jnp.concatenate([hi, lo], axis=1), weights, preferred_element_type=F32)
        return both[:, :width] + both[:, width:]

    def ends_of(x):
        return lax.dot_general(
            pick, x.astype(BF), (((1,), (1,)), ((), ())), preferred_element_type=F32
        )[0:2]

    voltage = v_ref[...]
    lag_left = TIME_STEP * AXIAL * cable[0:1, :]
    lag_right = TIME_STEP * AXIAL * cable[width - 1 : width, :]
    lags_ref[0:1, :] = lag_left
    lags_ref[1:2, :] = lag_right
    keep2 = jnp.concatenate([keep, keep], axis=0)
    resp = jnp.concatenate(
        [jnp.broadcast_to(lag_left, (cells, width)), jnp.broadcast_to(lag_right, (cells, width))],
        axis=0,
    )
    v_ends, l_ends, r_ends = [ends_of(voltage)], [], []
    both_ends = ends_of(resp)
    l_ends.append(both_ends[:, :cells])
    r_ends.append(both_ends[:, cells:])
    for k in range(steps):
        rhs = voltage * keep + source + TIME_STEP * drive_ref[k].astype(F32)
        if k < steps - 1:
            out = solve(jnp.concatenate([rhs, resp * keep2], axis=0))
            voltage, resp = out[:cells], out[cells:]
            resp_ref[k] = resp
            v_ends.append(ends_of(voltage))
            if k < steps - 2:
                both_ends = ends_of(resp)
                l_ends.append(both_ends[:, :cells])
                r_ends.append(both_ends[:, cells:])
        else:
            voltage = solve(rhs)
        vloc_ref[k] = voltage
    rows = v_ends + l_ends + r_ends
    rows.append(jnp.zeros((END_ROWS - 2 * len(rows), cells), F32))
    ends_ref[...] = jnp.concatenate(rows, axis=0).astype(BF)

    for copy in copies[5:7]:
        copy.wait()
    me = me_ref[0]
    row_count = spread_ref.shape[0]
    capacity = row_count // tiles
    owner = owner_ref[...]
    member = owner == iota((tiles, cells), 0)
    before = iota((cells, cells), 0) < iota((cells, cells), 1)
    rank = jnp.dot(one_hot(member), one_hot(before), preferred_element_type=F32)
    rank = jnp.sum(jnp.where(member, rank, 0.0), axis=0, keepdims=True).astype(jnp.int32)
    to = owner ^ me if paired else owner
    spread_ref[...] = one_hot(iota((row_count, cells), 0) == to * capacity + rank)

    counts = [counts_ref[0, u] for u in range(tiles)]
    row = iota((1, row_count), 1)
    slot_of = jnp.full((1, row_count), -1, jnp.int32)
    start = jnp.int32(0)
    for b in range(tiles):
        if paired:
            sender = b ^ me
            count = counts_ref[0, sender]
            start = sum(jnp.where(u < sender, counts[u], 0) for u in range(tiles))
        else:
            count = counts[b]
            start = start + (counts[b - 1] if b else 0)
        place = row - b * capacity
        slot_of = jnp.where((place >= 0) & (place < count), place + start, slot_of)
    order_ref[...] = one_hot(iota(order_ref.shape, 0) == slot_of)
    for copy in copies[7:]:
        copy.wait()


def couple_kernel(sections, block_count, *refs):
    sec_ref, *refs = refs
    ends_refs, refs = refs[:sections], refs[sections:]
    vloc_ref, resp_ref, g_ref, e_ref, drive_ref, lags_ref, spread_ref, *refs = refs
    final_hbm, *refs = refs
    out_refs, refs = refs[:block_count], refs[block_count:]
    ends32, incoming, leak, final_ref, sem = refs
    steps, cells, width = drive_ref.shape
    mine = sec_ref[0]
    for p in range(sections):
        ends32[mine ^ p] = ends_refs[p][...].astype(F32)

    def rows(q):
        return ends32[:, q, :]

    base_l, base_r = 2 * steps, 4 * steps - 2
    left_a = [None] + [rows(base_l + 2 * l) for l in range(steps - 1)]
    left_b = [None] + [rows(base_l + 2 * l + 1) for l in range(steps - 1)]
    right_a = [None] + [rows(base_r + 2 * l) for l in range(steps - 1)]
    right_b = [None] + [rows(base_r + 2 * l + 1) for l in range(steps - 1)]
    zero = jnp.zeros((1, cells), F32)
    from_left, from_right = [], []
    for k in range(steps):
        first, last = rows(2 * k), rows(2 * k + 1)
        for j in range(k):
            first = first + (left_a[k - j] * from_left[j] + right_a[k - j] * from_right[j])
            last = last + (left_b[k - j] * from_left[j] + right_b[k - j] * from_right[j])
        from_left.append(jnp.concatenate([zero, last[:-1]], axis=0))
        from_right.append(jnp.concatenate([first[1:], zero], axis=0))
    own = iota((sections, cells), 0) == mine
    for j in range(steps):
        incoming[pl.ds(2 * j, 1), :] = jnp.sum(
            jnp.where(own, from_left[j], 0.0), axis=0, keepdims=True
        )
        incoming[pl.ds(2 * j + 1, 1), :] = jnp.sum(
            jnp.where(own, from_right[j], 0.0), axis=0, keepdims=True
        )
    by_cell = incoming[...].T

    block = 8
    lag_left = jnp.broadcast_to(lags_ref[0:1, :], (block, width))
    lag_right = jnp.broadcast_to(lags_ref[1:2, :], (block, width))
    for c in range(0, cells, block):
        span = slice(c, c + block)
        unit = [
            jnp.broadcast_to(by_cell[span, q : q + 1], (block, width)) for q in range(2 * steps)
        ]
        lefts = [None, lag_left] + [resp_ref[l, span, :] for l in range(steps - 1)]
        rights = [None, lag_right] + [
            resp_ref[l, cells + c : cells + c + block, :] for l in range(steps - 1)
        ]
        cond, rev = g_ref[span, :], e_ref[span, :]
        for k in range(1, steps + 1):
            total = vloc_ref[k - 1, span, :]
            for j in range(k):
                total = total + (unit[2 * j] * lefts[k - j] + unit[2 * j + 1] * rights[k - j])
            leak[k - 1, span, :] = cond * (total - rev)
        final_ref[span, :] = total
    give = pltpu.make_async_copy(final_ref, final_hbm, sem)
    give.start()

    capacity = out_refs[0].shape[0]
    for k in range(steps):
        current = (leak[k] - drive_ref[k].astype(F32)).astype(BF)
        placed = jnp.dot(spread_ref[...], current, preferred_element_type=F32).astype(BF)
        for b in range(block_count):
            out_refs[b][:, k * width : (k + 1) * width] = placed[b * capacity : (b + 1) * capacity]
    give.wait()


def fetch_kernel(after_ref, transfer_hbm, transfer_ref, sems):
    del after_ref
    parts = sems.shape[0]
    size = transfer_ref.shape[0] // parts
    copies = []
    for p in range(parts):
        span = pl.ds(p * size, size)
        copies.append(
            pltpu.make_async_copy(transfer_hbm.at[span], transfer_ref.at[span], sems.at[p])
        )
    for copy in copies:
        copy.start()
    for copy in copies:
        copy.wait()


def readout_kernel(steps, pattern_ref, order_ref, *refs):
    *block_refs, transfer_ref, out_ref, slots, sums = refs
    slot_count = order_ref.shape[0]
    kinds, width, contacts = transfer_ref.shape[1:]
    for k in range(steps):
        span = slice(k * width, (k + 1) * width)
        rows = jnp.concatenate([ref[:, span] for ref in block_refs], axis=0)
        slots[pl.ds(k, slot_count, stride=steps), :] = jnp.dot(
            order_ref[...], rows, preferred_element_type=F32
        )
    sums[...] = jnp.zeros_like(sums)
    ways = sums.shape[0]
    turn = 0
    for s in range(slot_count):
        current = slots[s * steps : (s + 1) * steps, :].astype(BF)
        tile = jnp.concatenate([transfer_ref[s, t] for t in range(kinds)], axis=1)
        reach = jnp.dot(current, tile, preferred_element_type=F32)
        for t in range(kinds):
            sums[turn % ways, pattern_ref[t, s]] += reach[:, t * contacts : (t + 1) * contacts]
            turn += 1
    out_ref[...] = sum(sums[w] for w in range(ways))


def in_hbm(x):
    return pltpu.with_memory_space_constraint(x, pltpu.HBM)


def exchange(blocks, axis):
    count = lax.axis_size(axis)
    arrived = [blocks[0]]
    for p in range(1, count):
        arrived.append(lax.ppermute(blocks[p], axis, [(i, i ^ p) for i in range(count)]))
    return arrived


def on_device(
    voltage, conductance, reversal, drive, inv_cable, owner_map, peer_counts, pattern, transfer
):
    cells, width = voltage.shape
    steps = drive.shape[0]
    tiles = lax.axis_size("tile")
    sections = lax.axis_size("sec")
    capacity = 2 * cells // tiles
    row_count = tiles * capacity
    weights = transfer[0]
    slot_count, kinds, _, contact_width = weights.shape
    paired = PAIRED and tiles == 8
    vmem = pl.BlockSpec(memory_space=pltpu.VMEM)
    smem = pl.BlockSpec(memory_space=pltpu.SMEM)
    hbm = pl.BlockSpec(memory_space=pltpu.HBM)

    vloc, resp, ends, cond, rev, driven, lags, spread, order, layout = pl.pallas_call(
        functools.partial(local_kernel, tiles, paired),
        out_shape=(
            jax.ShapeDtypeStruct((steps, cells, width), F32),
            jax.ShapeDtypeStruct((steps - 1, 2 * cells, width), F32),
            jax.ShapeDtypeStruct((END_ROWS, cells), BF),
            jax.ShapeDtypeStruct((cells, width), F32),
            jax.ShapeDtypeStruct((cells, width), F32),
            jax.ShapeDtypeStruct((steps, cells, width), BF),
            jax.ShapeDtypeStruct((2, width), F32),
            jax.ShapeDtypeStruct((row_count, cells), BF),
            jax.ShapeDtypeStruct((slot_count, row_count), BF),
            jax.ShapeDtypeStruct((kinds, slot_count), jnp.int32),
        ),
        in_specs=[smem] + [hbm] * 8,
        out_specs=(vmem,) * 10,
        scratch_shapes=[
            pltpu.VMEM((cells, width), F32),
            pltpu.VMEM((width, width), F32),
            pltpu.VMEM((1, cells), jnp.int32),
            pltpu.SMEM((1, tiles), jnp.int32),
            pltpu.SemaphoreType.DMA((8,)),
        ],
        compiler_params=PARAMS,
        name="local_steps",
    )(
        lax.axis_index("tile").reshape(1),
        in_hbm(voltage),
        in_hbm(conductance),
        in_hbm(reversal),
        in_hbm(drive),
        in_hbm(inv_cable),
        in_hbm(owner_map.reshape(1, cells)),
        in_hbm(peer_counts),
        in_hbm(pattern[0].T),
    )

    all_ends = exchange([ends] * sections, "sec")
    block_count = tiles if paired else 1
    final_voltage, *outgoing = pl.pallas_call(
        functools.partial(couple_kernel, sections, block_count),
        out_shape=(
            jax.ShapeDtypeStruct((cells, width), F32),
        )
        + (jax.ShapeDtypeStruct((row_count // block_count, steps * width), BF),) * block_count,
        in_specs=[smem] + [vmem] * (sections + 7),
        out_specs=(hbm,) + (vmem,) * block_count,
        scratch_shapes=[
            pltpu.VMEM((sections, END_ROWS, cells), F32),
            pltpu.VMEM((2 * steps, cells), F32),
            pltpu.VMEM((steps, cells, width), F32),
            pltpu.VMEM((cells, width), F32),
            pltpu.SemaphoreType.DMA,
        ],
        compiler_params=PARAMS,
        name="couple_sections",
    )(
        lax.axis_index("sec").reshape(1),
        *all_ends,
        vloc,
        resp,
        cond,
        rev,
        driven,
        lags,
        spread,
    )

    if paired:
        arrived = exchange(outgoing, "tile")
    else:
        arrived = [lax.all_to_all(outgoing[0], "tile", split_axis=0, concat_axis=0, tiled=True)]

    tiles_here = pl.pallas_call(
        fetch_kernel,
        out_shape=jax.ShapeDtypeStruct(weights.shape, BF),
        in_specs=[vmem, hbm],
        out_specs=vmem,
        scratch_shapes=[pltpu.SemaphoreType.DMA((4,))],
        compiler_params=PARAMS,
        name="fetch_tiles",
    )(outgoing[0], in_hbm(weights))

    contact_tiles = CONTACTS // contact_width
    partial_sum = pl.pallas_call(
        functools.partial(readout_kernel, steps),
        out_shape=jax.ShapeDtypeStruct((contact_tiles, steps, contact_width), F32),
        in_specs=[smem] + [vmem] * (len(arrived) + 2),
        out_specs=vmem,
        scratch_shapes=[
            pltpu.VMEM((slot_count * steps, width), F32),
            pltpu.VMEM((4, contact_tiles, steps, contact_width), F32),
        ],
        compiler_params=PARAMS,
        name="readout",
    )(layout, order, *arrived, tiles_here)

    devices = tiles * sections
    share = CONTACTS // devices
    parts = contact_width // share
    if parts > 1:
        partial_sum = partial_sum.reshape(contact_tiles, steps, parts, share)
        partial_sum = partial_sum.transpose(0, 2, 1, 3).reshape(devices, steps, share)
    shares = lax.all_to_all(partial_sum, ("tile", "sec"), split_axis=0, concat_axis=0, tiled=True)
    return final_voltage, jnp.sum(shares, axis=0)


def solution(mesh):
    placed = (
        P("tile", "sec"),
        P("tile", "sec"),
        P("tile", "sec"),
        P(None, "tile", "sec"),
        P(),
        P("tile"),
        P("tile", None),
        P("sec", "tile", None),
        P("sec", "tile", None, None, None),
    )
    return jax.shard_map(
        on_device,
        mesh=mesh,
        in_specs=placed,
        out_specs=(P("tile", "sec"), P(None, ("tile", "sec"))),
        check_vma=False,
    )
```

```python
import functools

import jax
import jax.numpy as jnp
from jax import lax
from jax.experimental import pallas as pl
from jax.experimental.pallas import tpu as pltpu
from jax.sharding import PartitionSpec as P

CONTACTS = 4096
TIME_STEP = 0.25
AXIAL = 2.0
END_ROWS = 48
PAIRED = True
SEQUENCE = (0, 6, 1, 7, 2, 5, 3, 4)
BF = jnp.bfloat16
F32 = jnp.float32
PARAMS = pltpu.CompilerParams(vmem_limit_bytes=24 * 1024 * 1024)


def split_hi_lo(x):
    hi = x.astype(BF)
    return hi, (x - hi.astype(F32)).astype(BF)


def one_hot(condition):
    return jnp.where(condition, 1.0, 0.0).astype(BF)


def iota(shape, dim):
    return lax.broadcasted_iota(jnp.int32, shape, dim)


def local_kernel(
    tiles,
    paired,
    v_hbm,
    g_hbm,
    e_hbm,
    drive_hbm,
    cable_hbm,
    owner_hbm,
    counts_hbm,
    pattern_hbm,
    transfer_hbm,
    vloc_ref,
    resp_ref,
    ends_ref,
    g_ref,
    e_ref,
    drive_ref,
    lags_ref,
    spread_ref,
    order_ref,
    pattern_ref,
    transfer_ref,
    v_ref,
    cable_ref,
    owner_ref,
    counts_ref,
    sems,
):
    pairs = [
        (g_hbm, g_ref),
        (v_hbm, v_ref),
        (e_hbm, e_ref),
        (cable_hbm, cable_ref),
        (drive_hbm, drive_ref),
        (owner_hbm, owner_ref),
        (counts_hbm, counts_ref),
        (pattern_hbm, pattern_ref),
        (transfer_hbm, transfer_ref),
    ]
    copies = [pltpu.make_async_copy(src, dst, sems.at[i]) for i, (src, dst) in enumerate(pairs)]
    for copy in copies:
        copy.start()
    for copy in copies[:5]:
        copy.wait()

    cells, width = v_ref.shape
    steps = drive_ref.shape[0]
    cond = g_ref[...]
    lane = iota((cells, width), 1)
    at_end = jnp.where((lane == 0) | (lane == width - 1), TIME_STEP * AXIAL, 0.0).astype(F32)
    keep = 1.0 - TIME_STEP * cond - at_end
    source = TIME_STEP * cond * e_ref[...]
    cable = cable_ref[...].T
    cable_hi, cable_lo = split_hi_lo(cable)
    half = jnp.concatenate([cable_hi, cable_lo], axis=1)
    weights = jnp.concatenate([half, half], axis=0)
    pick_row, pick_lane = iota((16, width), 0), iota((16, width), 1)
    pick = one_hot(
        ((pick_row == 0) & (pick_lane == 0)) | ((pick_row == 1) & (pick_lane == width - 1))
    )

    def solve(rhs):
        hi, lo = split_hi_lo(rhs)
        both = jnp.dot(jnp.concatenate([hi, lo], axis=1), weights, preferred_element_type=F32)
        return both[:, :width] + both[:, width:]

    def ends_of(x):
        return lax.dot_general(
            pick, x.astype(BF), (((1,), (1,)), ((), ())), preferred_element_type=F32
        )[0:2]

    voltage = v_ref[...]
    lag_left = TIME_STEP * AXIAL * cable[0:1, :]
    lag_right = TIME_STEP * AXIAL * cable[width - 1 : width, :]
    lags_ref[0:1, :] = lag_left
    lags_ref[1:2, :] = lag_right
    keep2 = jnp.concatenate([keep, keep], axis=0)
    resp = jnp.concatenate(
        [jnp.broadcast_to(lag_left, (cells, width)), jnp.broadcast_to(lag_right, (cells, width))],
        axis=0,
    )
    v_ends, l_ends, r_ends = [ends_of(voltage)], [], []
    both_ends = ends_of(resp)
    l_ends.append(both_ends[:, :cells])
    r_ends.append(both_ends[:, cells:])
    for k in range(steps):
        rhs = voltage * keep + source + TIME_STEP * drive_ref[k].astype(F32)
        if k < steps - 1:
            out = solve(jnp.concatenate([rhs, resp * keep2], axis=0))
            voltage, resp = out[:cells], out[cells:]
            resp_ref[k] = resp
            v_ends.append(ends_of(voltage))
            if k < steps - 2:
                both_ends = ends_of(resp)
                l_ends.append(both_ends[:, :cells])
                r_ends.append(both_ends[:, cells:])
        else:
            voltage = solve(rhs)
        vloc_ref[k] = voltage
    rows = v_ends + l_ends + r_ends
    rows.append(jnp.zeros((END_ROWS - 2 * len(rows), cells), F32))
    ends_ref[...] = jnp.concatenate(rows, axis=0).astype(BF)

    for copy in copies[5:7]:
        copy.wait()
    me = lax.axis_index("tile")
    row_count = spread_ref.shape[0]
    capacity = row_count // tiles
    owner = owner_ref[...]
    member = owner == iota((tiles, cells), 0)
    before = iota((cells, cells), 0) < iota((cells, cells), 1)
    rank = jnp.dot(one_hot(member), one_hot(before), preferred_element_type=F32)
    rank = jnp.sum(jnp.where(member, rank, 0.0), axis=0, keepdims=True).astype(jnp.int32)
    to = owner ^ me if paired else owner
    spread_ref[...] = one_hot(iota((row_count, cells), 0) == to * capacity + rank)

    counts = [counts_ref[0, u] for u in range(tiles)]
    row = iota((1, row_count), 1)
    slot_of = jnp.full((1, row_count), -1, jnp.int32)
    start = jnp.int32(0)
    for b in range(tiles):
        if paired:
            sender = b ^ me
            count = counts_ref[0, sender]
            start = sum(jnp.where(u < sender, counts[u], 0) for u in range(tiles))
        else:
            count = counts[b]
            start = start + (counts[b - 1] if b else 0)
        place = row - b * capacity
        slot_of = jnp.where((place >= 0) & (place < count), place + start, slot_of)
    order_ref[...] = one_hot(iota(order_ref.shape, 0) == slot_of)
    for copy in copies[7:]:
        copy.wait()


def couple_kernel(sections, block_count, *refs):
    ends_refs, refs = refs[:sections], refs[sections:]
    vloc_ref, resp_ref, g_ref, e_ref, drive_ref, lags_ref, spread_ref, *refs = refs
    final_hbm, *refs = refs
    out_refs, refs = refs[:block_count], refs[block_count:]
    ends32, incoming, leak, final_ref, sem = refs
    steps, cells, width = drive_ref.shape
    mine = lax.axis_index("sec")
    for p in range(sections):
        ends32[mine ^ p] = ends_refs[p][...].astype(F32)

    def rows(q):
        return ends32[:, q, :]

    base_l, base_r = 2 * steps, 4 * steps - 2
    left_a = [None] + [rows(base_l + 2 * l) for l in range(steps - 1)]
    left_b = [None] + [rows(base_l + 2 * l + 1) for l in range(steps - 1)]
    right_a = [None] + [rows(base_r + 2 * l) for l in range(steps - 1)]
    right_b = [None] + [rows(base_r + 2 * l + 1) for l in range(steps - 1)]
    zero = jnp.zeros((1, cells), F32)
    from_left, from_right = [], []
    for k in range(steps):
        first, last = rows(2 * k), rows(2 * k + 1)
        for j in range(k):
            first = first + (left_a[k - j] * from_left[j] + right_a[k - j] * from_right[j])
            last = last + (left_b[k - j] * from_left[j] + right_b[k - j] * from_right[j])
        from_left.append(jnp.concatenate([zero, last[:-1]], axis=0))
        from_right.append(jnp.concatenate([first[1:], zero], axis=0))
    own = iota((sections, cells), 0) == mine
    for j in range(steps):
        incoming[pl.ds(2 * j, 1), :] = jnp.sum(
            jnp.where(own, from_left[j], 0.0), axis=0, keepdims=True
        )
        incoming[pl.ds(2 * j + 1, 1), :] = jnp.sum(
            jnp.where(own, from_right[j], 0.0), axis=0, keepdims=True
        )
    by_cell = incoming[...].T

    block = 8
    lag_left = jnp.broadcast_to(lags_ref[0:1, :], (block, width))
    lag_right = jnp.broadcast_to(lags_ref[1:2, :], (block, width))
    for c in range(0, cells, block):
        span = slice(c, c + block)
        unit = [
            jnp.broadcast_to(by_cell[span, q : q + 1], (block, width)) for q in range(2 * steps)
        ]
        lefts = [None, lag_left] + [resp_ref[l, span, :] for l in range(steps - 1)]
        rights = [None, lag_right] + [
            resp_ref[l, cells + c : cells + c + block, :] for l in range(steps - 1)
        ]
        cond, rev = g_ref[span, :], e_ref[span, :]
        for k in range(1, steps + 1):
            total = vloc_ref[k - 1, span, :]
            for j in range(k):
                total = total + (unit[2 * j] * lefts[k - j] + unit[2 * j + 1] * rights[k - j])
            leak[k - 1, span, :] = cond * (total - rev)
        final_ref[span, :] = total
    give = pltpu.make_async_copy(final_ref, final_hbm, sem)
    give.start()

    capacity = out_refs[0].shape[0]
    for k in range(steps):
        current = (leak[k] - drive_ref[k].astype(F32)).astype(BF)
        placed = jnp.dot(spread_ref[...], current, preferred_element_type=F32).astype(BF)
        for b in range(block_count):
            out_refs[b][:, k * width : (k + 1) * width] = placed[b * capacity : (b + 1) * capacity]
    give.wait()


def readout_kernel(steps, sequence, pattern_ref, order_ref, *refs):
    *block_refs, transfer_ref, out_ref, slots, sums = refs
    block_refs = [block_refs[sequence.index(p)] for p in range(len(block_refs))]
    slot_count = order_ref.shape[0]
    kinds, width, contacts = transfer_ref.shape[1:]
    for k in range(steps):
        span = slice(k * width, (k + 1) * width)
        rows = jnp.concatenate([ref[:, span] for ref in block_refs], axis=0)
        slots[pl.ds(k, slot_count, stride=steps), :] = jnp.dot(
            order_ref[...], rows, preferred_element_type=F32
        )
    sums[...] = jnp.zeros_like(sums)
    ways = sums.shape[0]
    turn = 0
    for s in range(slot_count):
        current = slots[s * steps : (s + 1) * steps, :].astype(BF)
        tile = jnp.concatenate([transfer_ref[s, t] for t in range(kinds)], axis=1)
        reach = jnp.dot(current, tile, preferred_element_type=F32)
        for t in range(kinds):
            sums[turn % ways, pattern_ref[t, s]] += reach[:, t * contacts : (t + 1) * contacts]
            turn += 1
    out_ref[...] = sum(sums[w] for w in range(ways))


def in_hbm(x):
    return pltpu.with_memory_space_constraint(x, pltpu.HBM)


def exchange(blocks, axis):
    count = lax.axis_size(axis)
    arrived = [blocks[0]]
    for p in range(1, count):
        arrived.append(lax.ppermute(blocks[p], axis, [(i, i ^ p) for i in range(count)]))
    return arrived


def on_device(
    voltage, conductance, reversal, drive, inv_cable, owner_map, peer_counts, pattern, transfer
):
    cells, width = voltage.shape
    steps = drive.shape[0]
    tiles = lax.axis_size("tile")
    sections = lax.axis_size("sec")
    capacity = 2 * cells // tiles
    row_count = tiles * capacity
    weights = transfer[0]
    slot_count, kinds, _, contact_width = weights.shape
    paired = PAIRED and tiles == 8
    vmem = pl.BlockSpec(memory_space=pltpu.VMEM)
    smem = pl.BlockSpec(memory_space=pltpu.SMEM)
    hbm = pl.BlockSpec(memory_space=pltpu.HBM)

    vloc, resp, ends, cond, rev, driven, lags, spread, order, layout, tiles_here = pl.pallas_call(
        functools.partial(local_kernel, tiles, paired),
        out_shape=(
            jax.ShapeDtypeStruct((steps, cells, width), F32),
            jax.ShapeDtypeStruct((steps - 1, 2 * cells, width), F32),
            jax.ShapeDtypeStruct((END_ROWS, cells), BF),
            jax.ShapeDtypeStruct((cells, width), F32),
            jax.ShapeDtypeStruct((cells, width), F32),
            jax.ShapeDtypeStruct((steps, cells, width), BF),
            jax.ShapeDtypeStruct((2, width), F32),
            jax.ShapeDtypeStruct((row_count, cells), BF),
            jax.ShapeDtypeStruct((slot_count, row_count), BF),
            jax.ShapeDtypeStruct((kinds, slot_count), jnp.int32),
            jax.ShapeDtypeStruct(weights.shape, BF),
        ),
        in_specs=[hbm] * 9,
        out_specs=(vmem,) * 11,
        scratch_shapes=[
            pltpu.VMEM((cells, width), F32),
            pltpu.VMEM((width, width), F32),
            pltpu.VMEM((1, cells), jnp.int32),
            pltpu.SMEM((1, tiles), jnp.int32),
            pltpu.SemaphoreType.DMA((9,)),
        ],
        compiler_params=PARAMS,
        name="local_steps",
    )(
        in_hbm(voltage),
        in_hbm(conductance),
        in_hbm(reversal),
        in_hbm(drive),
        in_hbm(inv_cable),
        in_hbm(owner_map.reshape(1, cells)),
        in_hbm(peer_counts),
        in_hbm(pattern[0].T),
        in_hbm(weights),
    )

    all_ends = exchange([ends] * sections, "sec")
    block_count = tiles if paired else 1
    final_voltage, *outgoing = pl.pallas_call(
        functools.partial(couple_kernel, sections, block_count),
        out_shape=(
            jax.ShapeDtypeStruct((cells, width), F32),
        )
        + (jax.ShapeDtypeStruct((row_count // block_count, steps * width), BF),) * block_count,
        in_specs=[vmem] * (sections + 7),
        out_specs=(hbm,) + (vmem,) * block_count,
        scratch_shapes=[
            pltpu.VMEM((sections, END_ROWS, cells), F32),
            pltpu.VMEM((2 * steps, cells), F32),
            pltpu.VMEM((steps, cells, width), F32),
            pltpu.VMEM((cells, width), F32),
            pltpu.SemaphoreType.DMA,
        ],
        compiler_params=PARAMS,
        name="couple_sections",
    )(
        *all_ends,
        vloc,
        resp,
        cond,
        rev,
        driven,
        lags,
        spread,
    )

    if paired:
        arrived = exchange(outgoing, "tile")
    else:
        arrived = [lax.all_to_all(outgoing[0], "tile", split_axis=0, concat_axis=0, tiled=True)]

    sequence = SEQUENCE if paired else (0,)
    arrived = [arrived[p] for p in sequence]
    contact_tiles = CONTACTS // contact_width
    partial_sum = pl.pallas_call(
        functools.partial(readout_kernel, steps, sequence),
        out_shape=jax.ShapeDtypeStruct((contact_tiles, steps, contact_width), F32),
        in_specs=[smem] + [vmem] * (len(arrived) + 2),
        out_specs=vmem,
        scratch_shapes=[
            pltpu.VMEM((slot_count * steps, width), F32),
            pltpu.VMEM((4, contact_tiles, steps, contact_width), F32),
        ],
        compiler_params=PARAMS,
        name="readout",
    )(layout, order, *arrived, tiles_here)

    devices = tiles * sections
    share = CONTACTS // devices
    parts = contact_width // share
    if parts > 1:
        partial_sum = partial_sum.reshape(contact_tiles, steps, parts, share)
        partial_sum = partial_sum.transpose(0, 2, 1, 3).reshape(devices, steps, share)
    shares = lax.all_to_all(partial_sum, ("tile", "sec"), split_axis=0, concat_axis=0, tiled=True)
    return final_voltage, jnp.sum(shares, axis=0)


def solution(mesh):
    placed = (
        P("tile", "sec"),
        P("tile", "sec"),
        P("tile", "sec"),
        P(None, "tile", "sec"),
        P(),
        P("tile"),
        P("tile", None),
        P("sec", "tile", None),
        P("sec", "tile", None, None, None),
    )
    return jax.shard_map(
        on_device,
        mesh=mesh,
        in_specs=placed,
        out_specs=(P("tile", "sec"), P(None, ("tile", "sec"))),
        check_vma=False,
    )
```

```python
import functools

import jax
import jax.numpy as jnp
from jax import lax
from jax.experimental import pallas as pl
from jax.experimental.pallas import tpu as pltpu
from jax.sharding import PartitionSpec as P

CONTACTS = 4096
TIME_STEP = 0.25
AXIAL = 2.0
END_ROWS = 48
PAIRED = True
PARTS = (48, 16, 64)
SEQUENCE = (0, 6, 1, 7, 2, 5, 3, 4)
BF = jnp.bfloat16
F32 = jnp.float32
PARAMS = pltpu.CompilerParams(vmem_limit_bytes=24 * 1024 * 1024)


def split_hi_lo(x):
    hi = x.astype(BF)
    return hi, (x - hi.astype(F32)).astype(BF)


def one_hot(condition):
    return jnp.where(condition, 1.0, 0.0).astype(BF)


def iota(shape, dim):
    return lax.broadcasted_iota(jnp.int32, shape, dim)


def hi_lo_weights(cable):
    cable_hi, cable_lo = split_hi_lo(cable)
    half = jnp.concatenate([cable_hi, cable_lo], axis=1)
    return jnp.concatenate([half, half], axis=0)


def solve(rhs, weights):
    width = rhs.shape[1]
    hi, lo = split_hi_lo(rhs)
    both = jnp.dot(jnp.concatenate([hi, lo], axis=1), weights, preferred_element_type=F32)
    return both[:, :width] + both[:, width:]


def keep_and_source(cond, rev):
    lane = iota(cond.shape, 1)
    at_end = (lane == 0) | (lane == cond.shape[1] - 1)
    keep = 1.0 - TIME_STEP * cond - jnp.where(at_end, TIME_STEP * AXIAL, 0.0).astype(F32)
    return keep, TIME_STEP * cond * rev


def start_all(pairs, sems):
    copies = [pltpu.make_async_copy(src, dst, sems.at[i]) for i, (src, dst) in enumerate(pairs)]
    for copy in copies:
        copy.start()
    return copies


def local_kernel(
    v_hbm,
    g_hbm,
    e_hbm,
    drive_hbm,
    cable_hbm,
    transfer_hbm,
    vloc_ref,
    resp_ref,
    ends_ref,
    g_ref,
    e_ref,
    drive_ref,
    turned_ref,
    early_ref,
    v_ref,
    cable_ref,
    sems,
):
    copies = start_all(
        [
            (g_hbm, g_ref),
            (v_hbm, v_ref),
            (cable_hbm, cable_ref),
            (e_hbm, e_ref),
            (drive_hbm, drive_ref),
            (transfer_hbm.at[pl.ds(0, PARTS[0])], early_ref),
        ],
        sems,
    )
    for copy in copies[:5]:
        copy.wait()
    cells, width = v_ref.shape
    steps = drive_ref.shape[0]
    keep, source = keep_and_source(g_ref[...], e_ref[...])
    cable = cable_ref[...].T
    turned_ref[...] = cable
    weights = hi_lo_weights(cable)
    lane = iota((cells, width), 1)

    def with_ends(table, x, row):
        return jnp.where((lane >= row) & (lane < row + 2), pltpu.roll(x, row + 1, 1), table)

    voltage = v_ref[...]
    left = jnp.broadcast_to(TIME_STEP * AXIAL * cable[0:1, :], (cells, width))
    right = jnp.broadcast_to(TIME_STEP * AXIAL * cable[width - 1 : width, :], (cells, width))
    left_row, right_row = 2 * steps, 4 * steps
    table = with_ends(jnp.zeros((cells, width), F32), voltage, 0)
    table = with_ends(with_ends(table, left, left_row), right, right_row)
    for k in range(steps - 1):
        rhs = voltage * keep + source + TIME_STEP * drive_ref[k].astype(F32)
        voltage = solve(rhs, weights)
        left = solve(left * keep, weights)
        right = solve(right * keep, weights)
        vloc_ref[k] = voltage
        resp_ref[k, :cells] = left
        resp_ref[k, cells:] = right
        table = with_ends(table, voltage, 2 * (k + 1))
        if k < steps - 2:
            table = with_ends(table, left, left_row + 2 * (k + 1))
            table = with_ends(table, right, right_row + 2 * (k + 1))
    ends_ref[...] = table.T[:END_ROWS].astype(BF)
    copies[5].wait()


def prepare_kernel(
    tiles,
    paired,
    vloc_ref,
    g_ref,
    e_ref,
    drive_ref,
    turned_ref,
    owner_hbm,
    counts_hbm,
    pattern_hbm,
    transfer_hbm,
    vlast_ref,
    spread_ref,
    order_ref,
    pattern_ref,
    middle_ref,
    owner_ref,
    counts_ref,
    sems,
):
    copies = start_all(
        [
            (owner_hbm, owner_ref),
            (counts_hbm, counts_ref),
            (pattern_hbm, pattern_ref),
            (transfer_hbm.at[pl.ds(PARTS[0], PARTS[1])], middle_ref),
        ],
        sems,
    )
    steps, cells, _ = drive_ref.shape
    keep, source = keep_and_source(g_ref[...], e_ref[...])
    rhs = vloc_ref[steps - 2] * keep + source + TIME_STEP * drive_ref[steps - 1].astype(F32)
    vlast_ref[...] = solve(rhs, hi_lo_weights(turned_ref[...]))

    for copy in copies[:2]:
        copy.wait()
    me = lax.axis_index("tile")
    row_count = spread_ref.shape[0]
    capacity = row_count // tiles
    owner = owner_ref[...]
    member = owner == iota((tiles, cells), 0)
    before = iota((cells, cells), 0) < iota((cells, cells), 1)
    rank = jnp.dot(one_hot(member), one_hot(before), preferred_element_type=F32)
    rank = jnp.sum(jnp.where(member, rank, 0.0), axis=0, keepdims=True).astype(jnp.int32)
    to = owner ^ me if paired else owner
    spread_ref[...] = one_hot(iota((row_count, cells), 0) == to * capacity + rank)

    counts = [counts_ref[0, u] for u in range(tiles)]
    row = iota((1, row_count), 1)
    slot_of = jnp.full((1, row_count), -1, jnp.int32)
    start = jnp.int32(0)
    for b in range(tiles):
        if paired:
            sender = b ^ me
            count = counts_ref[0, sender]
            start = sum(jnp.where(u < sender, counts[u], 0) for u in range(tiles))
        else:
            count = counts[b]
            start = start + (counts[b - 1] if b else 0)
        place = row - b * capacity
        slot_of = jnp.where((place >= 0) & (place < count), place + start, slot_of)
    order_ref[...] = one_hot(iota(order_ref.shape, 0) == slot_of)
    for copy in copies[2:]:
        copy.wait()


def couple_kernel(sections, block_count, *refs):
    ends_refs, refs = refs[:sections], refs[sections:]
    vloc_ref, vlast_ref, resp_ref, g_ref, e_ref, drive_ref, turned_ref, spread_ref, *refs = refs
    final_hbm, *refs = refs
    out_refs, refs = refs[:block_count], refs[block_count:]
    ends32, incoming, leak, final_ref, sem = refs
    steps, cells, width = drive_ref.shape
    mine = lax.axis_index("sec")
    for p in range(sections):
        ends32[mine ^ p] = ends_refs[p][...].astype(F32)

    def rows(q):
        return ends32[:, q, :]

    def lagged(row):
        return [None] + [rows(row + 2 * l) for l in range(steps - 1)]

    left_b, left_a = lagged(2 * steps), lagged(2 * steps + 1)
    right_b, right_a = lagged(4 * steps), lagged(4 * steps + 1)
    zero = jnp.zeros((1, cells), F32)
    from_left, from_right = [], []
    for k in range(steps):
        last, first = rows(2 * k), rows(2 * k + 1)
        for j in range(k):
            first = first + (left_a[k - j] * from_left[j] + right_a[k - j] * from_right[j])
            last = last + (left_b[k - j] * from_left[j] + right_b[k - j] * from_right[j])
        from_left.append(jnp.concatenate([zero, last[:-1]], axis=0))
        from_right.append(jnp.concatenate([first[1:], zero], axis=0))
    own = iota((sections, cells), 0) == mine
    for j in range(steps):
        incoming[pl.ds(2 * j, 1), :] = jnp.sum(
            jnp.where(own, from_left[j], 0.0), axis=0, keepdims=True
        )
        incoming[pl.ds(2 * j + 1, 1), :] = jnp.sum(
            jnp.where(own, from_right[j], 0.0), axis=0, keepdims=True
        )
    by_cell = incoming[...].T

    block = 8
    lag_left = jnp.broadcast_to(TIME_STEP * AXIAL * turned_ref[0:1, :], (block, width))
    lag_right = jnp.broadcast_to(
        TIME_STEP * AXIAL * turned_ref[width - 1 : width, :], (block, width)
    )
    for c in range(0, cells, block):
        span = slice(c, c + block)
        unit = [
            jnp.broadcast_to(by_cell[span, q : q + 1], (block, width)) for q in range(2 * steps)
        ]
        lefts = [None, lag_left] + [resp_ref[l, span, :] for l in range(steps - 1)]
        rights = [None, lag_right] + [
            resp_ref[l, cells + c : cells + c + block, :] for l in range(steps - 1)
        ]
        cond, rev = g_ref[span, :], e_ref[span, :]
        for k in range(1, steps + 1):
            total = vloc_ref[k - 1, span, :] if k < steps else vlast_ref[span, :]
            for j in range(k):
                total = total + (unit[2 * j] * lefts[k - j] + unit[2 * j + 1] * rights[k - j])
            leak[k - 1, span, :] = cond * (total - rev)
        final_ref[span, :] = total
    give = pltpu.make_async_copy(final_ref, final_hbm, sem)
    give.start()

    capacity = out_refs[0].shape[0]
    for k in range(steps):
        current = (leak[k] - drive_ref[k].astype(F32)).astype(BF)
        placed = jnp.dot(spread_ref[...], current, preferred_element_type=F32).astype(BF)
        for b in range(block_count):
            out_refs[b][:, k * width : (k + 1) * width] = placed[b * capacity : (b + 1) * capacity]
    give.wait()


def fetch_kernel(after_ref, transfer_hbm, late_ref, sem):
    del after_ref
    copy = pltpu.make_async_copy(
        transfer_hbm.at[pl.ds(PARTS[0] + PARTS[1], PARTS[2])], late_ref, sem
    )
    copy.start()
    copy.wait()


def readout_kernel(steps, sequence, pattern_ref, order_ref, *refs):
    *block_refs, early_ref, middle_ref, late_ref, out_ref, slots, sums = refs
    held = [(ref, at) for ref in (early_ref, middle_ref, late_ref) for at in range(ref.shape[0])]
    block_refs = [block_refs[sequence.index(p)] for p in range(len(block_refs))]
    slot_count = order_ref.shape[0]
    kinds, width, contacts = early_ref.shape[1:]
    for k in range(steps):
        span = slice(k * width, (k + 1) * width)
        rows = jnp.concatenate([ref[:, span] for ref in block_refs], axis=0)
        slots[pl.ds(k, slot_count, stride=steps), :] = jnp.dot(
            order_ref[...], rows, preferred_element_type=F32
        )
    sums[...] = jnp.zeros_like(sums)
    ways = sums.shape[0]
    turn = 0
    for s in range(slot_count):
        current = slots[s * steps : (s + 1) * steps, :].astype(BF)
        ref, at = held[s]
        tile = jnp.concatenate([ref[at, t] for t in range(kinds)], axis=1)
        reach = jnp.dot(current, tile, preferred_element_type=F32)
        for t in range(kinds):
            sums[turn % ways, pattern_ref[t, s]] += reach[:, t * contacts : (t + 1) * contacts]
            turn += 1
    out_ref[...] = sum(sums[w] for w in range(ways))


def in_hbm(x):
    return pltpu.with_memory_space_constraint(x, pltpu.HBM)


def exchange(blocks, axis):
    count = lax.axis_size(axis)
    arrived = [blocks[0]]
    for p in range(1, count):
        arrived.append(lax.ppermute(blocks[p], axis, [(i, i ^ p) for i in range(count)]))
    return arrived


def on_device(
    voltage, conductance, reversal, drive, inv_cable, owner_map, peer_counts, pattern, transfer
):
    cells, width = voltage.shape
    steps = drive.shape[0]
    tiles = lax.axis_size("tile")
    sections = lax.axis_size("sec")
    capacity = 2 * cells // tiles
    row_count = tiles * capacity
    weights = transfer[0]
    slot_count, kinds, _, contact_width = weights.shape
    paired = PAIRED and tiles == 8
    vmem = pl.BlockSpec(memory_space=pltpu.VMEM)
    smem = pl.BlockSpec(memory_space=pltpu.SMEM)
    hbm = pl.BlockSpec(memory_space=pltpu.HBM)

    vloc, resp, ends, cond, rev, driven, turned, early_tiles = pl.pallas_call(
        local_kernel,
        out_shape=(
            jax.ShapeDtypeStruct((steps - 1, cells, width), F32),
            jax.ShapeDtypeStruct((steps - 1, 2 * cells, width), F32),
            jax.ShapeDtypeStruct((END_ROWS, cells), BF),
            jax.ShapeDtypeStruct((cells, width), F32),
            jax.ShapeDtypeStruct((cells, width), F32),
            jax.ShapeDtypeStruct((steps, cells, width), BF),
            jax.ShapeDtypeStruct((width, width), F32),
            jax.ShapeDtypeStruct((PARTS[0],) + weights.shape[1:], BF),
        ),
        in_specs=[hbm] * 6,
        out_specs=(vmem,) * 8,
        scratch_shapes=[
            pltpu.VMEM((cells, width), F32),
            pltpu.VMEM((width, width), F32),
            pltpu.SemaphoreType.DMA((6,)),
        ],
        compiler_params=PARAMS,
        name="local_steps",
    )(
        in_hbm(voltage),
        in_hbm(conductance),
        in_hbm(reversal),
        in_hbm(drive),
        in_hbm(inv_cable),
        in_hbm(weights),
    )

    vlast, spread, order, layout, middle_tiles = pl.pallas_call(
        functools.partial(prepare_kernel, tiles, paired),
        out_shape=(
            jax.ShapeDtypeStruct((cells, width), F32),
            jax.ShapeDtypeStruct((row_count, cells), BF),
            jax.ShapeDtypeStruct((slot_count, row_count), BF),
            jax.ShapeDtypeStruct((kinds, slot_count), jnp.int32),
            jax.ShapeDtypeStruct((PARTS[1],) + weights.shape[1:], BF),
        ),
        in_specs=[vmem] * 5 + [hbm] * 4,
        out_specs=(vmem,) * 5,
        scratch_shapes=[
            pltpu.VMEM((1, cells), jnp.int32),
            pltpu.SMEM((1, tiles), jnp.int32),
            pltpu.SemaphoreType.DMA((4,)),
        ],
        compiler_params=PARAMS,
        name="prepare_rows",
    )(
        vloc,
        cond,
        rev,
        driven,
        turned,
        in_hbm(owner_map.reshape(1, cells)),
        in_hbm(peer_counts),
        in_hbm(pattern[0].T),
        in_hbm(weights),
    )

    all_ends = exchange([ends] * sections, "sec")
    block_count = tiles if paired else 1
    final_voltage, *outgoing = pl.pallas_call(
        functools.partial(couple_kernel, sections, block_count),
        out_shape=(
            jax.ShapeDtypeStruct((cells, width), F32),
        )
        + (jax.ShapeDtypeStruct((row_count // block_count, steps * width), BF),) * block_count,
        in_specs=[vmem] * (sections + 8),
        out_specs=(hbm,) + (vmem,) * block_count,
        scratch_shapes=[
            pltpu.VMEM((sections, END_ROWS, cells), F32),
            pltpu.VMEM((2 * steps, cells), F32),
            pltpu.VMEM((steps, cells, width), F32),
            pltpu.VMEM((cells, width), F32),
            pltpu.SemaphoreType.DMA,
        ],
        compiler_params=PARAMS,
        name="couple_sections",
    )(
        *all_ends,
        vloc,
        vlast,
        resp,
        cond,
        rev,
        driven,
        turned,
        spread,
    )

    if paired:
        arrived = exchange(outgoing, "tile")
    else:
        arrived = [lax.all_to_all(outgoing[0], "tile", split_axis=0, concat_axis=0, tiled=True)]

    late_tiles = pl.pallas_call(
        fetch_kernel,
        out_shape=jax.ShapeDtypeStruct((PARTS[2],) + weights.shape[1:], BF),
        in_specs=[vmem, hbm],
        out_specs=vmem,
        scratch_shapes=[pltpu.SemaphoreType.DMA],
        compiler_params=PARAMS,
        name="fetch_tiles",
    )(outgoing[0], in_hbm(weights))

    sequence = SEQUENCE if paired else (0,)
    arrived = [arrived[p] for p in sequence]
    contact_tiles = CONTACTS // contact_width
    partial_sum = pl.pallas_call(
        functools.partial(readout_kernel, steps, sequence),
        out_shape=jax.ShapeDtypeStruct((contact_tiles, steps, contact_width), F32),
        in_specs=[smem] + [vmem] * (len(arrived) + 4),
        out_specs=vmem,
        scratch_shapes=[
            pltpu.VMEM((slot_count * steps, width), F32),
            pltpu.VMEM((4, contact_tiles, steps, contact_width), F32),
        ],
        compiler_params=PARAMS,
        name="readout",
    )(layout, order, *arrived, early_tiles, middle_tiles, late_tiles)

    devices = tiles * sections
    share = CONTACTS // devices
    parts = contact_width // share
    if parts > 1:
        partial_sum = partial_sum.reshape(contact_tiles, steps, parts, share)
        partial_sum = partial_sum.transpose(0, 2, 1, 3).reshape(devices, steps, share)
    shares = lax.all_to_all(partial_sum, ("tile", "sec"), split_axis=0, concat_axis=0, tiled=True)
    return final_voltage, jnp.sum(shares, axis=0)


def solution(mesh):
    placed = (
        P("tile", "sec"),
        P("tile", "sec"),
        P("tile", "sec"),
        P(None, "tile", "sec"),
        P(),
        P("tile"),
        P("tile", None),
        P("sec", "tile", None),
        P("sec", "tile", None, None, None),
    )
    return jax.shard_map(
        on_device,
        mesh=mesh,
        in_specs=placed,
        out_specs=(P("tile", "sec"), P(None, ("tile", "sec"))),
        check_vma=False,
    )
```

```python
import functools

import jax
import jax.numpy as jnp
from jax import lax
from jax.experimental import pallas as pl
from jax.experimental.pallas import tpu as pltpu
from jax.sharding import PartitionSpec as P

CONTACTS = 4096
TIME_STEP = 0.25
AXIAL = 2.0
END_ROWS = 48
PAIRED = True
PARTS = (48, 16, 64)
SEQUENCE = (0, 6, 1, 7, 2, 5, 3, 4)
BF = jnp.bfloat16
F32 = jnp.float32
PARAMS = pltpu.CompilerParams(vmem_limit_bytes=24 * 1024 * 1024)


def split_hi_lo(x):
    hi = x.astype(BF)
    return hi, (x - hi.astype(F32)).astype(BF)


def one_hot(condition):
    return jnp.where(condition, 1.0, 0.0).astype(BF)


def iota(shape, dim):
    return lax.broadcasted_iota(jnp.int32, shape, dim)


def hi_lo_weights(cable):
    cable_hi, cable_lo = split_hi_lo(cable)
    half = jnp.concatenate([cable_hi, cable_lo], axis=1)
    return jnp.concatenate([half, half], axis=0)


def solve(rhs, weights):
    width = rhs.shape[1]
    hi, lo = split_hi_lo(rhs)
    both = jnp.dot(jnp.concatenate([hi, lo], axis=1), weights, preferred_element_type=F32)
    return both[:, :width] + both[:, width:]


def keep_and_source(cond, rev):
    lane = iota(cond.shape, 1)
    at_end = (lane == 0) | (lane == cond.shape[1] - 1)
    keep = 1.0 - TIME_STEP * cond - jnp.where(at_end, TIME_STEP * AXIAL, 0.0).astype(F32)
    return keep, TIME_STEP * cond * rev


def start_all(pairs, sems):
    copies = [pltpu.make_async_copy(src, dst, sems.at[i]) for i, (src, dst) in enumerate(pairs)]
    for copy in copies:
        copy.start()
    return copies


def local_kernel(
    v_hbm,
    g_hbm,
    e_hbm,
    drive_hbm,
    cable_hbm,
    transfer_hbm,
    vloc_ref,
    resp_ref,
    ends_ref,
    g_ref,
    e_ref,
    drive_ref,
    turned_ref,
    early_ref,
    v_ref,
    cable_ref,
    sems,
):
    copies = start_all(
        [
            (g_hbm, g_ref),
            (v_hbm, v_ref),
            (cable_hbm, cable_ref),
            (e_hbm, e_ref),
            (drive_hbm, drive_ref),
            (transfer_hbm.at[pl.ds(0, PARTS[0])], early_ref),
        ],
        sems,
    )
    for copy in copies[:5]:
        copy.wait()
    cells, width = v_ref.shape
    steps = drive_ref.shape[0]
    keep, source = keep_and_source(g_ref[...], e_ref[...])
    cable = cable_ref[...].T
    turned_ref[...] = cable
    weights = hi_lo_weights(cable)
    lane = iota((cells, width), 1)

    def with_ends(table, x, row):
        return jnp.where((lane >= row) & (lane < row + 2), pltpu.roll(x, row + 1, 1), table)

    voltage = v_ref[...]
    left = jnp.broadcast_to(TIME_STEP * AXIAL * cable[0:1, :], (cells, width))
    right = jnp.broadcast_to(TIME_STEP * AXIAL * cable[width - 1 : width, :], (cells, width))
    left_row, right_row = 2 * steps, 4 * steps
    table = with_ends(jnp.zeros((cells, width), F32), voltage, 0)
    table = with_ends(with_ends(table, left, left_row), right, right_row)
    for k in range(steps - 1):
        rhs = voltage * keep + source + TIME_STEP * drive_ref[k].astype(F32)
        voltage = solve(rhs, weights)
        left = solve(left * keep, weights)
        right = solve(right * keep, weights)
        vloc_ref[k] = voltage
        resp_ref[k, :cells] = left
        resp_ref[k, cells:] = right
        table = with_ends(table, voltage, 2 * (k + 1))
        if k < steps - 2:
            table = with_ends(table, left, left_row + 2 * (k + 1))
            table = with_ends(table, right, right_row + 2 * (k + 1))
    ends_ref[...] = table.T[:END_ROWS].astype(BF)
    copies[5].wait()


def prepare_kernel(
    tiles,
    paired,
    vloc_ref,
    g_ref,
    e_ref,
    drive_ref,
    turned_ref,
    owner_hbm,
    counts_hbm,
    pattern_hbm,
    transfer_hbm,
    vlast_ref,
    spread_ref,
    order_ref,
    select_ref,
    middle_ref,
    owner_ref,
    counts_ref,
    pattern_ref,
    sems,
):
    copies = start_all(
        [
            (owner_hbm, owner_ref),
            (counts_hbm, counts_ref),
            (pattern_hbm, pattern_ref),
            (transfer_hbm.at[pl.ds(PARTS[0], PARTS[1])], middle_ref),
        ],
        sems,
    )
    steps, cells, _ = drive_ref.shape
    keep, source = keep_and_source(g_ref[...], e_ref[...])
    rhs = vloc_ref[steps - 2] * keep + source + TIME_STEP * drive_ref[steps - 1].astype(F32)
    vlast_ref[...] = solve(rhs, hi_lo_weights(turned_ref[...]))

    for copy in copies[:2]:
        copy.wait()
    me = lax.axis_index("tile")
    row_count = spread_ref.shape[0]
    capacity = row_count // tiles
    owner = owner_ref[...]
    member = owner == iota((tiles, cells), 0)
    before = iota((cells, cells), 0) < iota((cells, cells), 1)
    rank = jnp.dot(one_hot(member), one_hot(before), preferred_element_type=F32)
    rank = jnp.sum(jnp.where(member, rank, 0.0), axis=0, keepdims=True).astype(jnp.int32)
    to = owner ^ me if paired else owner
    spread_ref[...] = one_hot(iota((row_count, cells), 0) == to * capacity + rank)

    counts = [counts_ref[0, u] for u in range(tiles)]
    row = iota((1, row_count), 1)
    slot_of = jnp.full((1, row_count), -1, jnp.int32)
    start = jnp.int32(0)
    for b in range(tiles):
        if paired:
            sender = b ^ me
            count = counts_ref[0, sender]
            start = sum(jnp.where(u < sender, counts[u], 0) for u in range(tiles))
        else:
            count = counts[b]
            start = start + (counts[b - 1] if b else 0)
        place = row - b * capacity
        slot_of = jnp.where((place >= 0) & (place < count), place + start, slot_of)
    order_ref[...] = one_hot(iota(order_ref.shape, 0) == slot_of)
    copies[2].wait()
    contact_tiles = select_ref.shape[0]
    kinds, slot_count = pattern_ref.shape
    for t in range(kinds):
        select_ref[:, t * slot_count : (t + 1) * slot_count] = one_hot(
            iota((contact_tiles, slot_count), 0) == pattern_ref[t : t + 1, :]
        )
    copies[3].wait()


def couple_kernel(sections, block_count, *refs):
    ends_refs, refs = refs[:sections], refs[sections:]
    vloc_ref, vlast_ref, resp_ref, g_ref, e_ref, drive_ref, turned_ref, spread_ref, *refs = refs
    final_hbm, *refs = refs
    out_refs, refs = refs[:block_count], refs[block_count:]
    ends32, incoming, leak, final_ref, sem = refs
    steps, cells, width = drive_ref.shape
    mine = lax.axis_index("sec")
    for p in range(sections):
        ends32[mine ^ p] = ends_refs[p][...].astype(F32)

    def rows(q):
        return ends32[:, q, :]

    def lagged(row):
        return [None] + [rows(row + 2 * l) for l in range(steps - 1)]

    left_b, left_a = lagged(2 * steps), lagged(2 * steps + 1)
    right_b, right_a = lagged(4 * steps), lagged(4 * steps + 1)
    zero = jnp.zeros((1, cells), F32)
    from_left, from_right = [], []
    for k in range(steps):
        last, first = rows(2 * k), rows(2 * k + 1)
        for j in range(k):
            first = first + (left_a[k - j] * from_left[j] + right_a[k - j] * from_right[j])
            last = last + (left_b[k - j] * from_left[j] + right_b[k - j] * from_right[j])
        from_left.append(jnp.concatenate([zero, last[:-1]], axis=0))
        from_right.append(jnp.concatenate([first[1:], zero], axis=0))
    own = iota((sections, cells), 0) == mine
    for j in range(steps):
        incoming[pl.ds(2 * j, 1), :] = jnp.sum(
            jnp.where(own, from_left[j], 0.0), axis=0, keepdims=True
        )
        incoming[pl.ds(2 * j + 1, 1), :] = jnp.sum(
            jnp.where(own, from_right[j], 0.0), axis=0, keepdims=True
        )
    by_cell = incoming[...].T

    block = 8
    lag_left = jnp.broadcast_to(TIME_STEP * AXIAL * turned_ref[0:1, :], (block, width))
    lag_right = jnp.broadcast_to(
        TIME_STEP * AXIAL * turned_ref[width - 1 : width, :], (block, width)
    )
    for c in range(0, cells, block):
        span = slice(c, c + block)
        unit = [
            jnp.broadcast_to(by_cell[span, q : q + 1], (block, width)) for q in range(2 * steps)
        ]
        lefts = [None, lag_left] + [resp_ref[l, span, :] for l in range(steps - 1)]
        rights = [None, lag_right] + [
            resp_ref[l, cells + c : cells + c + block, :] for l in range(steps - 1)
        ]
        cond, rev = g_ref[span, :], e_ref[span, :]
        for k in range(1, steps + 1):
            total = vloc_ref[k - 1, span, :] if k < steps else vlast_ref[span, :]
            for j in range(k):
                total = total + (unit[2 * j] * lefts[k - j] + unit[2 * j + 1] * rights[k - j])
            leak[k - 1, span, :] = cond * (total - rev)
        final_ref[span, :] = total
    give = pltpu.make_async_copy(final_ref, final_hbm, sem)
    give.start()

    capacity = out_refs[0].shape[0]
    for k in range(0, steps, 2):
        current = [(leak[i] - drive_ref[i].astype(F32)).astype(BF) for i in (k, k + 1)]
        placed = jnp.dot(
            spread_ref[...], jnp.concatenate(current, axis=1), preferred_element_type=F32
        ).astype(BF)
        for b in range(block_count):
            out_refs[b][:, k * width : (k + 2) * width] = placed[b * capacity : (b + 1) * capacity]
    give.wait()


def fetch_kernel(after_ref, transfer_hbm, late_ref, sem):
    del after_ref
    copy = pltpu.make_async_copy(
        transfer_hbm.at[pl.ds(PARTS[0] + PARTS[1], PARTS[2])], late_ref, sem
    )
    copy.start()
    copy.wait()


def readout_kernel(steps, sequence, select_ref, order_ref, *refs):
    *block_refs, early_ref, middle_ref, late_ref, out_ref, slots, reach = refs
    held = [(ref, at) for ref in (early_ref, middle_ref, late_ref) for at in range(ref.shape[0])]
    block_refs = [block_refs[sequence.index(p)] for p in range(len(block_refs))]
    slot_count = order_ref.shape[0]
    kinds, width, contacts = early_ref.shape[1:]
    for k in range(0, steps, 2):
        span = slice(k * width, (k + 2) * width)
        rows = jnp.concatenate([ref[:, span] for ref in block_refs], axis=0)
        both = jnp.dot(order_ref[...], rows, preferred_element_type=F32)
        for i in range(2):
            slots[pl.ds(k + i, slot_count, stride=steps), :] = both[:, i * width : (i + 1) * width]
    for s, (ref, at) in enumerate(held):
        current = slots[s * steps : (s + 1) * steps, :].astype(BF)
        tile = jnp.concatenate([ref[at, t] for t in range(kinds)], axis=1)
        product = jnp.dot(current, tile, preferred_element_type=F32)
        for t in range(kinds):
            row = (t * slot_count + s) * steps
            reach[row : row + steps, :] = product[:, t * contacts : (t + 1) * contacts]
    for k in range(steps):
        hi, lo = split_hi_lo(reach[pl.ds(k, kinds * slot_count, stride=steps), :])
        both = jnp.dot(
            select_ref[...], jnp.concatenate([hi, lo], axis=1), preferred_element_type=F32
        )
        out_ref[:, k, :] = both[:, :contacts] + both[:, contacts:]


def in_hbm(x):
    return pltpu.with_memory_space_constraint(x, pltpu.HBM)


def exchange(blocks, axis):
    count = lax.axis_size(axis)
    arrived = [blocks[0]]
    for p in range(1, count):
        arrived.append(lax.ppermute(blocks[p], axis, [(i, i ^ p) for i in range(count)]))
    return arrived


def on_device(
    voltage, conductance, reversal, drive, inv_cable, owner_map, peer_counts, pattern, transfer
):
    cells, width = voltage.shape
    steps = drive.shape[0]
    tiles = lax.axis_size("tile")
    sections = lax.axis_size("sec")
    capacity = 2 * cells // tiles
    row_count = tiles * capacity
    weights = transfer[0]
    slot_count, kinds, _, contact_width = weights.shape
    contact_tiles = CONTACTS // contact_width
    paired = PAIRED and tiles == 8
    vmem = pl.BlockSpec(memory_space=pltpu.VMEM)
    hbm = pl.BlockSpec(memory_space=pltpu.HBM)

    vloc, resp, ends, cond, rev, driven, turned, early_tiles = pl.pallas_call(
        local_kernel,
        out_shape=(
            jax.ShapeDtypeStruct((steps - 1, cells, width), F32),
            jax.ShapeDtypeStruct((steps - 1, 2 * cells, width), F32),
            jax.ShapeDtypeStruct((END_ROWS, cells), BF),
            jax.ShapeDtypeStruct((cells, width), F32),
            jax.ShapeDtypeStruct((cells, width), F32),
            jax.ShapeDtypeStruct((steps, cells, width), BF),
            jax.ShapeDtypeStruct((width, width), F32),
            jax.ShapeDtypeStruct((PARTS[0],) + weights.shape[1:], BF),
        ),
        in_specs=[hbm] * 6,
        out_specs=(vmem,) * 8,
        scratch_shapes=[
            pltpu.VMEM((cells, width), F32),
            pltpu.VMEM((width, width), F32),
            pltpu.SemaphoreType.DMA((6,)),
        ],
        compiler_params=PARAMS,
        name="local_steps",
    )(
        in_hbm(voltage),
        in_hbm(conductance),
        in_hbm(reversal),
        in_hbm(drive),
        in_hbm(inv_cable),
        in_hbm(weights),
    )

    vlast, spread, order, select, middle_tiles = pl.pallas_call(
        functools.partial(prepare_kernel, tiles, paired),
        out_shape=(
            jax.ShapeDtypeStruct((cells, width), F32),
            jax.ShapeDtypeStruct((row_count, cells), BF),
            jax.ShapeDtypeStruct((slot_count, row_count), BF),
            jax.ShapeDtypeStruct((contact_tiles, kinds * slot_count), BF),
            jax.ShapeDtypeStruct((PARTS[1],) + weights.shape[1:], BF),
        ),
        in_specs=[vmem] * 5 + [hbm] * 4,
        out_specs=(vmem,) * 5,
        scratch_shapes=[
            pltpu.VMEM((1, cells), jnp.int32),
            pltpu.SMEM((1, tiles), jnp.int32),
            pltpu.VMEM((kinds, slot_count), jnp.int32),
            pltpu.SemaphoreType.DMA((4,)),
        ],
        compiler_params=PARAMS,
        name="prepare_rows",
    )(
        vloc,
        cond,
        rev,
        driven,
        turned,
        in_hbm(owner_map.reshape(1, cells)),
        in_hbm(peer_counts),
        in_hbm(pattern[0].T),
        in_hbm(weights),
    )

    all_ends = exchange([ends] * sections, "sec")
    block_count = tiles if paired else 1
    final_voltage, *outgoing = pl.pallas_call(
        functools.partial(couple_kernel, sections, block_count),
        out_shape=(
            jax.ShapeDtypeStruct((cells, width), F32),
        )
        + (jax.ShapeDtypeStruct((row_count // block_count, steps * width), BF),) * block_count,
        in_specs=[vmem] * (sections + 8),
        out_specs=(hbm,) + (vmem,) * block_count,
        scratch_shapes=[
            pltpu.VMEM((sections, END_ROWS, cells), F32),
            pltpu.VMEM((2 * steps, cells), F32),
            pltpu.VMEM((steps, cells, width), F32),
            pltpu.VMEM((cells, width), F32),
            pltpu.SemaphoreType.DMA,
        ],
        compiler_params=PARAMS,
        name="couple_sections",
    )(
        *all_ends,
        vloc,
        vlast,
        resp,
        cond,
        rev,
        driven,
        turned,
        spread,
    )

    if paired:
        arrived = exchange(outgoing, "tile")
    else:
        arrived = [lax.all_to_all(outgoing[0], "tile", split_axis=0, concat_axis=0, tiled=True)]

    late_tiles = pl.pallas_call(
        fetch_kernel,
        out_shape=jax.ShapeDtypeStruct((PARTS[2],) + weights.shape[1:], BF),
        in_specs=[vmem, hbm],
        out_specs=vmem,
        scratch_shapes=[pltpu.SemaphoreType.DMA],
        compiler_params=PARAMS,
        name="fetch_tiles",
    )(outgoing[0], in_hbm(weights))

    sequence = SEQUENCE if paired else (0,)
    arrived = [arrived[p] for p in sequence]
    partial_sum = pl.pallas_call(
        functools.partial(readout_kernel, steps, sequence),
        out_shape=jax.ShapeDtypeStruct((contact_tiles, steps, contact_width), F32),
        in_specs=[vmem] * (len(arrived) + 5),
        out_specs=vmem,
        scratch_shapes=[
            pltpu.VMEM((slot_count * steps, width), F32),
            pltpu.VMEM((kinds * slot_count * steps, contact_width), F32),
        ],
        compiler_params=PARAMS,
        name="readout",
    )(select, order, *arrived, early_tiles, middle_tiles, late_tiles)

    devices = tiles * sections
    share = CONTACTS // devices
    parts = contact_width // share
    if parts > 1:
        partial_sum = partial_sum.reshape(contact_tiles, steps, parts, share)
        partial_sum = partial_sum.transpose(0, 2, 1, 3).reshape(devices, steps, share)
    shares = lax.all_to_all(partial_sum, ("tile", "sec"), split_axis=0, concat_axis=0, tiled=True)
    return final_voltage, jnp.sum(shares, axis=0)


def solution(mesh):
    placed = (
        P("tile", "sec"),
        P("tile", "sec"),
        P("tile", "sec"),
        P(None, "tile", "sec"),
        P(),
        P("tile"),
        P("tile", None),
        P("sec", "tile", None),
        P("sec", "tile", None, None, None),
    )
    return jax.shard_map(
        on_device,
        mesh=mesh,
        in_specs=placed,
        out_specs=(P("tile", "sec"), P(None, ("tile", "sec"))),
        check_vma=False,
    )
```

```python
import functools

import jax
import jax.numpy as jnp
from jax import lax
from jax.experimental import pallas as pl
from jax.experimental.pallas import tpu as pltpu
from jax.sharding import PartitionSpec as P

CONTACTS = 4096
TIME_STEP = 0.25
AXIAL = 2.0
END_ROWS = 48
PAIRED = True
PARTS = (48, 16, 64)
SEC_SEQUENCE = (0, 3, 2, 1)
SEQUENCE = (0, 6, 1, 7, 2, 4, 3, 5)
BF = jnp.bfloat16
F32 = jnp.float32
PARAMS = pltpu.CompilerParams(vmem_limit_bytes=24 * 1024 * 1024)


def split_hi_lo(x):
    hi = x.astype(BF)
    return hi, (x - hi.astype(F32)).astype(BF)


def one_hot(condition):
    return jnp.where(condition, 1.0, 0.0).astype(BF)


def iota(shape, dim):
    return lax.broadcasted_iota(jnp.int32, shape, dim)


def hi_lo_weights(cable):
    cable_hi, cable_lo = split_hi_lo(cable)
    half = jnp.concatenate([cable_hi, cable_lo], axis=1)
    return jnp.concatenate([half, half], axis=0)


def solve(rhs, weights):
    width = rhs.shape[1]
    hi, lo = split_hi_lo(rhs)
    both = jnp.dot(jnp.concatenate([hi, lo], axis=1), weights, preferred_element_type=F32)
    return both[:, :width] + both[:, width:]


def keep_and_source(cond, rev):
    lane = iota(cond.shape, 1)
    at_end = (lane == 0) | (lane == cond.shape[1] - 1)
    keep = 1.0 - TIME_STEP * cond - jnp.where(at_end, TIME_STEP * AXIAL, 0.0).astype(F32)
    return keep, TIME_STEP * cond * rev


def start_all(pairs, sems):
    copies = [pltpu.make_async_copy(src, dst, sems.at[i]) for i, (src, dst) in enumerate(pairs)]
    for copy in copies:
        copy.start()
    return copies


def local_kernel(
    v_hbm,
    g_hbm,
    e_hbm,
    drive_hbm,
    cable_hbm,
    transfer_hbm,
    vloc_ref,
    resp_ref,
    ends_ref,
    g_ref,
    e_ref,
    drive_ref,
    turned_ref,
    early_ref,
    v_ref,
    cable_ref,
    sems,
):
    copies = start_all(
        [
            (cable_hbm, cable_ref),
            (v_hbm, v_ref),
            (g_hbm, g_ref),
            (e_hbm, e_ref),
            (drive_hbm, drive_ref),
            (transfer_hbm.at[pl.ds(0, PARTS[0])], early_ref),
        ],
        sems,
    )
    cells, width = v_ref.shape
    steps = drive_ref.shape[0]
    copies[0].wait()
    cable = cable_ref[...].T
    turned_ref[...] = cable
    weights = hi_lo_weights(cable)
    for copy in copies[1:5]:
        copy.wait()
    keep, source = keep_and_source(g_ref[...], e_ref[...])
    lane = iota((cells, width), 1)

    def with_ends(table, x, row):
        return jnp.where((lane >= row) & (lane < row + 2), pltpu.roll(x, row + 1, 1), table)

    voltage = v_ref[...]
    left = jnp.broadcast_to(TIME_STEP * AXIAL * cable[0:1, :], (cells, width))
    right = jnp.broadcast_to(TIME_STEP * AXIAL * cable[width - 1 : width, :], (cells, width))
    left_row, right_row = 2 * steps, 4 * steps
    table = with_ends(jnp.zeros((cells, width), F32), voltage, 0)
    table = with_ends(with_ends(table, left, left_row), right, right_row)
    for k in range(steps - 1):
        rhs = voltage * keep + source + TIME_STEP * drive_ref[k].astype(F32)
        voltage = solve(rhs, weights)
        left = solve(left * keep, weights)
        right = solve(right * keep, weights)
        vloc_ref[k] = voltage
        resp_ref[k, :cells] = left
        resp_ref[k, cells:] = right
        table = with_ends(table, voltage, 2 * (k + 1))
        if k < steps - 2:
            table = with_ends(table, left, left_row + 2 * (k + 1))
            table = with_ends(table, right, right_row + 2 * (k + 1))
    ends_ref[...] = table.T[:END_ROWS].astype(BF)
    copies[5].wait()


def prepare_kernel(
    tiles,
    paired,
    vloc_ref,
    g_ref,
    e_ref,
    drive_ref,
    turned_ref,
    owner_hbm,
    counts_hbm,
    pattern_hbm,
    transfer_hbm,
    vlast_ref,
    spread_ref,
    order_ref,
    select_ref,
    middle_ref,
    owner_ref,
    counts_ref,
    pattern_ref,
    sems,
):
    copies = start_all(
        [
            (owner_hbm, owner_ref),
            (counts_hbm, counts_ref),
            (pattern_hbm, pattern_ref),
            (transfer_hbm.at[pl.ds(PARTS[0], PARTS[1])], middle_ref),
        ],
        sems,
    )
    steps, cells, _ = drive_ref.shape
    keep, source = keep_and_source(g_ref[...], e_ref[...])
    rhs = vloc_ref[steps - 2] * keep + source + TIME_STEP * drive_ref[steps - 1].astype(F32)
    vlast_ref[...] = solve(rhs, hi_lo_weights(turned_ref[...]))

    for copy in copies[:2]:
        copy.wait()
    me = lax.axis_index("tile")
    row_count = spread_ref.shape[0]
    capacity = row_count // tiles
    owner = owner_ref[...]
    member = owner == iota((tiles, cells), 0)
    before = iota((cells, cells), 0) < iota((cells, cells), 1)
    rank = jnp.dot(one_hot(member), one_hot(before), preferred_element_type=F32)
    rank = jnp.sum(jnp.where(member, rank, 0.0), axis=0, keepdims=True).astype(jnp.int32)
    to = owner ^ me if paired else owner
    spread_ref[...] = one_hot(iota((row_count, cells), 0) == to * capacity + rank)

    counts = [counts_ref[0, u] for u in range(tiles)]
    row = iota((1, row_count), 1)
    slot_of = jnp.full((1, row_count), -1, jnp.int32)
    start = jnp.int32(0)
    for b in range(tiles):
        if paired:
            sender = b ^ me
            count = counts_ref[0, sender]
            start = sum(jnp.where(u < sender, counts[u], 0) for u in range(tiles))
        else:
            count = counts[b]
            start = start + (counts[b - 1] if b else 0)
        place = row - b * capacity
        slot_of = jnp.where((place >= 0) & (place < count), place + start, slot_of)
    order_ref[...] = one_hot(iota(order_ref.shape, 0) == slot_of)
    copies[2].wait()
    contact_tiles = select_ref.shape[0]
    kinds, slot_count = pattern_ref.shape
    for t in range(kinds):
        select_ref[:, t * slot_count : (t + 1) * slot_count] = one_hot(
            iota((contact_tiles, slot_count), 0) == pattern_ref[t : t + 1, :]
        )
    copies[3].wait()


def couple_kernel(sections, block_count, *refs):
    ends_refs, refs = refs[:sections], refs[sections:]
    vloc_ref, vlast_ref, resp_ref, g_ref, e_ref, drive_ref, turned_ref, spread_ref, *refs = refs
    final_ref, *refs = refs
    out_refs, refs = refs[:block_count], refs[block_count:]
    ends32, incoming, leak = refs
    steps, cells, width = drive_ref.shape
    mine = lax.axis_index("sec")
    for p in range(sections):
        ends32[mine ^ SEC_SEQUENCE[p]] = ends_refs[p][...].astype(F32)

    def rows(q):
        return ends32[:, q, :]

    def lagged(row):
        return [None] + [rows(row + 2 * l) for l in range(steps - 1)]

    left_b, left_a = lagged(2 * steps), lagged(2 * steps + 1)
    right_b, right_a = lagged(4 * steps), lagged(4 * steps + 1)
    zero = jnp.zeros((1, cells), F32)
    from_left, from_right = [], []
    for k in range(steps):
        last, first = rows(2 * k), rows(2 * k + 1)
        for j in range(k):
            first = first + (left_a[k - j] * from_left[j] + right_a[k - j] * from_right[j])
            last = last + (left_b[k - j] * from_left[j] + right_b[k - j] * from_right[j])
        from_left.append(jnp.concatenate([zero, last[:-1]], axis=0))
        from_right.append(jnp.concatenate([first[1:], zero], axis=0))
    own = iota((sections, cells), 0) == mine
    for j in range(steps):
        incoming[pl.ds(2 * j, 1), :] = jnp.sum(
            jnp.where(own, from_left[j], 0.0), axis=0, keepdims=True
        )
        incoming[pl.ds(2 * j + 1, 1), :] = jnp.sum(
            jnp.where(own, from_right[j], 0.0), axis=0, keepdims=True
        )
    by_cell = incoming[...].T

    block = 8
    lag_left = jnp.broadcast_to(TIME_STEP * AXIAL * turned_ref[0:1, :], (block, width))
    lag_right = jnp.broadcast_to(
        TIME_STEP * AXIAL * turned_ref[width - 1 : width, :], (block, width)
    )
    for c in range(0, cells, block):
        span = slice(c, c + block)
        unit = [
            jnp.broadcast_to(by_cell[span, q : q + 1], (block, width)) for q in range(2 * steps)
        ]
        lefts = [None, lag_left] + [resp_ref[l, span, :] for l in range(steps - 1)]
        rights = [None, lag_right] + [
            resp_ref[l, cells + c : cells + c + block, :] for l in range(steps - 1)
        ]
        cond, rev = g_ref[span, :], e_ref[span, :]
        for k in range(1, steps + 1):
            total = vloc_ref[k - 1, span, :] if k < steps else vlast_ref[span, :]
            for j in range(k):
                total = total + (unit[2 * j] * lefts[k - j] + unit[2 * j + 1] * rights[k - j])
            leak[k - 1, span, :] = cond * (total - rev)
        final_ref[span, :] = total

    capacity = out_refs[0].shape[0]
    for k in range(0, steps, 2):
        current = [(leak[i] - drive_ref[i].astype(F32)).astype(BF) for i in (k, k + 1)]
        placed = jnp.dot(
            spread_ref[...], jnp.concatenate(current, axis=1), preferred_element_type=F32
        ).astype(BF)
        for b in range(block_count):
            out_refs[b][:, k * width : (k + 2) * width] = placed[b * capacity : (b + 1) * capacity]


def fetch_kernel(final_ref, transfer_hbm, late_ref, final_hbm, sems):
    copies = start_all(
        [
            (transfer_hbm.at[pl.ds(PARTS[0] + PARTS[1], PARTS[2])], late_ref),
            (final_ref, final_hbm),
        ],
        sems,
    )
    for copy in copies:
        copy.wait()


def readout_kernel(steps, sequence, select_ref, order_ref, *refs):
    *block_refs, early_ref, middle_ref, late_ref, out_ref, slots, reach = refs
    held = [(ref, at) for ref in (early_ref, middle_ref, late_ref) for at in range(ref.shape[0])]
    block_refs = [block_refs[sequence.index(p)] for p in range(len(block_refs))]
    slot_count = order_ref.shape[0]
    kinds, width, contacts = early_ref.shape[1:]
    for k in range(0, steps, 2):
        span = slice(k * width, (k + 2) * width)
        rows = jnp.concatenate([ref[:, span] for ref in block_refs], axis=0)
        both = jnp.dot(order_ref[...], rows, preferred_element_type=F32)
        for i in range(2):
            slots[pl.ds(k + i, slot_count, stride=steps), :] = both[:, i * width : (i + 1) * width]
    for s, (ref, at) in enumerate(held):
        current = slots[s * steps : (s + 1) * steps, :].astype(BF)
        tile = jnp.concatenate([ref[at, t] for t in range(kinds)], axis=1)
        product = jnp.dot(current, tile, preferred_element_type=F32)
        for t in range(kinds):
            row = (t * slot_count + s) * steps
            reach[row : row + steps, :] = product[:, t * contacts : (t + 1) * contacts]
    for k in range(steps):
        hi, lo = split_hi_lo(reach[pl.ds(k, kinds * slot_count, stride=steps), :])
        both = jnp.dot(
            select_ref[...], jnp.concatenate([hi, lo], axis=1), preferred_element_type=F32
        )
        out_ref[:, k, :] = both[:, :contacts] + both[:, contacts:]


def in_hbm(x):
    return pltpu.with_memory_space_constraint(x, pltpu.HBM)


def exchange(blocks, axis):
    count = lax.axis_size(axis)
    arrived = [blocks[0]]
    for p in range(1, count):
        arrived.append(lax.ppermute(blocks[p], axis, [(i, i ^ p) for i in range(count)]))
    return arrived


def on_device(
    voltage, conductance, reversal, drive, inv_cable, owner_map, peer_counts, pattern, transfer
):
    cells, width = voltage.shape
    steps = drive.shape[0]
    tiles = lax.axis_size("tile")
    sections = lax.axis_size("sec")
    capacity = 2 * cells // tiles
    row_count = tiles * capacity
    weights = transfer[0]
    slot_count, kinds, _, contact_width = weights.shape
    contact_tiles = CONTACTS // contact_width
    paired = PAIRED and tiles == 8
    vmem = pl.BlockSpec(memory_space=pltpu.VMEM)
    hbm = pl.BlockSpec(memory_space=pltpu.HBM)

    vloc, resp, ends, cond, rev, driven, turned, early_tiles = pl.pallas_call(
        local_kernel,
        out_shape=(
            jax.ShapeDtypeStruct((steps - 1, cells, width), F32),
            jax.ShapeDtypeStruct((steps - 1, 2 * cells, width), F32),
            jax.ShapeDtypeStruct((END_ROWS, cells), BF),
            jax.ShapeDtypeStruct((cells, width), F32),
            jax.ShapeDtypeStruct((cells, width), F32),
            jax.ShapeDtypeStruct((steps, cells, width), BF),
            jax.ShapeDtypeStruct((width, width), F32),
            jax.ShapeDtypeStruct((PARTS[0],) + weights.shape[1:], BF),
        ),
        in_specs=[hbm] * 6,
        out_specs=(vmem,) * 8,
        scratch_shapes=[
            pltpu.VMEM((cells, width), F32),
            pltpu.VMEM((width, width), F32),
            pltpu.SemaphoreType.DMA((6,)),
        ],
        compiler_params=PARAMS,
        name="local_steps",
    )(
        in_hbm(voltage),
        in_hbm(conductance),
        in_hbm(reversal),
        in_hbm(drive),
        in_hbm(inv_cable),
        in_hbm(weights),
    )

    vlast, spread, order, select, middle_tiles = pl.pallas_call(
        functools.partial(prepare_kernel, tiles, paired),
        out_shape=(
            jax.ShapeDtypeStruct((cells, width), F32),
            jax.ShapeDtypeStruct((row_count, cells), BF),
            jax.ShapeDtypeStruct((slot_count, row_count), BF),
            jax.ShapeDtypeStruct((contact_tiles, kinds * slot_count), BF),
            jax.ShapeDtypeStruct((PARTS[1],) + weights.shape[1:], BF),
        ),
        in_specs=[vmem] * 5 + [hbm] * 4,
        out_specs=(vmem,) * 5,
        scratch_shapes=[
            pltpu.VMEM((1, cells), jnp.int32),
            pltpu.SMEM((1, tiles), jnp.int32),
            pltpu.VMEM((kinds, slot_count), jnp.int32),
            pltpu.SemaphoreType.DMA((4,)),
        ],
        compiler_params=PARAMS,
        name="prepare_rows",
    )(
        vloc,
        cond,
        rev,
        driven,
        turned,
        in_hbm(owner_map.reshape(1, cells)),
        in_hbm(peer_counts),
        in_hbm(pattern[0].T),
        in_hbm(weights),
    )

    all_ends = exchange([ends] * sections, "sec")
    block_count = tiles if paired else 1
    final_here, *outgoing = pl.pallas_call(
        functools.partial(couple_kernel, sections, block_count),
        out_shape=(
            jax.ShapeDtypeStruct((cells, width), F32),
        )
        + (jax.ShapeDtypeStruct((row_count // block_count, steps * width), BF),) * block_count,
        in_specs=[vmem] * (sections + 8),
        out_specs=(vmem,) * (1 + block_count),
        scratch_shapes=[
            pltpu.VMEM((sections, END_ROWS, cells), F32),
            pltpu.VMEM((2 * steps, cells), F32),
            pltpu.VMEM((steps, cells, width), F32),
        ],
        compiler_params=PARAMS,
        name="couple_sections",
    )(
        *[all_ends[p] for p in SEC_SEQUENCE],
        vloc,
        vlast,
        resp,
        cond,
        rev,
        driven,
        turned,
        spread,
    )

    if paired:
        arrived = exchange(outgoing, "tile")
    else:
        arrived = [lax.all_to_all(outgoing[0], "tile", split_axis=0, concat_axis=0, tiled=True)]

    late_tiles, final_voltage = pl.pallas_call(
        fetch_kernel,
        out_shape=(
            jax.ShapeDtypeStruct((PARTS[2],) + weights.shape[1:], BF),
            jax.ShapeDtypeStruct((cells, width), F32),
        ),
        in_specs=[vmem, hbm],
        out_specs=(vmem, hbm),
        scratch_shapes=[pltpu.SemaphoreType.DMA((2,))],
        compiler_params=PARAMS,
        name="fetch_tiles",
    )(final_here, in_hbm(weights))

    sequence = SEQUENCE if paired else (0,)
    arrived = [arrived[p] for p in sequence]
    partial_sum = pl.pallas_call(
        functools.partial(readout_kernel, steps, sequence),
        out_shape=jax.ShapeDtypeStruct((contact_tiles, steps, contact_width), F32),
        in_specs=[vmem] * (len(arrived) + 5),
        out_specs=vmem,
        scratch_shapes=[
            pltpu.VMEM((slot_count * steps, width), F32),
            pltpu.VMEM((kinds * slot_count * steps, contact_width), F32),
        ],
        compiler_params=PARAMS,
        name="readout",
    )(select, order, *arrived, early_tiles, middle_tiles, late_tiles)

    devices = tiles * sections
    share = CONTACTS // devices
    parts = contact_width // share
    if parts > 1:
        partial_sum = partial_sum.reshape(contact_tiles, steps, parts, share)
        partial_sum = partial_sum.transpose(0, 2, 1, 3).reshape(devices, steps, share)
    shares = lax.all_to_all(partial_sum, ("tile", "sec"), split_axis=0, concat_axis=0, tiled=True)
    return final_voltage, jnp.sum(shares, axis=0)


def solution(mesh):
    placed = (
        P("tile", "sec"),
        P("tile", "sec"),
        P("tile", "sec"),
        P(None, "tile", "sec"),
        P(),
        P("tile"),
        P("tile", None),
        P("sec", "tile", None),
        P("sec", "tile", None, None, None),
    )
    return jax.shard_map(
        on_device,
        mesh=mesh,
        in_specs=placed,
        out_specs=(P("tile", "sec"), P(None, ("tile", "sec"))),
        check_vma=False,
    )
```

```python
import functools

import jax
import jax.numpy as jnp
from jax import lax
from jax.experimental import pallas as pl
from jax.experimental.pallas import tpu as pltpu
from jax.sharding import PartitionSpec as P

CONTACTS = 4096
TIME_STEP = 0.25
AXIAL = 2.0
END_ROWS = 48
PAIRED = True
PARTS = (48, 16, 64)
SEC_SEQUENCE = (0, 1, 2, 3)
SEQUENCE = (0, 6, 1, 7, 2, 4, 3, 5)
BF = jnp.bfloat16
F32 = jnp.float32
PARAMS = pltpu.CompilerParams(vmem_limit_bytes=24 * 1024 * 1024)


def split_hi_lo(x):
    hi = x.astype(BF)
    return hi, (x - hi.astype(F32)).astype(BF)


def one_hot(condition):
    return jnp.where(condition, 1.0, 0.0).astype(BF)


def iota(shape, dim):
    return lax.broadcasted_iota(jnp.int32, shape, dim)


def hi_lo_weights(cable):
    cable_hi, cable_lo = split_hi_lo(cable)
    half = jnp.concatenate([cable_hi, cable_lo], axis=1)
    return jnp.concatenate([half, half], axis=0)


def solve(rhs, weights):
    width = rhs.shape[1]
    hi, lo = split_hi_lo(rhs)
    both = jnp.dot(jnp.concatenate([hi, lo], axis=1), weights, preferred_element_type=F32)
    return both[:, :width] + both[:, width:]


def keep_and_source(cond, rev):
    lane = iota(cond.shape, 1)
    at_end = (lane == 0) | (lane == cond.shape[1] - 1)
    keep = 1.0 - TIME_STEP * cond - jnp.where(at_end, TIME_STEP * AXIAL, 0.0).astype(F32)
    return keep, TIME_STEP * cond * rev


def start_all(pairs, sems):
    copies = [pltpu.make_async_copy(src, dst, sems.at[i]) for i, (src, dst) in enumerate(pairs)]
    for copy in copies:
        copy.start()
    return copies


def local_kernel(
    v_hbm,
    g_hbm,
    e_hbm,
    drive_hbm,
    cable_hbm,
    transfer_hbm,
    vloc_ref,
    resp_ref,
    ends_ref,
    g_ref,
    e_ref,
    drive_ref,
    turned_ref,
    early_ref,
    v_ref,
    cable_ref,
    sems,
):
    copies = start_all(
        [
            (cable_hbm, cable_ref),
            (v_hbm, v_ref),
            (g_hbm, g_ref),
            (e_hbm, e_ref),
            (drive_hbm, drive_ref),
            (transfer_hbm.at[pl.ds(0, PARTS[0])], early_ref),
        ],
        sems,
    )
    cells, width = v_ref.shape
    steps = drive_ref.shape[0]
    copies[0].wait()
    cable = cable_ref[...].T
    turned_ref[...] = cable
    weights = hi_lo_weights(cable)
    for copy in copies[1:5]:
        copy.wait()
    keep, source = keep_and_source(g_ref[...], e_ref[...])
    lane = iota((cells, width), 1)

    def with_ends(table, x, row):
        return jnp.where((lane >= row) & (lane < row + 2), pltpu.roll(x, row + 1, 1), table)

    voltage = v_ref[...]
    left = jnp.broadcast_to(TIME_STEP * AXIAL * cable[0:1, :], (cells, width))
    right = jnp.broadcast_to(TIME_STEP * AXIAL * cable[width - 1 : width, :], (cells, width))
    left_row, right_row = 2 * steps, 4 * steps
    table = with_ends(jnp.zeros((cells, width), F32), voltage, 0)
    table = with_ends(with_ends(table, left, left_row), right, right_row)
    for k in range(steps - 1):
        rhs = voltage * keep + source + TIME_STEP * drive_ref[k].astype(F32)
        voltage = solve(rhs, weights)
        left = solve(left * keep, weights)
        right = solve(right * keep, weights)
        vloc_ref[k] = voltage
        resp_ref[k, :cells] = left
        resp_ref[k, cells:] = right
        table = with_ends(table, voltage, 2 * (k + 1))
        if k < steps - 2:
            table = with_ends(table, left, left_row + 2 * (k + 1))
            table = with_ends(table, right, right_row + 2 * (k + 1))
    ends_ref[...] = table.T[:END_ROWS].astype(BF)
    copies[5].wait()


def prepare_kernel(
    tiles,
    paired,
    vloc_ref,
    g_ref,
    e_ref,
    drive_ref,
    turned_ref,
    owner_hbm,
    counts_hbm,
    pattern_hbm,
    transfer_hbm,
    vlast_ref,
    spread_ref,
    order_ref,
    select_ref,
    middle_ref,
    owner_ref,
    counts_ref,
    pattern_ref,
    sems,
):
    copies = start_all(
        [
            (owner_hbm, owner_ref),
            (counts_hbm, counts_ref),
            (pattern_hbm, pattern_ref),
            (transfer_hbm.at[pl.ds(PARTS[0], PARTS[1])], middle_ref),
        ],
        sems,
    )
    steps, cells, _ = drive_ref.shape
    keep, source = keep_and_source(g_ref[...], e_ref[...])
    rhs = vloc_ref[steps - 2] * keep + source + TIME_STEP * drive_ref[steps - 1].astype(F32)
    vlast_ref[...] = solve(rhs, hi_lo_weights(turned_ref[...]))

    for copy in copies[:2]:
        copy.wait()
    me = lax.axis_index("tile")
    row_count = spread_ref.shape[0]
    capacity = row_count // tiles
    owner = owner_ref[...]
    member = owner == iota((tiles, cells), 0)
    before = iota((cells, cells), 0) < iota((cells, cells), 1)
    rank = jnp.dot(one_hot(member), one_hot(before), preferred_element_type=F32)
    rank = jnp.sum(jnp.where(member, rank, 0.0), axis=0, keepdims=True).astype(jnp.int32)
    to = owner ^ me if paired else owner
    spread_ref[...] = one_hot(iota((row_count, cells), 0) == to * capacity + rank)

    counts = [counts_ref[0, u] for u in range(tiles)]
    row = iota((1, row_count), 1)
    slot_of = jnp.full((1, row_count), -1, jnp.int32)
    start = jnp.int32(0)
    for b in range(tiles):
        if paired:
            sender = b ^ me
            count = counts_ref[0, sender]
            start = sum(jnp.where(u < sender, counts[u], 0) for u in range(tiles))
        else:
            count = counts[b]
            start = start + (counts[b - 1] if b else 0)
        place = row - b * capacity
        slot_of = jnp.where((place >= 0) & (place < count), place + start, slot_of)
    order_ref[...] = one_hot(iota(order_ref.shape, 0) == slot_of)
    copies[2].wait()
    contact_tiles = select_ref.shape[0]
    kinds, slot_count = pattern_ref.shape
    for t in range(kinds):
        select_ref[:, t * slot_count : (t + 1) * slot_count] = one_hot(
            iota((contact_tiles, slot_count), 0) == pattern_ref[t : t + 1, :]
        )
    copies[3].wait()


def couple_kernel(sections, block_count, *refs):
    ends_refs, refs = refs[:sections], refs[sections:]
    vloc_ref, vlast_ref, resp_ref, g_ref, e_ref, drive_ref, turned_ref, spread_ref, *refs = refs
    final_ref, *refs = refs
    out_refs, refs = refs[:block_count], refs[block_count:]
    ends32, incoming, leak = refs
    steps, cells, width = drive_ref.shape
    mine = lax.axis_index("sec")
    for p in range(sections):
        ends32[mine ^ SEC_SEQUENCE[p]] = ends_refs[p][...].astype(F32)

    def rows(q):
        return ends32[:, q, :]

    def lagged(row):
        return [None] + [rows(row + 2 * l) for l in range(steps - 1)]

    left_b, left_a = lagged(2 * steps), lagged(2 * steps + 1)
    right_b, right_a = lagged(4 * steps), lagged(4 * steps + 1)
    zero = jnp.zeros((1, cells), F32)
    from_left, from_right = [], []
    for k in range(steps):
        last, first = rows(2 * k), rows(2 * k + 1)
        for j in range(k):
            first = first + (left_a[k - j] * from_left[j] + right_a[k - j] * from_right[j])
            last = last + (left_b[k - j] * from_left[j] + right_b[k - j] * from_right[j])
        from_left.append(jnp.concatenate([zero, last[:-1]], axis=0))
        from_right.append(jnp.concatenate([first[1:], zero], axis=0))
    own = iota((sections, cells), 0) == mine
    for j in range(steps):
        incoming[pl.ds(2 * j, 1), :] = jnp.sum(
            jnp.where(own, from_left[j], 0.0), axis=0, keepdims=True
        )
        incoming[pl.ds(2 * j + 1, 1), :] = jnp.sum(
            jnp.where(own, from_right[j], 0.0), axis=0, keepdims=True
        )
    by_cell = incoming[...].T

    block = 8
    lag_left = jnp.broadcast_to(TIME_STEP * AXIAL * turned_ref[0:1, :], (block, width))
    lag_right = jnp.broadcast_to(
        TIME_STEP * AXIAL * turned_ref[width - 1 : width, :], (block, width)
    )
    for c in range(0, cells, block):
        span = slice(c, c + block)
        unit = [
            jnp.broadcast_to(by_cell[span, q : q + 1], (block, width)) for q in range(2 * steps)
        ]
        lefts = [None, lag_left] + [resp_ref[l, span, :] for l in range(steps - 1)]
        rights = [None, lag_right] + [
            resp_ref[l, cells + c : cells + c + block, :] for l in range(steps - 1)
        ]
        cond, rev = g_ref[span, :], e_ref[span, :]
        for k in range(1, steps + 1):
            total = vloc_ref[k - 1, span, :] if k < steps else vlast_ref[span, :]
            for j in range(k):
                total = total + (unit[2 * j] * lefts[k - j] + unit[2 * j + 1] * rights[k - j])
            leak[k - 1, span, :] = cond * (total - rev)
        final_ref[span, :] = total

    capacity = out_refs[0].shape[0]
    for k in range(0, steps, 2):
        current = [(leak[i] - drive_ref[i].astype(F32)).astype(BF) for i in (k, k + 1)]
        placed = jnp.dot(
            spread_ref[...], jnp.concatenate(current, axis=1), preferred_element_type=F32
        ).astype(BF)
        for b in range(block_count):
            out_refs[b][:, k * width : (k + 2) * width] = placed[b * capacity : (b + 1) * capacity]


def fetch_kernel(final_ref, transfer_hbm, late_ref, final_hbm, sems):
    copies = start_all(
        [
            (transfer_hbm.at[pl.ds(PARTS[0] + PARTS[1], PARTS[2])], late_ref),
            (final_ref, final_hbm),
        ],
        sems,
    )
    for copy in copies:
        copy.wait()


def readout_kernel(steps, sequence, select_ref, order_ref, *refs):
    *block_refs, early_ref, middle_ref, late_ref, out_ref, slots, reach, sums = refs
    held = [(ref, at) for ref in (early_ref, middle_ref, late_ref) for at in range(ref.shape[0])]
    block_refs = [block_refs[sequence.index(p)] for p in range(len(block_refs))]
    slot_count = order_ref.shape[0]
    kinds, width, contacts = early_ref.shape[1:]
    for k in range(0, steps, 2):
        span = slice(k * width, (k + 2) * width)
        rows = jnp.concatenate([ref[:, span] for ref in block_refs], axis=0)
        both = jnp.dot(order_ref[...], rows, preferred_element_type=F32)
        for i in range(2):
            slots[pl.ds(k + i, slot_count, stride=steps), :] = both[:, i * width : (i + 1) * width]
    for s, (ref, at) in enumerate(held):
        current = slots[s * steps : (s + 1) * steps, :].astype(BF)
        tile = jnp.concatenate([ref[at, t] for t in range(kinds)], axis=1)
        product = jnp.dot(current, tile, preferred_element_type=F32)
        for t in range(kinds):
            row = (t * slot_count + s) * steps
            reach[row : row + steps, :] = product[:, t * contacts : (t + 1) * contacts]
    for k in range(steps):
        hi, lo = split_hi_lo(reach[pl.ds(k, kinds * slot_count, stride=steps), :])
        both = jnp.dot(
            select_ref[...], jnp.concatenate([hi, lo], axis=1), preferred_element_type=F32
        )
        sums[:, k, :] = both[:, :contacts] + both[:, contacts:]
    out_ref[...] = sums[...].astype(BF)


def in_hbm(x):
    return pltpu.with_memory_space_constraint(x, pltpu.HBM)


def exchange(blocks, axis):
    count = lax.axis_size(axis)
    arrived = [blocks[0]]
    for p in range(1, count):
        arrived.append(lax.ppermute(blocks[p], axis, [(i, i ^ p) for i in range(count)]))
    return arrived


def on_device(
    voltage, conductance, reversal, drive, inv_cable, owner_map, peer_counts, pattern, transfer
):
    cells, width = voltage.shape
    steps = drive.shape[0]
    tiles = lax.axis_size("tile")
    sections = lax.axis_size("sec")
    capacity = 2 * cells // tiles
    row_count = tiles * capacity
    weights = transfer[0]
    slot_count, kinds, _, contact_width = weights.shape
    contact_tiles = CONTACTS // contact_width
    paired = PAIRED and tiles == 8
    vmem = pl.BlockSpec(memory_space=pltpu.VMEM)
    hbm = pl.BlockSpec(memory_space=pltpu.HBM)

    vloc, resp, ends, cond, rev, driven, turned, early_tiles = pl.pallas_call(
        local_kernel,
        out_shape=(
            jax.ShapeDtypeStruct((steps - 1, cells, width), F32),
            jax.ShapeDtypeStruct((steps - 1, 2 * cells, width), F32),
            jax.ShapeDtypeStruct((END_ROWS, cells), BF),
            jax.ShapeDtypeStruct((cells, width), F32),
            jax.ShapeDtypeStruct((cells, width), F32),
            jax.ShapeDtypeStruct((steps, cells, width), BF),
            jax.ShapeDtypeStruct((width, width), F32),
            jax.ShapeDtypeStruct((PARTS[0],) + weights.shape[1:], BF),
        ),
        in_specs=[hbm] * 6,
        out_specs=(vmem,) * 8,
        scratch_shapes=[
            pltpu.VMEM((cells, width), F32),
            pltpu.VMEM((width, width), F32),
            pltpu.SemaphoreType.DMA((6,)),
        ],
        compiler_params=PARAMS,
        name="local_steps",
    )(
        in_hbm(voltage),
        in_hbm(conductance),
        in_hbm(reversal),
        in_hbm(drive),
        in_hbm(inv_cable),
        in_hbm(weights),
    )

    vlast, spread, order, select, middle_tiles = pl.pallas_call(
        functools.partial(prepare_kernel, tiles, paired),
        out_shape=(
            jax.ShapeDtypeStruct((cells, width), F32),
            jax.ShapeDtypeStruct((row_count, cells), BF),
            jax.ShapeDtypeStruct((slot_count, row_count), BF),
            jax.ShapeDtypeStruct((contact_tiles, kinds * slot_count), BF),
            jax.ShapeDtypeStruct((PARTS[1],) + weights.shape[1:], BF),
        ),
        in_specs=[vmem] * 5 + [hbm] * 4,
        out_specs=(vmem,) * 5,
        scratch_shapes=[
            pltpu.VMEM((1, cells), jnp.int32),
            pltpu.SMEM((1, tiles), jnp.int32),
            pltpu.VMEM((kinds, slot_count), jnp.int32),
            pltpu.SemaphoreType.DMA((4,)),
        ],
        compiler_params=PARAMS,
        name="prepare_rows",
    )(
        vloc,
        cond,
        rev,
        driven,
        turned,
        in_hbm(owner_map.reshape(1, cells)),
        in_hbm(peer_counts),
        in_hbm(pattern[0].T),
        in_hbm(weights),
    )

    all_ends = exchange([ends] * sections, "sec")
    block_count = tiles if paired else 1
    final_here, *outgoing = pl.pallas_call(
        functools.partial(couple_kernel, sections, block_count),
        out_shape=(
            jax.ShapeDtypeStruct((cells, width), F32),
        )
        + (jax.ShapeDtypeStruct((row_count // block_count, steps * width), BF),) * block_count,
        in_specs=[vmem] * (sections + 8),
        out_specs=(vmem,) * (1 + block_count),
        scratch_shapes=[
            pltpu.VMEM((sections, END_ROWS, cells), F32),
            pltpu.VMEM((2 * steps, cells), F32),
            pltpu.VMEM((steps, cells, width), F32),
        ],
        compiler_params=PARAMS,
        name="couple_sections",
    )(
        *[all_ends[p] for p in SEC_SEQUENCE],
        vloc,
        vlast,
        resp,
        cond,
        rev,
        driven,
        turned,
        spread,
    )

    if paired:
        arrived = exchange(outgoing, "tile")
    else:
        arrived = [lax.all_to_all(outgoing[0], "tile", split_axis=0, concat_axis=0, tiled=True)]

    late_tiles, final_voltage = pl.pallas_call(
        fetch_kernel,
        out_shape=(
            jax.ShapeDtypeStruct((PARTS[2],) + weights.shape[1:], BF),
            jax.ShapeDtypeStruct((cells, width), F32),
        ),
        in_specs=[vmem, hbm],
        out_specs=(vmem, hbm),
        scratch_shapes=[pltpu.SemaphoreType.DMA((2,))],
        compiler_params=PARAMS,
        name="fetch_tiles",
    )(final_here, in_hbm(weights))

    sequence = SEQUENCE if paired else (0,)
    arrived = [arrived[p] for p in sequence]
    partial_sum = pl.pallas_call(
        functools.partial(readout_kernel, steps, sequence),
        out_shape=jax.ShapeDtypeStruct((contact_tiles, steps, contact_width), BF),
        in_specs=[vmem] * (len(arrived) + 5),
        out_specs=vmem,
        scratch_shapes=[
            pltpu.VMEM((slot_count * steps, width), F32),
            pltpu.VMEM((kinds * slot_count * steps, contact_width), F32),
            pltpu.VMEM((contact_tiles, steps, contact_width), F32),
        ],
        compiler_params=PARAMS,
        name="readout",
    )(select, order, *arrived, early_tiles, middle_tiles, late_tiles)

    devices = tiles * sections
    share = CONTACTS // devices
    parts = contact_width // share
    if parts > 1:
        partial_sum = partial_sum.reshape(contact_tiles, steps, parts, share)
        partial_sum = partial_sum.transpose(0, 2, 1, 3).reshape(devices, steps, share)
    shares = lax.all_to_all(partial_sum, ("tile", "sec"), split_axis=0, concat_axis=0, tiled=True)
    return final_voltage, jnp.sum(shares.astype(F32), axis=0)


def solution(mesh):
    placed = (
        P("tile", "sec"),
        P("tile", "sec"),
        P("tile", "sec"),
        P(None, "tile", "sec"),
        P(),
        P("tile"),
        P("tile", None),
        P("sec", "tile", None),
        P("sec", "tile", None, None, None),
    )
    return jax.shard_map(
        on_device,
        mesh=mesh,
        in_specs=placed,
        out_specs=(P("tile", "sec"), P(None, ("tile", "sec"))),
        check_vma=False,
    )
```

```python
import functools

import jax
import jax.numpy as jnp
from jax import lax
from jax.experimental import pallas as pl
from jax.experimental.pallas import tpu as pltpu
from jax.sharding import PartitionSpec as P

CONTACTS = 4096
TIME_STEP = 0.25
AXIAL = 2.0
END_ROWS = 48
PAIRED = True
PARTS = (48, 16, 64)
SEC_SEQUENCE = (0, 1, 2, 3)
SEQUENCE = (0, 6, 1, 7, 5, 2, 4, 3)
BF = jnp.bfloat16
F32 = jnp.float32
PARAMS = pltpu.CompilerParams(vmem_limit_bytes=24 * 1024 * 1024)


def split_hi_lo(x):
    hi = x.astype(BF)
    return hi, (x - hi.astype(F32)).astype(BF)


def one_hot(condition):
    return jnp.where(condition, 1.0, 0.0).astype(BF)


def iota(shape, dim):
    return lax.broadcasted_iota(jnp.int32, shape, dim)


def hi_lo_weights(cable):
    cable_hi, cable_lo = split_hi_lo(cable)
    half = jnp.concatenate([cable_hi, cable_lo], axis=1)
    return jnp.concatenate([half, half], axis=0)


def solve(rhs, weights):
    width = rhs.shape[1]
    hi, lo = split_hi_lo(rhs)
    both = jnp.dot(jnp.concatenate([hi, lo], axis=1), weights, preferred_element_type=F32)
    return both[:, :width] + both[:, width:]


def keep_and_source(cond, rev):
    lane = iota(cond.shape, 1)
    at_end = (lane == 0) | (lane == cond.shape[1] - 1)
    keep = 1.0 - TIME_STEP * cond - jnp.where(at_end, TIME_STEP * AXIAL, 0.0).astype(F32)
    return keep, TIME_STEP * cond * rev


def start_all(pairs, sems):
    copies = [pltpu.make_async_copy(src, dst, sems.at[i]) for i, (src, dst) in enumerate(pairs)]
    for copy in copies:
        copy.start()
    return copies


def local_kernel(
    v_hbm,
    g_hbm,
    e_hbm,
    drive_hbm,
    cable_hbm,
    transfer_hbm,
    vloc_ref,
    resp_ref,
    ends_ref,
    g_ref,
    e_ref,
    drive_ref,
    turned_ref,
    early_ref,
    v_ref,
    cable_ref,
    sems,
):
    copies = start_all(
        [
            (cable_hbm, cable_ref),
            (v_hbm, v_ref),
            (g_hbm, g_ref),
            (e_hbm, e_ref),
            (drive_hbm, drive_ref),
            (transfer_hbm.at[pl.ds(0, PARTS[0])], early_ref),
        ],
        sems,
    )
    cells, width = v_ref.shape
    steps = drive_ref.shape[0]
    copies[0].wait()
    cable = cable_ref[...].T
    turned_ref[...] = cable
    weights = hi_lo_weights(cable)
    for copy in copies[1:5]:
        copy.wait()
    keep, source = keep_and_source(g_ref[...], e_ref[...])
    lane = iota((cells, width), 1)

    def with_ends(table, x, row):
        return jnp.where((lane >= row) & (lane < row + 2), pltpu.roll(x, row + 1, 1), table)

    voltage = v_ref[...]
    left = jnp.broadcast_to(TIME_STEP * AXIAL * cable[0:1, :], (cells, width))
    right = jnp.broadcast_to(TIME_STEP * AXIAL * cable[width - 1 : width, :], (cells, width))
    left_row, right_row = 2 * steps, 4 * steps
    table = with_ends(jnp.zeros((cells, width), F32), voltage, 0)
    table = with_ends(with_ends(table, left, left_row), right, right_row)
    for k in range(steps - 1):
        rhs = voltage * keep + source + TIME_STEP * drive_ref[k].astype(F32)
        voltage = solve(rhs, weights)
        left = solve(left * keep, weights)
        right = solve(right * keep, weights)
        vloc_ref[k] = voltage
        resp_ref[k, :cells] = left.astype(BF)
        resp_ref[k, cells:] = right.astype(BF)
        table = with_ends(table, voltage, 2 * (k + 1))
        if k < steps - 2:
            table = with_ends(table, left, left_row + 2 * (k + 1))
            table = with_ends(table, right, right_row + 2 * (k + 1))
    ends_ref[...] = table.T[:END_ROWS].astype(BF)
    copies[5].wait()


def prepare_kernel(
    tiles,
    paired,
    vloc_ref,
    g_ref,
    e_ref,
    drive_ref,
    turned_ref,
    owner_hbm,
    counts_hbm,
    pattern_hbm,
    transfer_hbm,
    vlast_ref,
    spread_ref,
    order_ref,
    select_ref,
    middle_ref,
    owner_ref,
    counts_ref,
    pattern_ref,
    sems,
):
    copies = start_all(
        [
            (owner_hbm, owner_ref),
            (counts_hbm, counts_ref),
            (pattern_hbm, pattern_ref),
            (transfer_hbm.at[pl.ds(PARTS[0], PARTS[1])], middle_ref),
        ],
        sems,
    )
    steps, cells, _ = drive_ref.shape
    keep, source = keep_and_source(g_ref[...], e_ref[...])
    rhs = vloc_ref[steps - 2] * keep + source + TIME_STEP * drive_ref[steps - 1].astype(F32)
    vlast_ref[...] = solve(rhs, hi_lo_weights(turned_ref[...]))

    for copy in copies[:2]:
        copy.wait()
    me = lax.axis_index("tile")
    row_count = spread_ref.shape[0]
    capacity = row_count // tiles
    owner = owner_ref[...]
    member = owner == iota((tiles, cells), 0)
    before = iota((cells, cells), 0) < iota((cells, cells), 1)
    rank = jnp.dot(one_hot(member), one_hot(before), preferred_element_type=F32)
    rank = jnp.sum(jnp.where(member, rank, 0.0), axis=0, keepdims=True).astype(jnp.int32)
    to = owner ^ me if paired else owner
    spread_ref[...] = one_hot(iota((row_count, cells), 0) == to * capacity + rank)

    counts = [counts_ref[0, u] for u in range(tiles)]
    row = iota((1, row_count), 1)
    slot_of = jnp.full((1, row_count), -1, jnp.int32)
    start = jnp.int32(0)
    for b in range(tiles):
        if paired:
            sender = b ^ me
            count = counts_ref[0, sender]
            start = sum(jnp.where(u < sender, counts[u], 0) for u in range(tiles))
        else:
            count = counts[b]
            start = start + (counts[b - 1] if b else 0)
        place = row - b * capacity
        slot_of = jnp.where((place >= 0) & (place < count), place + start, slot_of)
    order_ref[...] = one_hot(iota(order_ref.shape, 0) == slot_of)
    copies[2].wait()
    contact_tiles = select_ref.shape[0]
    kinds, slot_count = pattern_ref.shape
    for t in range(kinds):
        select_ref[:, t * slot_count : (t + 1) * slot_count] = one_hot(
            iota((contact_tiles, slot_count), 0) == pattern_ref[t : t + 1, :]
        )
    copies[3].wait()


def couple_kernel(sections, block_count, *refs):
    ends_refs, refs = refs[:sections], refs[sections:]
    vloc_ref, vlast_ref, resp_ref, g_ref, e_ref, drive_ref, turned_ref, spread_ref, *refs = refs
    final_ref, *refs = refs
    out_refs, refs = refs[:block_count], refs[block_count:]
    ends32, incoming, leak = refs
    steps, cells, width = drive_ref.shape
    mine = lax.axis_index("sec")
    for p in range(sections):
        ends32[mine ^ SEC_SEQUENCE[p]] = ends_refs[p][...].astype(F32)

    def rows(q):
        return ends32[:, q, :]

    def lagged(row):
        return [None] + [rows(row + 2 * l) for l in range(steps - 1)]

    left_b, left_a = lagged(2 * steps), lagged(2 * steps + 1)
    right_b, right_a = lagged(4 * steps), lagged(4 * steps + 1)
    zero = jnp.zeros((1, cells), F32)
    from_left, from_right = [], []
    for k in range(steps):
        last, first = rows(2 * k), rows(2 * k + 1)
        for j in range(k):
            first = first + (left_a[k - j] * from_left[j] + right_a[k - j] * from_right[j])
            last = last + (left_b[k - j] * from_left[j] + right_b[k - j] * from_right[j])
        from_left.append(jnp.concatenate([zero, last[:-1]], axis=0))
        from_right.append(jnp.concatenate([first[1:], zero], axis=0))
    own = iota((sections, cells), 0) == mine
    for j in range(steps):
        incoming[pl.ds(2 * j, 1), :] = jnp.sum(
            jnp.where(own, from_left[j], 0.0), axis=0, keepdims=True
        )
        incoming[pl.ds(2 * j + 1, 1), :] = jnp.sum(
            jnp.where(own, from_right[j], 0.0), axis=0, keepdims=True
        )
    by_cell = incoming[...].T

    block = 16
    lag_left = jnp.broadcast_to(TIME_STEP * AXIAL * turned_ref[0:1, :], (block, width)).astype(BF)
    lag_right = TIME_STEP * AXIAL * turned_ref[width - 1 : width, :]
    lag_right = jnp.broadcast_to(lag_right, (block, width)).astype(BF)
    for c in range(0, cells, block):
        span = slice(c, c + block)
        unit = [
            jnp.broadcast_to(by_cell[span, q : q + 1], (block, width)).astype(BF)
            for q in range(2 * steps)
        ]
        lefts = [None, lag_left] + [resp_ref[l, span, :] for l in range(steps - 1)]
        rights = [None, lag_right] + [
            resp_ref[l, cells + c : cells + c + block, :] for l in range(steps - 1)
        ]
        cond, rev = g_ref[span, :], e_ref[span, :]
        for k in range(1, steps + 1):
            total = vloc_ref[k - 1, span, :] if k < steps else vlast_ref[span, :]
            inflow = [
                unit[2 * j] * lefts[k - j] + unit[2 * j + 1] * rights[k - j] for j in range(k)
            ]
            total = total + sum(inflow[1:], inflow[0]).astype(F32)
            leak[k - 1, span, :] = cond * (total - rev)
        final_ref[span, :] = total

    capacity = out_refs[0].shape[0]
    for k in range(0, steps, 2):
        current = [(leak[i] - drive_ref[i].astype(F32)).astype(BF) for i in (k, k + 1)]
        placed = jnp.dot(
            spread_ref[...], jnp.concatenate(current, axis=1), preferred_element_type=F32
        ).astype(BF)
        for b in range(block_count):
            out_refs[b][:, k * width : (k + 2) * width] = placed[b * capacity : (b + 1) * capacity]


def fetch_kernel(final_ref, transfer_hbm, late_ref, final_hbm, sems):
    copies = start_all(
        [
            (transfer_hbm.at[pl.ds(PARTS[0] + PARTS[1], PARTS[2])], late_ref),
            (final_ref, final_hbm),
        ],
        sems,
    )
    for copy in copies:
        copy.wait()


def readout_kernel(steps, sequence, select_ref, order_ref, *refs):
    *block_refs, early_ref, middle_ref, late_ref, out_ref, slots, reach, sums = refs
    held = [(ref, at) for ref in (early_ref, middle_ref, late_ref) for at in range(ref.shape[0])]
    block_refs = [block_refs[sequence.index(p)] for p in range(len(block_refs))]
    slot_count = order_ref.shape[0]
    kinds, width, contacts = early_ref.shape[1:]
    for k in range(0, steps, 2):
        span = slice(k * width, (k + 2) * width)
        rows = jnp.concatenate([ref[:, span] for ref in block_refs], axis=0)
        both = jnp.dot(order_ref[...], rows, preferred_element_type=F32)
        for i in range(2):
            slots[pl.ds(k + i, slot_count, stride=steps), :] = both[:, i * width : (i + 1) * width]
    for s, (ref, at) in enumerate(held):
        current = slots[s * steps : (s + 1) * steps, :].astype(BF)
        tile = jnp.concatenate([ref[at, t] for t in range(kinds)], axis=1)
        product = jnp.dot(current, tile, preferred_element_type=F32)
        for t in range(kinds):
            row = (t * slot_count + s) * steps
            reach[row : row + steps, :] = product[:, t * contacts : (t + 1) * contacts]
    for k in range(steps):
        hi, lo = split_hi_lo(reach[pl.ds(k, kinds * slot_count, stride=steps), :])
        both = jnp.dot(
            select_ref[...], jnp.concatenate([hi, lo], axis=1), preferred_element_type=F32
        )
        sums[:, k, :] = both[:, :contacts] + both[:, contacts:]
    out_ref[...] = sums[...].astype(BF)


def in_hbm(x):
    return pltpu.with_memory_space_constraint(x, pltpu.HBM)


def exchange(blocks, axis):
    count = lax.axis_size(axis)
    arrived = [blocks[0]]
    for p in range(1, count):
        arrived.append(lax.ppermute(blocks[p], axis, [(i, i ^ p) for i in range(count)]))
    return arrived


def on_device(
    voltage, conductance, reversal, drive, inv_cable, owner_map, peer_counts, pattern, transfer
):
    cells, width = voltage.shape
    steps = drive.shape[0]
    tiles = lax.axis_size("tile")
    sections = lax.axis_size("sec")
    capacity = 2 * cells // tiles
    row_count = tiles * capacity
    weights = transfer[0]
    slot_count, kinds, _, contact_width = weights.shape
    contact_tiles = CONTACTS // contact_width
    paired = PAIRED and tiles == 8
    vmem = pl.BlockSpec(memory_space=pltpu.VMEM)
    hbm = pl.BlockSpec(memory_space=pltpu.HBM)

    vloc, resp, ends, cond, rev, driven, turned, early_tiles = pl.pallas_call(
        local_kernel,
        out_shape=(
            jax.ShapeDtypeStruct((steps - 1, cells, width), F32),
            jax.ShapeDtypeStruct((steps - 1, 2 * cells, width), BF),
            jax.ShapeDtypeStruct((END_ROWS, cells), BF),
            jax.ShapeDtypeStruct((cells, width), F32),
            jax.ShapeDtypeStruct((cells, width), F32),
            jax.ShapeDtypeStruct((steps, cells, width), BF),
            jax.ShapeDtypeStruct((width, width), F32),
            jax.ShapeDtypeStruct((PARTS[0],) + weights.shape[1:], BF),
        ),
        in_specs=[hbm] * 6,
        out_specs=(vmem,) * 8,
        scratch_shapes=[
            pltpu.VMEM((cells, width), F32),
            pltpu.VMEM((width, width), F32),
            pltpu.SemaphoreType.DMA((6,)),
        ],
        compiler_params=PARAMS,
        name="local_steps",
    )(
        in_hbm(voltage),
        in_hbm(conductance),
        in_hbm(reversal),
        in_hbm(drive),
        in_hbm(inv_cable),
        in_hbm(weights),
    )

    vlast, spread, order, select, middle_tiles = pl.pallas_call(
        functools.partial(prepare_kernel, tiles, paired),
        out_shape=(
            jax.ShapeDtypeStruct((cells, width), F32),
            jax.ShapeDtypeStruct((row_count, cells), BF),
            jax.ShapeDtypeStruct((slot_count, row_count), BF),
            jax.ShapeDtypeStruct((contact_tiles, kinds * slot_count), BF),
            jax.ShapeDtypeStruct((PARTS[1],) + weights.shape[1:], BF),
        ),
        in_specs=[vmem] * 5 + [hbm] * 4,
        out_specs=(vmem,) * 5,
        scratch_shapes=[
            pltpu.VMEM((1, cells), jnp.int32),
            pltpu.SMEM((1, tiles), jnp.int32),
            pltpu.VMEM((kinds, slot_count), jnp.int32),
            pltpu.SemaphoreType.DMA((4,)),
        ],
        compiler_params=PARAMS,
        name="prepare_rows",
    )(
        vloc,
        cond,
        rev,
        driven,
        turned,
        in_hbm(owner_map.reshape(1, cells)),
        in_hbm(peer_counts),
        in_hbm(pattern[0].T),
        in_hbm(weights),
    )

    all_ends = exchange([ends] * sections, "sec")
    block_count = tiles if paired else 1
    final_here, *outgoing = pl.pallas_call(
        functools.partial(couple_kernel, sections, block_count),
        out_shape=(
            jax.ShapeDtypeStruct((cells, width), F32),
        )
        + (jax.ShapeDtypeStruct((row_count // block_count, steps * width), BF),) * block_count,
        in_specs=[vmem] * (sections + 8),
        out_specs=(vmem,) * (1 + block_count),
        scratch_shapes=[
            pltpu.VMEM((sections, END_ROWS, cells), F32),
            pltpu.VMEM((2 * steps, cells), F32),
            pltpu.VMEM((steps, cells, width), F32),
        ],
        compiler_params=PARAMS,
        name="couple_sections",
    )(
        *[all_ends[p] for p in SEC_SEQUENCE],
        vloc,
        vlast,
        resp,
        cond,
        rev,
        driven,
        turned,
        spread,
    )

    if paired:
        arrived = exchange(outgoing, "tile")
    else:
        arrived = [lax.all_to_all(outgoing[0], "tile", split_axis=0, concat_axis=0, tiled=True)]

    late_tiles, final_voltage = pl.pallas_call(
        fetch_kernel,
        out_shape=(
            jax.ShapeDtypeStruct((PARTS[2],) + weights.shape[1:], BF),
            jax.ShapeDtypeStruct((cells, width), F32),
        ),
        in_specs=[vmem, hbm],
        out_specs=(vmem, hbm),
        scratch_shapes=[pltpu.SemaphoreType.DMA((2,))],
        compiler_params=PARAMS,
        name="fetch_tiles",
    )(final_here, in_hbm(weights))

    sequence = SEQUENCE if paired else (0,)
    arrived = [arrived[p] for p in sequence]
    partial_sum = pl.pallas_call(
        functools.partial(readout_kernel, steps, sequence),
        out_shape=jax.ShapeDtypeStruct((contact_tiles, steps, contact_width), BF),
        in_specs=[vmem] * (len(arrived) + 5),
        out_specs=vmem,
        scratch_shapes=[
            pltpu.VMEM((slot_count * steps, width), F32),
            pltpu.VMEM((kinds * slot_count * steps, contact_width), F32),
            pltpu.VMEM((contact_tiles, steps, contact_width), F32),
        ],
        compiler_params=PARAMS,
        name="readout",
    )(select, order, *arrived, early_tiles, middle_tiles, late_tiles)

    devices = tiles * sections
    share = CONTACTS // devices
    parts = contact_width // share
    if parts > 1:
        partial_sum = partial_sum.reshape(contact_tiles, steps, parts, share)
        partial_sum = partial_sum.transpose(0, 2, 1, 3).reshape(devices, steps, share)
    shares = lax.all_to_all(partial_sum, ("tile", "sec"), split_axis=0, concat_axis=0, tiled=True)
    return final_voltage, jnp.sum(shares.astype(F32), axis=0)


def solution(mesh):
    placed = (
        P("tile", "sec"),
        P("tile", "sec"),
        P("tile", "sec"),
        P(None, "tile", "sec"),
        P(),
        P("tile"),
        P("tile", None),
        P("sec", "tile", None),
        P("sec", "tile", None, None, None),
    )
    return jax.shard_map(
        on_device,
        mesh=mesh,
        in_specs=placed,
        out_specs=(P("tile", "sec"), P(None, ("tile", "sec"))),
        check_vma=False,
    )
```

```python
import functools

import jax
import jax.numpy as jnp
from jax import lax
from jax.experimental import pallas as pl
from jax.experimental.pallas import tpu as pltpu
from jax.sharding import PartitionSpec as P

CONTACTS = 4096
TIME_STEP = 0.25
AXIAL = 2.0
END_ROWS = 48
PAIRED = True
PARTS = (48, 16, 64)
SEC_SEQUENCE = (0, 1, 2, 3)
SEQUENCE = (0, 6, 1, 7, 5, 2, 4, 3)
BF = jnp.bfloat16
F32 = jnp.float32
PARAMS = pltpu.CompilerParams(vmem_limit_bytes=24 * 1024 * 1024)


def split_hi_lo(x):
    hi = x.astype(BF)
    return hi, (x - hi.astype(F32)).astype(BF)


def one_hot(condition):
    return jnp.where(condition, 1.0, 0.0).astype(BF)


def iota(shape, dim):
    return lax.broadcasted_iota(jnp.int32, shape, dim)


def hi_lo_weights(cable):
    cable_hi, cable_lo = split_hi_lo(cable)
    half = jnp.concatenate([cable_hi, cable_lo], axis=1)
    return jnp.concatenate([half, half], axis=0)


def solve(rhs, weights):
    width = rhs.shape[1]
    hi, lo = split_hi_lo(rhs)
    both = jnp.dot(jnp.concatenate([hi, lo], axis=1), weights, preferred_element_type=F32)
    return both[:, :width] + both[:, width:]


def keep_and_source(cond, rev):
    lane = iota(cond.shape, 1)
    at_end = (lane == 0) | (lane == cond.shape[1] - 1)
    keep = 1.0 - TIME_STEP * cond - jnp.where(at_end, TIME_STEP * AXIAL, 0.0).astype(F32)
    return keep, TIME_STEP * cond * rev


def start_all(pairs, sems):
    copies = [pltpu.make_async_copy(src, dst, sems.at[i]) for i, (src, dst) in enumerate(pairs)]
    for copy in copies:
        copy.start()
    return copies


def local_kernel(
    v_hbm,
    g_hbm,
    e_hbm,
    drive_hbm,
    cable_hbm,
    transfer_hbm,
    vloc_ref,
    resp_ref,
    ends_ref,
    g_ref,
    e_ref,
    drive_ref,
    turned_ref,
    early_ref,
    v_ref,
    cable_ref,
    sems,
):
    copies = start_all(
        [
            (cable_hbm, cable_ref),
            (v_hbm, v_ref),
            (g_hbm, g_ref),
            (e_hbm, e_ref),
            (drive_hbm, drive_ref),
            (transfer_hbm.at[pl.ds(0, PARTS[0])], early_ref),
        ],
        sems,
    )
    cells, width = v_ref.shape
    steps = drive_ref.shape[0]
    copies[0].wait()
    cable = cable_ref[...].T
    turned_ref[...] = cable
    weights = hi_lo_weights(cable)
    for copy in copies[1:5]:
        copy.wait()
    keep, source = keep_and_source(g_ref[...], e_ref[...])
    lane = iota((cells, width), 1)

    def with_ends(table, x, row):
        return jnp.where((lane >= row) & (lane < row + 2), pltpu.roll(x, row + 1, 1), table)

    voltage = v_ref[...]
    left = jnp.broadcast_to(TIME_STEP * AXIAL * cable[0:1, :], (cells, width))
    right = jnp.broadcast_to(TIME_STEP * AXIAL * cable[width - 1 : width, :], (cells, width))
    left_row, right_row = 2 * steps, 4 * steps
    table = with_ends(jnp.zeros((cells, width), F32), voltage, 0)
    table = with_ends(with_ends(table, left, left_row), right, right_row)
    for k in range(steps - 1):
        rhs = voltage * keep + source + TIME_STEP * drive_ref[k].astype(F32)
        voltage = solve(rhs, weights)
        left = solve(left * keep, weights)
        right = solve(right * keep, weights)
        vloc_ref[k] = voltage
        resp_ref[k, :cells] = left.astype(BF)
        resp_ref[k, cells:] = right.astype(BF)
        table = with_ends(table, voltage, 2 * (k + 1))
        if k < steps - 2:
            table = with_ends(table, left, left_row + 2 * (k + 1))
            table = with_ends(table, right, right_row + 2 * (k + 1))
    ends_ref[...] = table.T[:END_ROWS].astype(BF)
    copies[5].wait()


def prepare_kernel(
    tiles,
    paired,
    vloc_ref,
    g_ref,
    e_ref,
    drive_ref,
    turned_ref,
    owner_hbm,
    counts_hbm,
    pattern_hbm,
    transfer_hbm,
    vlast_ref,
    spread_ref,
    order_ref,
    select_ref,
    middle_ref,
    owner_ref,
    counts_ref,
    pattern_ref,
    sems,
):
    copies = start_all(
        [
            (owner_hbm, owner_ref),
            (counts_hbm, counts_ref),
            (pattern_hbm, pattern_ref),
            (transfer_hbm.at[pl.ds(PARTS[0], PARTS[1])], middle_ref),
        ],
        sems,
    )
    steps, cells, _ = drive_ref.shape
    keep, source = keep_and_source(g_ref[...], e_ref[...])
    rhs = vloc_ref[steps - 2] * keep + source + TIME_STEP * drive_ref[steps - 1].astype(F32)
    vlast_ref[...] = solve(rhs, hi_lo_weights(turned_ref[...]))

    for copy in copies[:2]:
        copy.wait()
    me = lax.axis_index("tile")
    row_count = spread_ref.shape[0]
    capacity = row_count // tiles
    owner = owner_ref[...]
    member = owner == iota((tiles, cells), 0)
    before = iota((cells, cells), 0) < iota((cells, cells), 1)
    rank = jnp.dot(one_hot(member), one_hot(before), preferred_element_type=F32)
    rank = jnp.sum(jnp.where(member, rank, 0.0), axis=0, keepdims=True).astype(jnp.int32)
    to = owner ^ me if paired else owner
    spread_ref[...] = one_hot(iota((row_count, cells), 0) == to * capacity + rank)

    counts = [counts_ref[0, u] for u in range(tiles)]
    row = iota((1, row_count), 1)
    slot_of = jnp.full((1, row_count), -1, jnp.int32)
    start = jnp.int32(0)
    for b in range(tiles):
        if paired:
            sender = b ^ me
            count = counts_ref[0, sender]
            start = sum(jnp.where(u < sender, counts[u], 0) for u in range(tiles))
        else:
            count = counts[b]
            start = start + (counts[b - 1] if b else 0)
        place = row - b * capacity
        slot_of = jnp.where((place >= 0) & (place < count), place + start, slot_of)
    order_ref[...] = one_hot(iota(order_ref.shape, 0) == slot_of)
    copies[2].wait()
    contact_tiles = select_ref.shape[0]
    kinds, slot_count = pattern_ref.shape
    for t in range(kinds):
        select_ref[:, t * slot_count : (t + 1) * slot_count] = one_hot(
            iota((contact_tiles, slot_count), 0) == pattern_ref[t : t + 1, :]
        )
    copies[3].wait()


def couple_kernel(sections, block_count, *refs):
    ends_refs, refs = refs[:sections], refs[sections:]
    vloc_ref, vlast_ref, resp_ref, g_ref, e_ref, drive_ref, turned_ref, spread_ref, *refs = refs
    final_ref, *refs = refs
    out_refs, refs = refs[:block_count], refs[block_count:]
    ends32, incoming, leak = refs
    steps, cells, width = drive_ref.shape
    mine = lax.axis_index("sec")
    for p in range(sections):
        ends32[mine ^ SEC_SEQUENCE[p]] = ends_refs[p][...].astype(F32)

    def rows(q):
        return ends32[:, q, :]

    def lagged(row):
        return [None] + [rows(row + 2 * l) for l in range(steps - 1)]

    left_b, left_a = lagged(2 * steps), lagged(2 * steps + 1)
    right_b, right_a = lagged(4 * steps), lagged(4 * steps + 1)
    zero = jnp.zeros((1, cells), F32)
    from_left, from_right = [], []
    for k in range(steps):
        last, first = rows(2 * k), rows(2 * k + 1)
        for j in range(k):
            first = first + (left_a[k - j] * from_left[j] + right_a[k - j] * from_right[j])
            last = last + (left_b[k - j] * from_left[j] + right_b[k - j] * from_right[j])
        from_left.append(jnp.concatenate([zero, last[:-1]], axis=0))
        from_right.append(jnp.concatenate([first[1:], zero], axis=0))
    own = iota((sections, cells), 0) == mine
    for j in range(steps):
        incoming[pl.ds(2 * j, 1), :] = jnp.sum(
            jnp.where(own, from_left[j], 0.0), axis=0, keepdims=True
        )
        incoming[pl.ds(2 * j + 1, 1), :] = jnp.sum(
            jnp.where(own, from_right[j], 0.0), axis=0, keepdims=True
        )
    by_cell = incoming[...].T.astype(BF)

    block = 16
    lag_left = jnp.broadcast_to(TIME_STEP * AXIAL * turned_ref[0:1, :], (block, width)).astype(BF)
    lag_right = TIME_STEP * AXIAL * turned_ref[width - 1 : width, :]
    lag_right = jnp.broadcast_to(lag_right, (block, width)).astype(BF)
    for c in range(0, cells, block):
        span = slice(c, c + block)
        unit = [
            jnp.broadcast_to(by_cell[span, q : q + 1], (block, width))
            for q in range(2 * steps)
        ]
        lefts = [None, lag_left] + [resp_ref[l, span, :] for l in range(steps - 1)]
        rights = [None, lag_right] + [
            resp_ref[l, cells + c : cells + c + block, :] for l in range(steps - 1)
        ]
        cond, rev = g_ref[span, :], e_ref[span, :]
        for k in range(1, steps + 1):
            total = vloc_ref[k - 1, span, :] if k < steps else vlast_ref[span, :]
            inflow = [
                unit[2 * j] * lefts[k - j] + unit[2 * j + 1] * rights[k - j] for j in range(k)
            ]
            total = total + sum(inflow[1:], inflow[0]).astype(F32)
            leak[k - 1, span, :] = cond * (total - rev)
        final_ref[span, :] = total

    capacity = out_refs[0].shape[0]
    for k in range(0, steps, 2):
        current = [(leak[i] - drive_ref[i].astype(F32)).astype(BF) for i in (k, k + 1)]
        placed = jnp.dot(
            spread_ref[...], jnp.concatenate(current, axis=1), preferred_element_type=F32
        ).astype(BF)
        for b in range(block_count):
            out_refs[b][:, k * width : (k + 2) * width] = placed[b * capacity : (b + 1) * capacity]


def fetch_kernel(final_ref, transfer_hbm, late_ref, final_hbm, sems):
    copies = start_all(
        [
            (transfer_hbm.at[pl.ds(PARTS[0] + PARTS[1], PARTS[2])], late_ref),
            (final_ref, final_hbm),
        ],
        sems,
    )
    for copy in copies:
        copy.wait()


def readout_kernel(steps, sequence, select_ref, order_ref, *refs):
    *block_refs, early_ref, middle_ref, late_ref, out_ref, slots, reach, sums = refs
    held = [(ref, at) for ref in (early_ref, middle_ref, late_ref) for at in range(ref.shape[0])]
    block_refs = [block_refs[sequence.index(p)] for p in range(len(block_refs))]
    slot_count = order_ref.shape[0]
    kinds, width, contacts = early_ref.shape[1:]
    for k in range(0, steps, 2):
        span = slice(k * width, (k + 2) * width)
        rows = jnp.concatenate([ref[:, span] for ref in block_refs], axis=0)
        both = jnp.dot(order_ref[...], rows, preferred_element_type=F32)
        for i in range(2):
            slots[pl.ds(k + i, slot_count, stride=steps), :] = both[:, i * width : (i + 1) * width]
    for s, (ref, at) in enumerate(held):
        current = slots[s * steps : (s + 1) * steps, :].astype(BF)
        tile = jnp.concatenate([ref[at, t] for t in range(kinds)], axis=1)
        product = jnp.dot(current, tile, preferred_element_type=F32)
        for t in range(kinds):
            row = (t * slot_count + s) * steps
            reach[row : row + steps, :] = product[:, t * contacts : (t + 1) * contacts]
    for k in range(steps):
        hi, lo = split_hi_lo(reach[pl.ds(k, kinds * slot_count, stride=steps), :])
        both = jnp.dot(
            select_ref[...], jnp.concatenate([hi, lo], axis=1), preferred_element_type=F32
        )
        sums[:, k, :] = both[:, :contacts] + both[:, contacts:]
    out_ref[...] = sums[...].astype(BF)


def in_hbm(x):
    return pltpu.with_memory_space_constraint(x, pltpu.HBM)


def exchange(blocks, axis):
    count = lax.axis_size(axis)
    arrived = [blocks[0]]
    for p in range(1, count):
        arrived.append(lax.ppermute(blocks[p], axis, [(i, i ^ p) for i in range(count)]))
    return arrived


def on_device(
    voltage, conductance, reversal, drive, inv_cable, owner_map, peer_counts, pattern, transfer
):
    cells, width = voltage.shape
    steps = drive.shape[0]
    tiles = lax.axis_size("tile")
    sections = lax.axis_size("sec")
    capacity = 2 * cells // tiles
    row_count = tiles * capacity
    weights = transfer[0]
    slot_count, kinds, _, contact_width = weights.shape
    contact_tiles = CONTACTS // contact_width
    paired = PAIRED and tiles == 8
    vmem = pl.BlockSpec(memory_space=pltpu.VMEM)
    hbm = pl.BlockSpec(memory_space=pltpu.HBM)

    vloc, resp, ends, cond, rev, driven, turned, early_tiles = pl.pallas_call(
        local_kernel,
        out_shape=(
            jax.ShapeDtypeStruct((steps - 1, cells, width), F32),
            jax.ShapeDtypeStruct((steps - 1, 2 * cells, width), BF),
            jax.ShapeDtypeStruct((END_ROWS, cells), BF),
            jax.ShapeDtypeStruct((cells, width), F32),
            jax.ShapeDtypeStruct((cells, width), F32),
            jax.ShapeDtypeStruct((steps, cells, width), BF),
            jax.ShapeDtypeStruct((width, width), F32),
            jax.ShapeDtypeStruct((PARTS[0],) + weights.shape[1:], BF),
        ),
        in_specs=[hbm] * 6,
        out_specs=(vmem,) * 8,
        scratch_shapes=[
            pltpu.VMEM((cells, width), F32),
            pltpu.VMEM((width, width), F32),
            pltpu.SemaphoreType.DMA((6,)),
        ],
        compiler_params=PARAMS,
        name="local_steps",
    )(
        in_hbm(voltage),
        in_hbm(conductance),
        in_hbm(reversal),
        in_hbm(drive),
        in_hbm(inv_cable),
        in_hbm(weights),
    )

    vlast, spread, order, select, middle_tiles = pl.pallas_call(
        functools.partial(prepare_kernel, tiles, paired),
        out_shape=(
            jax.ShapeDtypeStruct((cells, width), F32),
            jax.ShapeDtypeStruct((row_count, cells), BF),
            jax.ShapeDtypeStruct((slot_count, row_count), BF),
            jax.ShapeDtypeStruct((contact_tiles, kinds * slot_count), BF),
            jax.ShapeDtypeStruct((PARTS[1],) + weights.shape[1:], BF),
        ),
        in_specs=[vmem] * 5 + [hbm] * 4,
        out_specs=(vmem,) * 5,
        scratch_shapes=[
            pltpu.VMEM((1, cells), jnp.int32),
            pltpu.SMEM((1, tiles), jnp.int32),
            pltpu.VMEM((kinds, slot_count), jnp.int32),
            pltpu.SemaphoreType.DMA((4,)),
        ],
        compiler_params=PARAMS,
        name="prepare_rows",
    )(
        vloc,
        cond,
        rev,
        driven,
        turned,
        in_hbm(owner_map.reshape(1, cells)),
        in_hbm(peer_counts),
        in_hbm(pattern[0].T),
        in_hbm(weights),
    )

    all_ends = exchange([ends] * sections, "sec")
    block_count = tiles if paired else 1
    final_here, *outgoing = pl.pallas_call(
        functools.partial(couple_kernel, sections, block_count),
        out_shape=(
            jax.ShapeDtypeStruct((cells, width), F32),
        )
        + (jax.ShapeDtypeStruct((row_count // block_count, steps * width), BF),) * block_count,
        in_specs=[vmem] * (sections + 8),
        out_specs=(vmem,) * (1 + block_count),
        scratch_shapes=[
            pltpu.VMEM((sections, END_ROWS, cells), F32),
            pltpu.VMEM((2 * steps, cells), F32),
            pltpu.VMEM((steps, cells, width), F32),
        ],
        compiler_params=PARAMS,
        name="couple_sections",
    )(
        *[all_ends[p] for p in SEC_SEQUENCE],
        vloc,
        vlast,
        resp,
        cond,
        rev,
        driven,
        turned,
        spread,
    )

    if paired:
        arrived = exchange(outgoing, "tile")
    else:
        arrived = [lax.all_to_all(outgoing[0], "tile", split_axis=0, concat_axis=0, tiled=True)]

    late_tiles, final_voltage = pl.pallas_call(
        fetch_kernel,
        out_shape=(
            jax.ShapeDtypeStruct((PARTS[2],) + weights.shape[1:], BF),
            jax.ShapeDtypeStruct((cells, width), F32),
        ),
        in_specs=[vmem, hbm],
        out_specs=(vmem, hbm),
        scratch_shapes=[pltpu.SemaphoreType.DMA((2,))],
        compiler_params=PARAMS,
        name="fetch_tiles",
    )(final_here, in_hbm(weights))

    sequence = SEQUENCE if paired else (0,)
    arrived = [arrived[p] for p in sequence]
    partial_sum = pl.pallas_call(
        functools.partial(readout_kernel, steps, sequence),
        out_shape=jax.ShapeDtypeStruct((contact_tiles, steps, contact_width), BF),
        in_specs=[vmem] * (len(arrived) + 5),
        out_specs=vmem,
        scratch_shapes=[
            pltpu.VMEM((slot_count * steps, width), F32),
            pltpu.VMEM((kinds * slot_count * steps, contact_width), F32),
            pltpu.VMEM((contact_tiles, steps, contact_width), F32),
        ],
        compiler_params=PARAMS,
        name="readout",
    )(select, order, *arrived, early_tiles, middle_tiles, late_tiles)

    devices = tiles * sections
    share = CONTACTS // devices
    parts = contact_width // share
    if parts > 1:
        partial_sum = partial_sum.reshape(contact_tiles, steps, parts, share)
        partial_sum = partial_sum.transpose(0, 2, 1, 3).reshape(devices, steps, share)
    shares = lax.all_to_all(partial_sum, ("tile", "sec"), split_axis=0, concat_axis=0, tiled=True)
    return final_voltage, jnp.sum(shares.astype(F32), axis=0)


def solution(mesh):
    placed = (
        P("tile", "sec"),
        P("tile", "sec"),
        P("tile", "sec"),
        P(None, "tile", "sec"),
        P(),
        P("tile"),
        P("tile", None),
        P("sec", "tile", None),
        P("sec", "tile", None, None, None),
    )
    return jax.shard_map(
        on_device,
        mesh=mesh,
        in_specs=placed,
        out_specs=(P("tile", "sec"), P(None, ("tile", "sec"))),
        check_vma=False,
    )
```

```python
import functools

import jax
import jax.numpy as jnp
from jax import lax
from jax.experimental import pallas as pl
from jax.experimental.pallas import tpu as pltpu
from jax.sharding import PartitionSpec as P

CONTACTS = 4096
TIME_STEP = 0.25
AXIAL = 2.0
END_ROWS = 48
PAIRED = True
PARTS = (48, 16, 64)
SEC_SEQUENCE = (0, 1, 2, 3)
SEQUENCE = (0, 6, 1, 7, 5, 2, 4, 3)
BF = jnp.bfloat16
F32 = jnp.float32
PARAMS = pltpu.CompilerParams(vmem_limit_bytes=24 * 1024 * 1024)


def split_hi_lo(x):
    hi = x.astype(BF)
    return hi, (x - hi.astype(F32)).astype(BF)


def one_hot(condition):
    return jnp.where(condition, 1.0, 0.0).astype(BF)


def iota(shape, dim):
    return lax.broadcasted_iota(jnp.int32, shape, dim)


def hi_lo_weights(cable):
    cable_hi, cable_lo = split_hi_lo(cable)
    half = jnp.concatenate([cable_hi, cable_lo], axis=1)
    return jnp.concatenate([half, half], axis=0)


def solve(rhs, weights):
    width = rhs.shape[1]
    hi, lo = split_hi_lo(rhs)
    both = jnp.dot(jnp.concatenate([hi, lo], axis=1), weights, preferred_element_type=F32)
    return both[:, :width] + both[:, width:]


def keep_and_source(cond, rev):
    lane = iota(cond.shape, 1)
    at_end = (lane == 0) | (lane == cond.shape[1] - 1)
    keep = 1.0 - TIME_STEP * cond - jnp.where(at_end, TIME_STEP * AXIAL, 0.0).astype(F32)
    return keep, TIME_STEP * cond * rev


def start_all(pairs, sems):
    copies = [pltpu.make_async_copy(src, dst, sems.at[i]) for i, (src, dst) in enumerate(pairs)]
    for copy in copies:
        copy.start()
    return copies


def local_kernel(
    v_hbm,
    g_hbm,
    e_hbm,
    drive_hbm,
    cable_hbm,
    transfer_hbm,
    vloc_ref,
    resp_ref,
    ends_ref,
    g_ref,
    e_ref,
    drive_ref,
    turned_ref,
    early_ref,
    v_ref,
    cable_ref,
    sems,
):
    copies = start_all(
        [
            (cable_hbm, cable_ref),
            (g_hbm, g_ref),
            (e_hbm, e_ref),
            (v_hbm, v_ref),
            (drive_hbm, drive_ref),
            (transfer_hbm.at[pl.ds(0, PARTS[0])], early_ref),
        ],
        sems,
    )
    cells, width = v_ref.shape
    steps = drive_ref.shape[0]
    copies[0].wait()
    cable = cable_ref[...].T
    turned_ref[...] = cable
    weights = hi_lo_weights(cable)
    for copy in copies[1:3]:
        copy.wait()
    keep, source = keep_and_source(g_ref[...], e_ref[...])
    left = jnp.broadcast_to(TIME_STEP * AXIAL * cable[0:1, :], (cells, width))
    right = jnp.broadcast_to(TIME_STEP * AXIAL * cable[width - 1 : width, :], (cells, width))
    next_sides = solve(left * keep, weights), solve(right * keep, weights)
    for copy in copies[3:5]:
        copy.wait()
    lane = iota((cells, width), 1)

    def with_ends(table, x, row):
        return jnp.where((lane >= row) & (lane < row + 2), pltpu.roll(x, row + 1, 1), table)

    voltage = v_ref[...]
    left_row, right_row = 2 * steps, 4 * steps
    table = with_ends(jnp.zeros((cells, width), F32), voltage, 0)
    table = with_ends(with_ends(table, left, left_row), right, right_row)
    for k in range(steps - 1):
        rhs = voltage * keep + source + TIME_STEP * drive_ref[k].astype(F32)
        voltage = solve(rhs, weights)
        left, right = next_sides
        if k < steps - 2:
            next_sides = solve(left * keep, weights), solve(right * keep, weights)
        vloc_ref[k] = voltage
        resp_ref[k, :cells] = left.astype(BF)
        resp_ref[k, cells:] = right.astype(BF)
        table = with_ends(table, voltage, 2 * (k + 1))
        if k < steps - 2:
            table = with_ends(table, left, left_row + 2 * (k + 1))
            table = with_ends(table, right, right_row + 2 * (k + 1))
    ends_ref[...] = table.T[:END_ROWS].astype(BF)
    copies[5].wait()


def prepare_kernel(
    tiles,
    paired,
    vloc_ref,
    g_ref,
    e_ref,
    drive_ref,
    turned_ref,
    owner_hbm,
    counts_hbm,
    pattern_hbm,
    transfer_hbm,
    vlast_ref,
    spread_ref,
    order_ref,
    select_ref,
    middle_ref,
    owner_ref,
    counts_ref,
    pattern_ref,
    sems,
):
    copies = start_all(
        [
            (owner_hbm, owner_ref),
            (counts_hbm, counts_ref),
            (pattern_hbm, pattern_ref),
            (transfer_hbm.at[pl.ds(PARTS[0], PARTS[1])], middle_ref),
        ],
        sems,
    )
    steps, cells, _ = drive_ref.shape
    keep, source = keep_and_source(g_ref[...], e_ref[...])
    rhs = vloc_ref[steps - 2] * keep + source + TIME_STEP * drive_ref[steps - 1].astype(F32)
    vlast_ref[...] = solve(rhs, hi_lo_weights(turned_ref[...]))

    for copy in copies[:2]:
        copy.wait()
    me = lax.axis_index("tile")
    row_count = spread_ref.shape[0]
    capacity = row_count // tiles
    owner = owner_ref[...]
    member = owner == iota((tiles, cells), 0)
    before = iota((cells, cells), 0) < iota((cells, cells), 1)
    rank = jnp.dot(one_hot(member), one_hot(before), preferred_element_type=F32)
    rank = jnp.sum(jnp.where(member, rank, 0.0), axis=0, keepdims=True).astype(jnp.int32)
    to = owner ^ me if paired else owner
    spread_ref[...] = one_hot(iota((row_count, cells), 0) == to * capacity + rank)

    counts = [counts_ref[0, u] for u in range(tiles)]
    row = iota((1, row_count), 1)
    slot_of = jnp.full((1, row_count), -1, jnp.int32)
    start = jnp.int32(0)
    for b in range(tiles):
        if paired:
            sender = b ^ me
            count = counts_ref[0, sender]
            start = sum(jnp.where(u < sender, counts[u], 0) for u in range(tiles))
        else:
            count = counts[b]
            start = start + (counts[b - 1] if b else 0)
        place = row - b * capacity
        slot_of = jnp.where((place >= 0) & (place < count), place + start, slot_of)
    order_ref[...] = one_hot(iota(order_ref.shape, 0) == slot_of)
    copies[2].wait()
    contact_tiles = select_ref.shape[0]
    kinds, slot_count = pattern_ref.shape
    for t in range(kinds):
        select_ref[:, t * slot_count : (t + 1) * slot_count] = one_hot(
            iota((contact_tiles, slot_count), 0) == pattern_ref[t : t + 1, :]
        )
    copies[3].wait()


def couple_kernel(sections, block_count, *refs):
    ends_refs, refs = refs[:sections], refs[sections:]
    vloc_ref, vlast_ref, resp_ref, g_ref, e_ref, drive_ref, turned_ref, spread_ref, *refs = refs
    final_ref, *refs = refs
    out_refs, refs = refs[:block_count], refs[block_count:]
    ends32, incoming, leak = refs
    steps, cells, width = drive_ref.shape
    mine = lax.axis_index("sec")
    for p in range(sections):
        ends32[mine ^ SEC_SEQUENCE[p]] = ends_refs[p][...].astype(F32)

    def rows(q):
        return ends32[:, q, :]

    def lagged(row):
        return [None] + [rows(row + 2 * l) for l in range(steps - 1)]

    left_b, left_a = lagged(2 * steps), lagged(2 * steps + 1)
    right_b, right_a = lagged(4 * steps), lagged(4 * steps + 1)
    zero = jnp.zeros((1, cells), F32)
    from_left, from_right = [], []
    for k in range(steps):
        last, first = rows(2 * k), rows(2 * k + 1)
        for j in range(k):
            first = first + (left_a[k - j] * from_left[j] + right_a[k - j] * from_right[j])
            last = last + (left_b[k - j] * from_left[j] + right_b[k - j] * from_right[j])
        from_left.append(jnp.concatenate([zero, last[:-1]], axis=0))
        from_right.append(jnp.concatenate([first[1:], zero], axis=0))
    own = iota((sections, cells), 0) == mine
    for j in range(steps):
        incoming[pl.ds(2 * j, 1), :] = jnp.sum(
            jnp.where(own, from_left[j], 0.0), axis=0, keepdims=True
        )
        incoming[pl.ds(2 * j + 1, 1), :] = jnp.sum(
            jnp.where(own, from_right[j], 0.0), axis=0, keepdims=True
        )
    by_cell = incoming[...].T.astype(BF)

    block = 16
    lag_left = jnp.broadcast_to(TIME_STEP * AXIAL * turned_ref[0:1, :], (block, width)).astype(BF)
    lag_right = TIME_STEP * AXIAL * turned_ref[width - 1 : width, :]
    lag_right = jnp.broadcast_to(lag_right, (block, width)).astype(BF)
    for c in range(0, cells, block):
        span = slice(c, c + block)
        unit = [
            jnp.broadcast_to(by_cell[span, q : q + 1], (block, width))
            for q in range(2 * steps)
        ]
        lefts = [None, lag_left] + [resp_ref[l, span, :] for l in range(steps - 1)]
        rights = [None, lag_right] + [
            resp_ref[l, cells + c : cells + c + block, :] for l in range(steps - 1)
        ]
        cond, rev = g_ref[span, :], e_ref[span, :]
        for k in range(1, steps + 1):
            total = vloc_ref[k - 1, span, :] if k < steps else vlast_ref[span, :]
            inflow = [
                unit[2 * j] * lefts[k - j] + unit[2 * j + 1] * rights[k - j] for j in range(k)
            ]
            total = total + sum(inflow[1:], inflow[0]).astype(F32)
            leak[k - 1, span, :] = cond * (total - rev)
        final_ref[span, :] = total

    capacity = out_refs[0].shape[0]
    for k in range(0, steps, 2):
        current = [(leak[i] - drive_ref[i].astype(F32)).astype(BF) for i in (k, k + 1)]
        placed = jnp.dot(
            spread_ref[...], jnp.concatenate(current, axis=1), preferred_element_type=F32
        ).astype(BF)
        for b in range(block_count):
            out_refs[b][:, k * width : (k + 2) * width] = placed[b * capacity : (b + 1) * capacity]


def fetch_kernel(final_ref, transfer_hbm, late_ref, final_hbm, sems):
    copies = start_all(
        [
            (transfer_hbm.at[pl.ds(PARTS[0] + PARTS[1], PARTS[2])], late_ref),
            (final_ref, final_hbm),
        ],
        sems,
    )
    for copy in copies:
        copy.wait()


def readout_kernel(steps, sequence, select_ref, order_ref, *refs):
    *block_refs, early_ref, middle_ref, late_ref, out_ref, slots, reach, sums = refs
    held = [(ref, at) for ref in (early_ref, middle_ref, late_ref) for at in range(ref.shape[0])]
    block_refs = [block_refs[sequence.index(p)] for p in range(len(block_refs))]
    slot_count = order_ref.shape[0]
    kinds, width, contacts = early_ref.shape[1:]
    for k in range(0, steps, 2):
        span = slice(k * width, (k + 2) * width)
        rows = jnp.concatenate([ref[:, span] for ref in block_refs], axis=0)
        both = jnp.dot(order_ref[...], rows, preferred_element_type=F32)
        for i in range(2):
            slots[pl.ds(k + i, slot_count, stride=steps), :] = both[:, i * width : (i + 1) * width]
    for s, (ref, at) in enumerate(held):
        current = slots[s * steps : (s + 1) * steps, :].astype(BF)
        tile = jnp.concatenate([ref[at, t] for t in range(kinds)], axis=1)
        product = jnp.dot(current, tile, preferred_element_type=F32)
        for t in range(kinds):
            row = (t * slot_count + s) * steps
            reach[row : row + steps, :] = product[:, t * contacts : (t + 1) * contacts]
    for k in range(steps):
        hi, lo = split_hi_lo(reach[pl.ds(k, kinds * slot_count, stride=steps), :])
        both = jnp.dot(
            select_ref[...], jnp.concatenate([hi, lo], axis=1), preferred_element_type=F32
        )
        sums[:, k, :] = both[:, :contacts] + both[:, contacts:]
    out_ref[...] = sums[...].astype(BF)


def in_hbm(x):
    return pltpu.with_memory_space_constraint(x, pltpu.HBM)


def exchange(blocks, axis):
    count = lax.axis_size(axis)
    arrived = [blocks[0]]
    for p in range(1, count):
        arrived.append(lax.ppermute(blocks[p], axis, [(i, i ^ p) for i in range(count)]))
    return arrived


def on_device(
    voltage, conductance, reversal, drive, inv_cable, owner_map, peer_counts, pattern, transfer
):
    cells, width = voltage.shape
    steps = drive.shape[0]
    tiles = lax.axis_size("tile")
    sections = lax.axis_size("sec")
    capacity = 2 * cells // tiles
    row_count = tiles * capacity
    weights = transfer[0]
    slot_count, kinds, _, contact_width = weights.shape
    contact_tiles = CONTACTS // contact_width
    paired = PAIRED and tiles == 8
    vmem = pl.BlockSpec(memory_space=pltpu.VMEM)
    hbm = pl.BlockSpec(memory_space=pltpu.HBM)

    vloc, resp, ends, cond, rev, driven, turned, early_tiles = pl.pallas_call(
        local_kernel,
        out_shape=(
            jax.ShapeDtypeStruct((steps - 1, cells, width), F32),
            jax.ShapeDtypeStruct((steps - 1, 2 * cells, width), BF),
            jax.ShapeDtypeStruct((END_ROWS, cells), BF),
            jax.ShapeDtypeStruct((cells, width), F32),
            jax.ShapeDtypeStruct((cells, width), F32),
            jax.ShapeDtypeStruct((steps, cells, width), BF),
            jax.ShapeDtypeStruct((width, width), F32),
            jax.ShapeDtypeStruct((PARTS[0],) + weights.shape[1:], BF),
        ),
        in_specs=[hbm] * 6,
        out_specs=(vmem,) * 8,
        scratch_shapes=[
            pltpu.VMEM((cells, width), F32),
            pltpu.VMEM((width, width), F32),
            pltpu.SemaphoreType.DMA((6,)),
        ],
        compiler_params=PARAMS,
        name="local_steps",
    )(
        in_hbm(voltage),
        in_hbm(conductance),
        in_hbm(reversal),
        in_hbm(drive),
        in_hbm(inv_cable),
        in_hbm(weights),
    )

    vlast, spread, order, select, middle_tiles = pl.pallas_call(
        functools.partial(prepare_kernel, tiles, paired),
        out_shape=(
            jax.ShapeDtypeStruct((cells, width), F32),
            jax.ShapeDtypeStruct((row_count, cells), BF),
            jax.ShapeDtypeStruct((slot_count, row_count), BF),
            jax.ShapeDtypeStruct((contact_tiles, kinds * slot_count), BF),
            jax.ShapeDtypeStruct((PARTS[1],) + weights.shape[1:], BF),
        ),
        in_specs=[vmem] * 5 + [hbm] * 4,
        out_specs=(vmem,) * 5,
        scratch_shapes=[
            pltpu.VMEM((1, cells), jnp.int32),
            pltpu.SMEM((1, tiles), jnp.int32),
            pltpu.VMEM((kinds, slot_count), jnp.int32),
            pltpu.SemaphoreType.DMA((4,)),
        ],
        compiler_params=PARAMS,
        name="prepare_rows",
    )(
        vloc,
        cond,
        rev,
        driven,
        turned,
        in_hbm(owner_map.reshape(1, cells)),
        in_hbm(peer_counts),
        in_hbm(pattern[0].T),
        in_hbm(weights),
    )

    all_ends = exchange([ends] * sections, "sec")
    block_count = tiles if paired else 1
    final_here, *outgoing = pl.pallas_call(
        functools.partial(couple_kernel, sections, block_count),
        out_shape=(
            jax.ShapeDtypeStruct((cells, width), F32),
        )
        + (jax.ShapeDtypeStruct((row_count // block_count, steps * width), BF),) * block_count,
        in_specs=[vmem] * (sections + 8),
        out_specs=(vmem,) * (1 + block_count),
        scratch_shapes=[
            pltpu.VMEM((sections, END_ROWS, cells), F32),
            pltpu.VMEM((2 * steps, cells), F32),
            pltpu.VMEM((steps, cells, width), F32),
        ],
        compiler_params=PARAMS,
        name="couple_sections",
    )(
        *[all_ends[p] for p in SEC_SEQUENCE],
        vloc,
        vlast,
        resp,
        cond,
        rev,
        driven,
        turned,
        spread,
    )

    if paired:
        arrived = exchange(outgoing, "tile")
    else:
        arrived = [lax.all_to_all(outgoing[0], "tile", split_axis=0, concat_axis=0, tiled=True)]

    late_tiles, final_voltage = pl.pallas_call(
        fetch_kernel,
        out_shape=(
            jax.ShapeDtypeStruct((PARTS[2],) + weights.shape[1:], BF),
            jax.ShapeDtypeStruct((cells, width), F32),
        ),
        in_specs=[vmem, hbm],
        out_specs=(vmem, hbm),
        scratch_shapes=[pltpu.SemaphoreType.DMA((2,))],
        compiler_params=PARAMS,
        name="fetch_tiles",
    )(final_here, in_hbm(weights))

    sequence = SEQUENCE if paired else (0,)
    arrived = [arrived[p] for p in sequence]
    partial_sum = pl.pallas_call(
        functools.partial(readout_kernel, steps, sequence),
        out_shape=jax.ShapeDtypeStruct((contact_tiles, steps, contact_width), BF),
        in_specs=[vmem] * (len(arrived) + 5),
        out_specs=vmem,
        scratch_shapes=[
            pltpu.VMEM((slot_count * steps, width), F32),
            pltpu.VMEM((kinds * slot_count * steps, contact_width), F32),
            pltpu.VMEM((contact_tiles, steps, contact_width), F32),
        ],
        compiler_params=PARAMS,
        name="readout",
    )(select, order, *arrived, early_tiles, middle_tiles, late_tiles)

    devices = tiles * sections
    share = CONTACTS // devices
    parts = contact_width // share
    if parts > 1:
        partial_sum = partial_sum.reshape(contact_tiles, steps, parts, share)
        partial_sum = partial_sum.transpose(0, 2, 1, 3).reshape(devices, steps, share)
    shares = lax.all_to_all(partial_sum, ("tile", "sec"), split_axis=0, concat_axis=0, tiled=True)
    return final_voltage, jnp.sum(shares.astype(F32), axis=0)


def solution(mesh):
    placed = (
        P("tile", "sec"),
        P("tile", "sec"),
        P("tile", "sec"),
        P(None, "tile", "sec"),
        P(),
        P("tile"),
        P("tile", None),
        P("sec", "tile", None),
        P("sec", "tile", None, None, None),
    )
    return jax.shard_map(
        on_device,
        mesh=mesh,
        in_specs=placed,
        out_specs=(P("tile", "sec"), P(None, ("tile", "sec"))),
        check_vma=False,
    )
```

```python
import functools

import jax
import jax.numpy as jnp
from jax import lax
from jax.experimental import pallas as pl
from jax.experimental.pallas import tpu as pltpu
from jax.sharding import PartitionSpec as P

CONTACTS = 4096
TIME_STEP = 0.25
AXIAL = 2.0
END_ROWS = 48
PAIRED = True
PARTS = (48, 16, 64)
SEC_SEQUENCE = (0, 1, 2, 3)
SEQUENCE = (0, 6, 3, 7, 5, 2, 4, 1)
BF = jnp.bfloat16
F32 = jnp.float32
PARAMS = pltpu.CompilerParams(vmem_limit_bytes=24 * 1024 * 1024)


def split_hi_lo(x):
    hi = x.astype(BF)
    return hi, (x - hi.astype(F32)).astype(BF)


def one_hot(condition):
    return jnp.where(condition, 1.0, 0.0).astype(BF)


def iota(shape, dim):
    return lax.broadcasted_iota(jnp.int32, shape, dim)


def hi_lo_weights(cable):
    cable_hi, cable_lo = split_hi_lo(cable)
    half = jnp.concatenate([cable_hi, cable_lo], axis=1)
    return jnp.concatenate([half, half], axis=0)


def solve(rhs, weights):
    width = rhs.shape[1]
    hi, lo = split_hi_lo(rhs)
    both = jnp.dot(jnp.concatenate([hi, lo], axis=1), weights, preferred_element_type=F32)
    return both[:, :width] + both[:, width:]


def keep_and_source(cond, rev):
    lane = iota(cond.shape, 1)
    at_end = (lane == 0) | (lane == cond.shape[1] - 1)
    keep = 1.0 - TIME_STEP * cond - jnp.where(at_end, TIME_STEP * AXIAL, 0.0).astype(F32)
    return keep, TIME_STEP * cond * rev


def start_all(pairs, sems):
    copies = [pltpu.make_async_copy(src, dst, sems.at[i]) for i, (src, dst) in enumerate(pairs)]
    for copy in copies:
        copy.start()
    return copies


def local_kernel(
    v_hbm,
    g_hbm,
    e_hbm,
    drive_hbm,
    cable_hbm,
    transfer_hbm,
    vloc_ref,
    resp_ref,
    ends_ref,
    g_ref,
    e_ref,
    drive_ref,
    turned_ref,
    early_ref,
    v_ref,
    cable_ref,
    sems,
):
    copies = start_all(
        [
            (cable_hbm, cable_ref),
            (v_hbm, v_ref),
            (g_hbm, g_ref),
            (e_hbm, e_ref),
            (drive_hbm, drive_ref),
            (transfer_hbm.at[pl.ds(0, PARTS[0])], early_ref),
        ],
        sems,
    )
    cells, width = v_ref.shape
    steps = drive_ref.shape[0]
    copies[0].wait()
    cable = cable_ref[...].T
    turned_ref[...] = cable
    weights = hi_lo_weights(cable)
    for copy in copies[1:5]:
        copy.wait()
    keep, source = keep_and_source(g_ref[...], e_ref[...])
    lane = iota((cells, width), 1)

    def with_ends(table, x, row):
        return jnp.where((lane >= row) & (lane < row + 2), pltpu.roll(x, row + 1, 1), table)

    voltage = v_ref[...]
    left = jnp.broadcast_to(TIME_STEP * AXIAL * cable[0:1, :], (cells, width))
    right = jnp.broadcast_to(TIME_STEP * AXIAL * cable[width - 1 : width, :], (cells, width))
    left_row, right_row = 2 * steps, 4 * steps
    table = with_ends(jnp.zeros((cells, width), F32), voltage, 0)
    table = with_ends(with_ends(table, left, left_row), right, right_row)
    for k in range(steps - 1):
        rhs = voltage * keep + source + TIME_STEP * drive_ref[k].astype(F32)
        voltage = solve(rhs, weights)
        left = solve(left * keep, weights)
        right = solve(right * keep, weights)
        vloc_ref[k] = voltage
        resp_ref[k, :cells] = left.astype(BF)
        resp_ref[k, cells:] = right.astype(BF)
        table = with_ends(table, voltage, 2 * (k + 1))
        if k < steps - 2:
            table = with_ends(table, left, left_row + 2 * (k + 1))
            table = with_ends(table, right, right_row + 2 * (k + 1))
    ends_ref[...] = table.T[:END_ROWS].astype(BF)
    copies[5].wait()


def prepare_kernel(
    tiles,
    paired,
    vloc_ref,
    g_ref,
    e_ref,
    drive_ref,
    turned_ref,
    owner_hbm,
    counts_hbm,
    pattern_hbm,
    transfer_hbm,
    vlast_ref,
    spread_ref,
    order_ref,
    select_ref,
    middle_ref,
    owner_ref,
    counts_ref,
    pattern_ref,
    sems,
):
    copies = start_all(
        [
            (owner_hbm, owner_ref),
            (counts_hbm, counts_ref),
            (pattern_hbm, pattern_ref),
            (transfer_hbm.at[pl.ds(PARTS[0], PARTS[1])], middle_ref),
        ],
        sems,
    )
    steps, cells, _ = drive_ref.shape
    keep, source = keep_and_source(g_ref[...], e_ref[...])
    rhs = vloc_ref[steps - 2] * keep + source + TIME_STEP * drive_ref[steps - 1].astype(F32)
    vlast_ref[...] = solve(rhs, hi_lo_weights(turned_ref[...]))

    for copy in copies[:2]:
        copy.wait()
    me = lax.axis_index("tile")
    row_count = spread_ref.shape[0]
    capacity = row_count // tiles
    owner = owner_ref[...]
    member = owner == iota((tiles, cells), 0)
    before = iota((cells, cells), 0) < iota((cells, cells), 1)
    rank = jnp.dot(one_hot(member), one_hot(before), preferred_element_type=F32)
    rank = jnp.sum(jnp.where(member, rank, 0.0), axis=0, keepdims=True).astype(jnp.int32)
    to = owner ^ me if paired else owner
    spread_ref[...] = one_hot(iota((row_count, cells), 0) == to * capacity + rank)

    counts = [counts_ref[0, u] for u in range(tiles)]
    row = iota((1, row_count), 1)
    slot_of = jnp.full((1, row_count), -1, jnp.int32)
    start = jnp.int32(0)
    for b in range(tiles):
        if paired:
            sender = b ^ me
            count = counts_ref[0, sender]
            start = sum(jnp.where(u < sender, counts[u], 0) for u in range(tiles))
        else:
            count = counts[b]
            start = start + (counts[b - 1] if b else 0)
        place = row - b * capacity
        slot_of = jnp.where((place >= 0) & (place < count), place + start, slot_of)
    order_ref[...] = one_hot(iota(order_ref.shape, 0) == slot_of)
    copies[2].wait()
    contact_tiles = select_ref.shape[0]
    kinds, slot_count = pattern_ref.shape
    for t in range(kinds):
        select_ref[:, t * slot_count : (t + 1) * slot_count] = one_hot(
            iota((contact_tiles, slot_count), 0) == pattern_ref[t : t + 1, :]
        )
    copies[3].wait()


def couple_kernel(sections, block_count, *refs):
    ends_refs, refs = refs[:sections], refs[sections:]
    vloc_ref, vlast_ref, resp_ref, g_ref, e_ref, drive_ref, turned_ref, spread_ref, *refs = refs
    final_ref, *refs = refs
    out_refs, refs = refs[:block_count], refs[block_count:]
    ends32, incoming, leak = refs
    steps, cells, width = drive_ref.shape
    mine = lax.axis_index("sec")
    for p in range(sections):
        ends32[mine ^ SEC_SEQUENCE[p]] = ends_refs[p][...].astype(F32)

    def rows(q):
        return ends32[:, q, :]

    def lagged(row):
        return [None] + [rows(row + 2 * l) for l in range(steps - 1)]

    left_b, left_a = lagged(2 * steps), lagged(2 * steps + 1)
    right_b, right_a = lagged(4 * steps), lagged(4 * steps + 1)
    zero = jnp.zeros((1, cells), F32)
    from_left, from_right = [], []
    for k in range(steps):
        last, first = rows(2 * k), rows(2 * k + 1)
        for j in range(k):
            first = first + (left_a[k - j] * from_left[j] + right_a[k - j] * from_right[j])
            last = last + (left_b[k - j] * from_left[j] + right_b[k - j] * from_right[j])
        from_left.append(jnp.concatenate([zero, last[:-1]], axis=0))
        from_right.append(jnp.concatenate([first[1:], zero], axis=0))
    own = iota((sections, cells), 0) == mine
    for j in range(steps):
        incoming[pl.ds(2 * j, 1), :] = jnp.sum(
            jnp.where(own, from_left[j], 0.0), axis=0, keepdims=True
        )
        incoming[pl.ds(2 * j + 1, 1), :] = jnp.sum(
            jnp.where(own, from_right[j], 0.0), axis=0, keepdims=True
        )
    by_cell = incoming[...].T.astype(BF)

    block = 16
    lag_left = jnp.broadcast_to(TIME_STEP * AXIAL * turned_ref[0:1, :], (block, width)).astype(BF)
    lag_right = TIME_STEP * AXIAL * turned_ref[width - 1 : width, :]
    lag_right = jnp.broadcast_to(lag_right, (block, width)).astype(BF)
    for c in range(0, cells, block):
        span = slice(c, c + block)
        unit = [
            jnp.broadcast_to(by_cell[span, q : q + 1], (block, width))
            for q in range(2 * steps)
        ]
        lefts = [None, lag_left] + [resp_ref[l, span, :] for l in range(steps - 1)]
        rights = [None, lag_right] + [
            resp_ref[l, cells + c : cells + c + block, :] for l in range(steps - 1)
        ]
        cond, rev = g_ref[span, :], e_ref[span, :]
        for k in range(1, steps + 1):
            total = vloc_ref[k - 1, span, :] if k < steps else vlast_ref[span, :]
            inflow = [
                unit[2 * j] * lefts[k - j] + unit[2 * j + 1] * rights[k - j] for j in range(k)
            ]
            total = total + sum(inflow[1:], inflow[0]).astype(F32)
            leak[k - 1, span, :] = cond * (total - rev)
        final_ref[span, :] = total

    capacity = out_refs[0].shape[0]
    for k in range(0, steps, 2):
        current = [(leak[i] - drive_ref[i].astype(F32)).astype(BF) for i in (k, k + 1)]
        placed = jnp.dot(
            spread_ref[...], jnp.concatenate(current, axis=1), preferred_element_type=F32
        ).astype(BF)
        for b in range(block_count):
            out_refs[b][:, k * width : (k + 2) * width] = placed[b * capacity : (b + 1) * capacity]


def fetch_kernel(final_ref, transfer_hbm, late_ref, final_hbm, sems):
    copies = start_all(
        [
            (transfer_hbm.at[pl.ds(PARTS[0] + PARTS[1], PARTS[2])], late_ref),
            (final_ref, final_hbm),
        ],
        sems,
    )
    for copy in copies:
        copy.wait()


def readout_kernel(steps, sequence, select_ref, order_ref, *refs):
    *block_refs, early_ref, middle_ref, late_ref, out_ref, slots, reach, sums = refs
    held = [(ref, at) for ref in (early_ref, middle_ref, late_ref) for at in range(ref.shape[0])]
    block_refs = [block_refs[sequence.index(p)] for p in range(len(block_refs))]
    slot_count = order_ref.shape[0]
    kinds, width, contacts = early_ref.shape[1:]
    for k in range(0, steps, 2):
        span = slice(k * width, (k + 2) * width)
        rows = jnp.concatenate([ref[:, span] for ref in block_refs], axis=0)
        both = jnp.dot(order_ref[...], rows, preferred_element_type=F32)
        for i in range(2):
            slots[pl.ds(k + i, slot_count, stride=steps), :] = both[:, i * width : (i + 1) * width]
    for s, (ref, at) in enumerate(held):
        current = slots[s * steps : (s + 1) * steps, :].astype(BF)
        tile = jnp.concatenate([ref[at, t] for t in range(kinds)], axis=1)
        product = jnp.dot(current, tile, preferred_element_type=F32)
        for t in range(kinds):
            row = (t * slot_count + s) * steps
            reach[row : row + steps, :] = product[:, t * contacts : (t + 1) * contacts]
    for k in range(steps):
        hi, lo = split_hi_lo(reach[pl.ds(k, kinds * slot_count, stride=steps), :])
        both = jnp.dot(
            select_ref[...], jnp.concatenate([hi, lo], axis=1), preferred_element_type=F32
        )
        sums[:, k, :] = both[:, :contacts] + both[:, contacts:]
    out_ref[...] = sums[...].astype(BF)


def in_hbm(x):
    return pltpu.with_memory_space_constraint(x, pltpu.HBM)


def exchange(blocks, axis):
    count = lax.axis_size(axis)
    arrived = [blocks[0]]
    for p in range(1, count):
        arrived.append(lax.ppermute(blocks[p], axis, [(i, i ^ p) for i in range(count)]))
    return arrived


def on_device(
    voltage, conductance, reversal, drive, inv_cable, owner_map, peer_counts, pattern, transfer
):
    cells, width = voltage.shape
    steps = drive.shape[0]
    tiles = lax.axis_size("tile")
    sections = lax.axis_size("sec")
    capacity = 2 * cells // tiles
    row_count = tiles * capacity
    weights = transfer[0]
    slot_count, kinds, _, contact_width = weights.shape
    contact_tiles = CONTACTS // contact_width
    paired = PAIRED and tiles == 8
    vmem = pl.BlockSpec(memory_space=pltpu.VMEM)
    hbm = pl.BlockSpec(memory_space=pltpu.HBM)

    vloc, resp, ends, cond, rev, driven, turned, early_tiles = pl.pallas_call(
        local_kernel,
        out_shape=(
            jax.ShapeDtypeStruct((steps - 1, cells, width), F32),
            jax.ShapeDtypeStruct((steps - 1, 2 * cells, width), BF),
            jax.ShapeDtypeStruct((END_ROWS, cells), BF),
            jax.ShapeDtypeStruct((cells, width), F32),
            jax.ShapeDtypeStruct((cells, width), F32),
            jax.ShapeDtypeStruct((steps, cells, width), BF),
            jax.ShapeDtypeStruct((width, width), F32),
            jax.ShapeDtypeStruct((PARTS[0],) + weights.shape[1:], BF),
        ),
        in_specs=[hbm] * 6,
        out_specs=(vmem,) * 8,
        scratch_shapes=[
            pltpu.VMEM((cells, width), F32),
            pltpu.VMEM((width, width), F32),
            pltpu.SemaphoreType.DMA((6,)),
        ],
        compiler_params=PARAMS,
        name="local_steps",
    )(
        in_hbm(voltage),
        in_hbm(conductance),
        in_hbm(reversal),
        in_hbm(drive),
        in_hbm(inv_cable),
        in_hbm(weights),
    )

    vlast, spread, order, select, middle_tiles = pl.pallas_call(
        functools.partial(prepare_kernel, tiles, paired),
        out_shape=(
            jax.ShapeDtypeStruct((cells, width), F32),
            jax.ShapeDtypeStruct((row_count, cells), BF),
            jax.ShapeDtypeStruct((slot_count, row_count), BF),
            jax.ShapeDtypeStruct((contact_tiles, kinds * slot_count), BF),
            jax.ShapeDtypeStruct((PARTS[1],) + weights.shape[1:], BF),
        ),
        in_specs=[vmem] * 5 + [hbm] * 4,
        out_specs=(vmem,) * 5,
        scratch_shapes=[
            pltpu.VMEM((1, cells), jnp.int32),
            pltpu.SMEM((1, tiles), jnp.int32),
            pltpu.VMEM((kinds, slot_count), jnp.int32),
            pltpu.SemaphoreType.DMA((4,)),
        ],
        compiler_params=PARAMS,
        name="prepare_rows",
    )(
        vloc,
        cond,
        rev,
        driven,
        turned,
        in_hbm(owner_map.reshape(1, cells)),
        in_hbm(peer_counts),
        in_hbm(pattern[0].T),
        in_hbm(weights),
    )

    all_ends = exchange([ends] * sections, "sec")
    block_count = tiles if paired else 1
    final_here, *outgoing = pl.pallas_call(
        functools.partial(couple_kernel, sections, block_count),
        out_shape=(
            jax.ShapeDtypeStruct((cells, width), F32),
        )
        + (jax.ShapeDtypeStruct((row_count // block_count, steps * width), BF),) * block_count,
        in_specs=[vmem] * (sections + 8),
        out_specs=(vmem,) * (1 + block_count),
        scratch_shapes=[
            pltpu.VMEM((sections, END_ROWS, cells), F32),
            pltpu.VMEM((2 * steps, cells), F32),
            pltpu.VMEM((steps, cells, width), F32),
        ],
        compiler_params=PARAMS,
        name="couple_sections",
    )(
        *[all_ends[p] for p in SEC_SEQUENCE],
        vloc,
        vlast,
        resp,
        cond,
        rev,
        driven,
        turned,
        spread,
    )

    if paired:
        arrived = exchange(outgoing, "tile")
    else:
        arrived = [lax.all_to_all(outgoing[0], "tile", split_axis=0, concat_axis=0, tiled=True)]

    late_tiles, final_voltage = pl.pallas_call(
        fetch_kernel,
        out_shape=(
            jax.ShapeDtypeStruct((PARTS[2],) + weights.shape[1:], BF),
            jax.ShapeDtypeStruct((cells, width), F32),
        ),
        in_specs=[vmem, hbm],
        out_specs=(vmem, hbm),
        scratch_shapes=[pltpu.SemaphoreType.DMA((2,))],
        compiler_params=PARAMS,
        name="fetch_tiles",
    )(final_here, in_hbm(weights))

    sequence = SEQUENCE if paired else (0,)
    arrived = [arrived[p] for p in sequence]
    partial_sum = pl.pallas_call(
        functools.partial(readout_kernel, steps, sequence),
        out_shape=jax.ShapeDtypeStruct((contact_tiles, steps, contact_width), BF),
        in_specs=[vmem] * (len(arrived) + 5),
        out_specs=vmem,
        scratch_shapes=[
            pltpu.VMEM((slot_count * steps, width), F32),
            pltpu.VMEM((kinds * slot_count * steps, contact_width), F32),
            pltpu.VMEM((contact_tiles, steps, contact_width), F32),
        ],
        compiler_params=PARAMS,
        name="readout",
    )(select, order, *arrived, early_tiles, middle_tiles, late_tiles)

    devices = tiles * sections
    share = CONTACTS // devices
    parts = contact_width // share
    if parts > 1:
        partial_sum = partial_sum.reshape(contact_tiles, steps, parts, share)
        partial_sum = partial_sum.transpose(0, 2, 1, 3).reshape(devices, steps, share)
    shares = lax.all_to_all(partial_sum, ("tile", "sec"), split_axis=0, concat_axis=0, tiled=True)
    return final_voltage, jnp.sum(shares.astype(F32), axis=0)


def solution(mesh):
    placed = (
        P("tile", "sec"),
        P("tile", "sec"),
        P("tile", "sec"),
        P(None, "tile", "sec"),
        P(),
        P("tile"),
        P("tile", None),
        P("sec", "tile", None),
        P("sec", "tile", None, None, None),
    )
    return jax.shard_map(
        on_device,
        mesh=mesh,
        in_specs=placed,
        out_specs=(P("tile", "sec"), P(None, ("tile", "sec"))),
        check_vma=False,
    )
```
